256 devices in a mesh: mkt: 2 (over core), sku: 32 (over y, z), cat: 4 (over x).
Axes of the slice: x: 4, y: 4, z: 8, core: 2. Of those that a mesh axis runs over, the one named last changes fastest.
Arguments:
- features: bfloat16 [1024, 512], P('mkt'), may hold values from -8 to 8
- taste: bfloat16 [512, 4, 65536], P(None, 'cat', 'sku'), may hold values from -3 to 3
- price: float32 [4, 65536], P('cat', 'sku'), may hold values from 0.5 to 2
- alpha: float32 [1024], P('mkt'), may hold values from 0.3 to 1
- market_size: float32 [1024], P('mkt'), may hold values from 0.5 to 8
- store_brand: float32 [4, 128], P('cat'), may hold values from -4 to 4
- sub_scale: float32 [4, 128], P('cat'), may hold values from 0.45 to 0.85
- cat_scale: float32 [4, 16], P('cat'), may hold values from 0.85 to 1
- availability: int32 [1024, 4, 65536], P('mkt', 'cat', 'sku'), may hold values 0 or 1
- sku_subcat: int32 [4, 65536], P('cat', 'sku'), may hold values from 0 to 127, never falling along the last dimension, each value on 1 to 2048 neighbouring positions
- subcat_cat: int32 [4, 128], P('cat'), may hold values from 0 to 15, never falling along the last dimension, each value on 1 to 24 neighbouring positions
- cotangent: bfloat16 [1024, 4, 65536], P('mkt', 'cat', 'sku'), may hold values from -0.29882812 to 0.29882812
Outputs:
- log_demand: float32 [1024, 4, 65536], P('mkt', 'cat', 'sku')
- price_grad: float32 [4, 65536], P('cat', 'sku')
The draws below stay inside these ranges and needn't reach their ends.
Inputs may be any that keep to these rules, and one draw needn't show every extreme that they name: `sku_subcat`: never falls along a group; every one of the 128 subcategories holds at least one SKU, at most 2048. `subcat_cat`: never falls along a group; every one of the 16 categories holds at least one subcategory.
All inputs are finite; a program needn't handle non-finite values. No bound on the sum of `availability` on one device may be relied on, other than what follows from the above.
Results may differ from the reference program's by a relative error of at most 0.0003.
Values sent between devices are 32-bit elements; how exact they have to be, the bound alone decides.
A program may use at most 128 MiB of HBM per device.

```python
import math
import jax
import jax.numpy as jnp
import numpy as np
from jax import lax

F = 512
MARKETS = 1024
GROUP_SKUS = 65536
SUB_GRP = 128
CAT_GRP = 16
N_CAT = 4


def draw_features(key, part):
    key = jax.random.fold_in(key, 11)
    values = jax.random.normal(key, (MARKETS, F), jnp.float32)
    return values.astype(jnp.bfloat16)


def draw_taste(key, part):
    key = jax.random.fold_in(key, 12)
    values = jax.random.normal(key, (F, N_CAT, GROUP_SKUS), jnp.float32) / F ** 0.5
    return values.astype(jnp.bfloat16)


def touch_ends(array, own_key, smallest, high):
    longest = array.shape.index(max(array.shape))
    spots = []
    for shift in (0, 1):
        where = [jax.random.randint(jax.random.fold_in(own_key, axis), (), 0, length) for axis, length in enumerate(array.shape)]
        where[longest] = (where[longest] + shift) % array.shape[longest]
        spots.append(tuple(where))
    return array.at[spots[0]].set(smallest).at[spots[1]].set(high)


def block_scale(stream_key, shape, cuts, low, top_value):
    factor_of = 1.0
    for dim, parts in cuts:
        heights = jax.random.uniform(jax.random.fold_in(jax.random.fold_in(stream_key, 6), dim), (parts,), jnp.float32, low / len(cuts), top_value / len(cuts))
        factor_of = factor_of * jnp.repeat(jnp.exp(heights), shape[dim] // parts).reshape((-1,) + (1,) * (len(shape) - 1 - dim))
    return factor_of


def split_up(count, total, limit, skew):
    weights = [(1 << 20) // math.isqrt(grade ** skew) + 1 for grade in range(2, count + 1)]
    rest, holding = total - limit - (count - 1), [1] * (count - 1)
    while rest > 0:
        candidates = [i for i in range(count - 1) if holding[i] < limit]
        mass, budget = sum([weights[i] for i in candidates]), rest
        for i in candidates:
            addition = min(limit - holding[i], max(1, budget * weights[i] // mass), rest)
            holding[i] = holding[i] + addition
            rest = rest - addition
    return np.array([limit] + holding)


def ragged(key, number_of, total, bound, skew):
    if number_of == 2:
        one = jax.random.randint(key, (), max(1, total - bound), min(bound, total - 1) + 1)
        return jnp.stack([one, total - one])
    lengths = jnp.asarray(split_up(number_of, total, bound, skew), jnp.int32)
    pairs = (number_of - 1) // 2
    donor, sink = lengths[1:1 + 2 * pairs:2], lengths[2:2 + 2 * pairs:2]
    margin = jnp.minimum(donor - 1, bound - sink)
    shifted = jax.random.randint(jax.random.fold_in(key, 1), (pairs,), 0, 1 << 20) % (margin + 1)
    lengths = lengths.at[1:1 + 2 * pairs:2].set(donor - shifted).at[2:2 + 2 * pairs:2].set(sink + shifted)
    return lengths[jax.random.permutation(jax.random.fold_in(key, 2), number_of)]


def centred(stream_key, extent, spread, limit, pieces=(), dtype=jnp.bfloat16):
    level = block_scale(stream_key, extent, pieces, -0.22, 0.18) if pieces else 1.0
    array = jax.random.normal(stream_key, extent, jnp.float32) * spread * level
    return jnp.minimum(jnp.maximum(array, -limit), limit).astype(dtype)


def setup_inputs(seed: int = 0) -> dict:
    splits = jax.random.split(jax.random.key(seed), 13)
    features = draw_features(jax.random.fold_in(splits[12], 71), 0)
    taste = draw_taste(jax.random.fold_in(splits[12], 71), 0)
    price = jnp.clip(jnp.exp(math.log(2.0) - 1.3862944 * jax.random.uniform(splits[2], (N_CAT, GROUP_SKUS), jnp.float32) ** block_scale(splits[2], (N_CAT, GROUP_SKUS), ((0, 4), (1, 32)), -0.2, 0.2)), 0.5, 2.0)
    alpha = jnp.clip(jnp.exp(math.log(1.0) - 1.2039728 * jax.random.uniform(splits[3], (MARKETS,), jnp.float32) ** block_scale(splits[3], (MARKETS,), ((0, 2),), -0.2, 0.2)), 0.3, 1.0)
    market_size = jnp.clip(jnp.exp(math.log(8.0) - 2.7725887 * jax.random.uniform(splits[4], (MARKETS,), jnp.float32) ** block_scale(splits[4], (MARKETS,), ((0, 2),), -0.2, 0.2)), 0.5, 8.0)
    store_brand = centred(splits[5], (N_CAT, SUB_GRP), 1.0, 4.0, ((0, 4),), jnp.float32)
    sub_scale = jnp.clip(0.45 + 0.40000004 * jax.random.uniform(splits[6], (N_CAT, SUB_GRP), jnp.float32) ** block_scale(splits[6], (N_CAT, SUB_GRP), ((0, 4),), -0.2, 0.2), 0.45, 0.85)
    cat_scale = jnp.clip(0.85 + 0.14999998 * jax.random.uniform(splits[7], (N_CAT, CAT_GRP), jnp.float32) ** block_scale(splits[7], (N_CAT, CAT_GRP), ((0, 4),), -0.2, 0.2), 0.85, 1.0)
    availability = touch_ends((jax.random.randint(splits[8], (MARKETS, N_CAT, GROUP_SKUS), 0, 4) < 3).astype(jnp.int32), jax.random.fold_in(splits[8], 1), 0, 1)
    sku_subcat = jax.vmap(lambda own: jnp.searchsorted(jnp.cumsum(ragged(own, SUB_GRP, GROUP_SKUS, GROUP_SKUS // SUB_GRP * 4, 2)), jnp.arange(GROUP_SKUS), side="right"))(jax.random.split(splits[9], N_CAT)).reshape((N_CAT, GROUP_SKUS)).astype(jnp.int32)
    subcat_cat = jax.vmap(lambda own: jnp.searchsorted(jnp.cumsum(ragged(own, CAT_GRP, SUB_GRP, SUB_GRP // CAT_GRP * 3, 2)), jnp.arange(SUB_GRP), side="right"))(jax.random.split(splits[10], N_CAT)).reshape((N_CAT, SUB_GRP)).astype(jnp.int32)
    cotangent = centred(splits[11], (MARKETS, N_CAT, GROUP_SKUS), 0.05, 0.29882812, ((0, 2), (1, 4), (2, 32)))
    return {"features": features, "taste": taste, "price": price, "alpha": alpha, "market_size": market_size, "store_brand": store_brand, "sub_scale": sub_scale, "cat_scale": cat_scale, "availability": availability, "sku_subcat": sku_subcat, "subcat_cat": subcat_cat, "cotangent": cotangent}


def segment_top(values, members, count):
    def combine(first, second):
        same = first[0] == second[0]
        return (second[0], jnp.where(same, jnp.maximum(first[1], second[1]), second[1]))

    labels = jnp.broadcast_to(members[None, :], values.shape)
    _, running = lax.associative_scan(combine, (labels, values), axis=1)
    slots = jnp.arange(count).astype(jnp.int32)
    ends = jnp.sum((members[:, None] <= slots[None, :]).astype(jnp.int32), axis=0).astype(jnp.int32) - 1
    safe = jnp.maximum(ends, 0).astype(jnp.int32)
    present = (ends >= 0) & (jnp.take(members, safe) == slots)
    return jnp.where(present[None, :], jnp.take(running, safe, axis=1), -jnp.inf)


def nest_values(features, alpha, taste_g, price_g, store_g, lam_g, rho_g, mask_g, members, parents):
    sub_count = lam_g.shape[0]
    cat_count = rho_g.shape[0]
    utility = jnp.dot(features, taste_g, preferred_element_type=jnp.float32) - alpha[:, None] * price_g[None, :]
    lam_sku = jnp.take(lam_g, members)
    scaled = utility / lam_sku[None, :]
    offered = mask_g == 1
    member_table = (members[:, None] == jnp.arange(sub_count)[None, :]).astype(jnp.float32)
    store_scaled = store_g / lam_g
    top = jnp.maximum(segment_top(jnp.where(offered, scaled, -jnp.inf), members, sub_count), store_scaled[None, :])
    weights = jnp.where(offered, jnp.exp(scaled - jnp.take(top, members, axis=1)), 0.0)
    total = jnp.dot(weights, member_table, precision=lax.Precision.HIGHEST) + jnp.exp(store_scaled[None, :] - top)
    sub_value = lam_g[None, :] * (top + jnp.log(total))
    rho_sub = jnp.take(rho_g, parents)
    ratio_sub = sub_value / rho_sub[None, :]
    parent_table = (parents[:, None] == jnp.arange(cat_count)[None, :]).astype(jnp.float32)
    cat_max = segment_top(ratio_sub, parents, cat_count)
    cat_sum = jnp.dot(jnp.exp(ratio_sub - jnp.take(cat_max, parents, axis=1)), parent_table, precision=lax.Precision.HIGHEST)
    cat_value = rho_g[None, :] * (cat_max + jnp.log(cat_sum))
    return scaled, offered, lam_sku, member_table, parent_table, rho_sub, sub_value, cat_value


def reference(features, taste, price, alpha, market_size, store_brand, sub_scale, cat_scale, availability, sku_subcat, subcat_cat, cotangent):
    taste_groups = jnp.moveaxis(taste, 1, 0)
    mask_groups = jnp.moveaxis(availability, 1, 0)
    cot_groups = jnp.moveaxis(cotangent, 1, 0)
    stacked = (taste_groups, price, store_brand, sub_scale, cat_scale, mask_groups, sku_subcat, subcat_cat)

    def upper(items):
        return nest_values(features, alpha, *items)[7]

    cat_values = lax.map(upper, stacked)
    ceiling = jnp.maximum(jnp.max(cat_values, axis=(0, 2)), 0.0)
    inclusive = ceiling + jnp.log(jnp.exp(-ceiling) + jnp.sum(jnp.exp(cat_values - ceiling[None, :, None]), axis=(0, 2)))
    all_cot = jnp.sum(jnp.where(availability == 1, cotangent.astype(jnp.float32), 0.0), axis=(1, 2))

    def lower(items):
        cot_g = items[-1]
        taste_g, price_g, store_g, lam_g, rho_g, mask_g, members, parents = items[:-1]
        scaled, offered, lam_sku, member_table, parent_table, rho_sub, sub_value, cat_value = nest_values(features, alpha, *items[:-1])
        log_within = scaled - jnp.take(sub_value / lam_g[None, :], members, axis=1)
        log_sub = (sub_value - jnp.take(cat_value, parents, axis=1)) / rho_sub[None, :]
        log_cat = cat_value - inclusive[:, None]
        log_path = log_within + jnp.take(log_sub + jnp.take(log_cat, parents, axis=1), members, axis=1)
        log_demand = jnp.where(offered, jnp.log(market_size)[:, None] + log_path, 0.0)
        cot = jnp.where(offered, cot_g.astype(jnp.float32), 0.0)
        sub_cot = jnp.dot(cot, member_table, precision=lax.Precision.HIGHEST)
        cat_cot = jnp.dot(sub_cot, parent_table, precision=lax.Precision.HIGHEST)
        d_cat = (1.0 - 1.0 / rho_g[None, :]) * cat_cot - all_cot[:, None] * jnp.exp(log_cat)
        d_sub = (1.0 / rho_sub[None, :] - 1.0 / lam_g[None, :]) * sub_cot + jnp.exp(log_sub) * jnp.take(d_cat, parents, axis=1)
        d_util = jnp.where(offered, cot / lam_sku[None, :] + jnp.exp(log_within) * jnp.take(d_sub, members, axis=1), 0.0)
        grad = -jnp.dot(alpha, d_util, precision=lax.Precision.HIGHEST)
        return log_demand, grad

    log_groups, grads = lax.map(lower, stacked + (cot_groups,))
    return jnp.moveaxis(log_groups, 0, 1), grads
```

```python
import functools

import jax
import jax.numpy as jnp
from jax import lax
from jax.experimental import pallas as pl
from jax.experimental.pallas import tpu as pltpu
from jax.sharding import PartitionSpec as P

F32 = jnp.float32
BF16 = jnp.bfloat16
NEG = -1e30
EMPTY = -1e29
SAFE = 60.0
LANES = 128
CHUNK = 256
MESH = pl.DeviceIdType.MESH
NT = (((1,), (1,)), ((), ()))


def dot(a, b):
    return jnp.dot(a, b, preferred_element_type=F32)


def dot_nt(a, b):
    return lax.dot_general(a, b, NT, preferred_element_type=F32)


def iota(shape, dim):
    return lax.broadcasted_iota(jnp.int32, shape, dim)


def lse2(a, b):
    top = jnp.maximum(a, b)
    return top + jnp.log(1.0 + jnp.exp(jnp.minimum(a, b) - top))


def halves(x):
    high = x.astype(BF16)
    return high, (x - high.astype(F32)).astype(BF16)


def thirds(x):
    high = x.astype(BF16)
    rest = x - high.astype(F32)
    mid = rest.astype(BF16)
    return high, mid, (rest - mid.astype(F32)).astype(BF16)


def column(row):
    n = row.shape[1]
    return jnp.sum(jnp.where(iota((n, n), 0) == iota((n, n), 1), row, 0.0), axis=1, keepdims=True)


def nest_columns(lam_ref, store_ref, rho_ref, par_ref):
    lam = column(lam_ref[...])
    store = column(store_ref[...]) / lam
    par = column(par_ref[...].astype(F32))
    subs, cats = lam_ref.shape[1], rho_ref.shape[1]
    mine = par == iota((subs, cats), 1).astype(F32)
    rho = jnp.sum(jnp.where(mine, rho_ref[...], 0.0), axis=1, keepdims=True)
    return lam, 1.0 / lam, store, par, 1.0 / rho


def local_kernel(
    feat_ref, taste_ref, price_ref, alpha_ref, lam_ref, store_ref, rho_ref, par_ref, avail_ref, mem_ref, cot_ref,
    ms_ref, wh_ref, wl_ref, lst_ref, r_ref, c_ref, part_ref, left_ref, right_ref, own_ref, cg_ref,
    table, inv_ref, cols, acc, cotacc, sums,
):
    step = pl.program_id(0)
    subs = lam_ref.shape[1]
    cats = rho_ref.shape[1]
    width = mem_ref.shape[1]
    tiles = width // LANES

    @pl.when(step == 0)
    def _():
        lam, ilam, store, par, irho = nest_columns(lam_ref, store_ref, rho_ref, par_ref)
        cols[0] = jnp.broadcast_to(lam, (subs, LANES))
        cols[1] = jnp.broadcast_to(store, (subs, LANES))
        cols[2] = jnp.broadcast_to(par, (subs, LANES))
        cols[3] = jnp.broadcast_to(irho, (subs, LANES))
        for k in range(width // CHUNK):
            at = pl.ds(k * CHUNK, CHUNK)
            hit = iota((subs, CHUNK), 0) == mem_ref[:, at]
            table[:, at] = jnp.where(hit, 1.0, 0.0).astype(BF16)
            lam_j = jnp.sum(jnp.where(hit, lam, 0.0), axis=0, keepdims=True)
            inv = 1.0 / lam_j
            inv_ref[0:1, at] = inv
            inv_ref[1:2, at] = inv * price_ref[:, at]
        acc[...] = jnp.zeros_like(acc)

    alpha_row = alpha_ref[...]
    alpha = jnp.transpose(jnp.broadcast_to(alpha_row, (LANES, LANES)))
    alpha2 = jnp.concatenate([alpha, alpha], axis=1)
    ah, al = halves(alpha_row)
    pick = iota((16, LANES), 0)
    alpha_rows = jnp.where(pick == 0, ah.astype(F32), jnp.where(pick == 1, al.astype(F32), 0.0)).astype(BF16)
    feats = feat_ref[...]
    worst = jnp.zeros((8, CHUNK), F32)
    total = jnp.zeros((subs, 2 * LANES), F32)
    cot_total = jnp.zeros((subs, LANES), F32)
    for k in range(width // CHUNK):
        at = pl.ds(k * CHUNK, CHUNK)
        util = dot(feats, taste_ref[:, at])
        scaled = util * inv_ref[0:1, at] - alpha2 * inv_ref[1:2, at]
        open_ = jnp.concatenate(
            [avail_ref[pl.ds(k * (CHUNK // LANES) + t, LANES, stride=tiles), :] for t in range(CHUNK // LANES)], axis=1
        )
        masked = jnp.where(open_ == 1, scaled, NEG)
        ms_ref[:, at] = masked
        worst = jnp.maximum(worst, jnp.max(jnp.abs(scaled).reshape(LANES // 8, 8, CHUNK), axis=0))
        wh, wl = halves(jnp.exp(masked))
        wh_ref[:, at] = wh
        wl_ref[:, at] = wl
        cotm = cot_ref[:, at] * open_.astype(F32).astype(BF16)
        total = total + dot_nt(table[:, at], jnp.concatenate([wh, wl], axis=0))
        cot_total = cot_total + dot_nt(table[:, at], cotm)
        acc[:, at] += dot(alpha_rows, cotm)
    sums[...] = total[:, :LANES] + total[:, LANES:]
    r_ref[...] = jnp.zeros_like(r_ref)

    @pl.when(jnp.max(worst) > SAFE)
    def _():
        lane = iota((1, LANES), 1)
        carry = jnp.full((LANES, 1), NEG, F32)
        carry_id = jnp.full((1, 1), -1, jnp.int32)
        peak = jnp.zeros((LANES, subs), F32)
        for t in range(tiles):
            at = pl.ds(t * LANES, LANES)
            ids = mem_ref[:, at]
            run = ms_ref[:, at]
            shift = 1
            while shift < LANES:
                same = (pltpu.roll(ids, shift, 1) == ids) & (lane >= shift)
                run = jnp.where(same, jnp.maximum(run, pltpu.roll(run, shift, 1)), run)
                shift *= 2
            run = jnp.where(ids == carry_id, jnp.maximum(run, carry), run)
            carry = run[:, LANES - 1 :]
            carry_id = ids[:, LANES - 1 :]
            if t + 1 < tiles:
                following = mem_ref[:, pl.ds((t + 1) * LANES, LANES)][:, 0:1]
            else:
                following = jnp.full((1, 1), -1, jnp.int32)
            nxt = jnp.where(lane == LANES - 1, following, pltpu.roll(ids, LANES - 1, 1))
            ends = jnp.where((iota((subs, LANES), 0) == ids) & (ids != nxt), 1.0, 0.0).astype(BF16)
            peak = peak + dot_nt(run.astype(BF16), ends)
        peak = jnp.where(peak < EMPTY, 0.0, peak)
        r_ref[...] = jnp.transpose(peak)
        peak_half = peak.astype(BF16)
        total = jnp.zeros((subs, 2 * LANES), F32)
        for t in range(tiles):
            at = pl.ds(t * LANES, LANES)
            wh, wl = halves(jnp.exp(ms_ref[:, at] - dot(peak_half, table[:, at])))
            wh_ref[:, at] = wh
            wl_ref[:, at] = wl
            total = total + dot_nt(table[:, at], jnp.concatenate([wh, wl], axis=0))
        sums[...] = total[:, :LANES] + total[:, LANES:]

    total = sums[...]
    raw = jnp.where(total > 0.0, r_ref[...] + jnp.log(jnp.where(total > 0.0, total, 1.0)), NEG)
    lam, store, par, irho = cols[0], cols[1], cols[2], cols[3]
    full = lse2(raw, store)
    lst_ref[...] = full
    c_ref[...] = cot_total
    row = iota((subs, LANES), 0)
    ids = mem_ref[...]
    first, last = ids[:, 0:1], ids[:, width - 1 :]
    is_first, is_last = row == first, row == last
    factor = lam * irho
    ratio = jnp.where((row > first) & (row < last), full * factor, NEG)
    spread = jnp.full((subs, LANES), NEG, F32)
    tops = []
    for c in range(cats):
        hit = par == c
        top = jnp.max(jnp.where(hit, ratio, NEG), axis=0, keepdims=True)
        tops.append(top)
        spread = jnp.where(hit, top, spread)
    terms = jnp.where(ratio > EMPTY, jnp.exp(ratio - spread), 0.0)
    for c in range(cats):
        hit = par == c
        amount = jnp.sum(jnp.where(hit, terms, 0.0), axis=0, keepdims=True)
        part_ref[0, c : c + 1, :] = jnp.where(amount > 0.0, tops[c] + jnp.log(jnp.maximum(amount, 1.0)), NEG)
        part_ref[0, cats + c : cats + c + 1, :] = jnp.sum(jnp.where(hit, cot_total, 0.0), axis=0, keepdims=True)

    def at_row(mask, values):
        return jnp.sum(jnp.where(mask, values, 0.0), axis=0, keepdims=True)

    first_id = jnp.broadcast_to(first.astype(F32), (1, LANES))
    last_id = jnp.broadcast_to(last.astype(F32), (1, LANES))
    blank = jnp.zeros((5, LANES), F32)
    left_ref[0] = jnp.concatenate([at_row(is_first, raw), at_row(is_first, cot_total), first_id, blank], axis=0)
    right_ref[0] = jnp.concatenate([at_row(is_last, raw), at_row(is_last, cot_total), last_id, blank], axis=0)
    own_ref[0] = jnp.concatenate(
        [
            at_row(is_first, store), at_row(is_first, factor), at_row(is_first, par),
            at_row(is_last, store), at_row(is_last, factor), at_row(is_last, par),
            first_id, last_id,
        ],
        axis=0,
    )

    @pl.when(step == pl.num_programs(0) - 1)
    def _():
        cg_ref[...] = jnp.sum(acc[...], axis=0, keepdims=True) * inv_ref[0:1, :]


def merge(logs):
    top = functools.reduce(jnp.maximum, logs)
    return top + jnp.log(sum(jnp.exp(value - top) for value in logs))


def swap_kernel(
    ny, nz, nx, part_ref, left_ref, right_ref, own_ref, rho_ref,
    cv_ref, nbl_ref, nbr_ref,
    pq, ybuf, qbuf, zbuf, xsrc, xbuf, cvs,
    nb_send, nb_recv, y_send, y_recv, z_send, z_recv, x_send, x_recv, g_send, g_recv,
):
    cats = rho_ref.shape[1]
    sku = lax.axis_index("sku")
    cat = lax.axis_index("cat")
    y, z = sku // nz, sku % nz
    n = ny * nz
    to_right, to_left = (sku + 1) % n, (sku + n - 1) % n
    along_y = [((y + k) % ny) * nz + z for k in range(1, ny)]
    along_z = [y * nz + (z + k) % nz for k in range(1, nz)]
    along_x = [(cat + k) % nx for k in range(1, nx)]

    barrier = pltpu.get_barrier_semaphore()
    for other in [to_right, to_left] + along_y + along_z:
        pl.semaphore_signal(barrier, inc=1, device_id={"sku": other}, device_id_type=MESH)
    for other in along_x:
        pl.semaphore_signal(barrier, inc=1, device_id={"cat": other}, device_id_type=MESH)
    pl.semaphore_wait(barrier, 2 + len(along_y) + len(along_z) + len(along_x))

    def send(src, dst, send_sem, recv_sem, device):
        copy = pltpu.make_async_remote_copy(
            src_ref=src, dst_ref=dst, send_sem=send_sem, recv_sem=recv_sem, device_id=device, device_id_type=MESH
        )
        copy.start()
        return copy

    rounds = [
        send(right_ref, nbl_ref, nb_send.at[0], nb_recv.at[0], {"sku": to_right}),
        send(left_ref, nbr_ref, nb_send.at[1], nb_recv.at[1], {"sku": to_left}),
    ]
    for copy in rounds:
        copy.wait_recv()
    own = own_ref[...]
    from_left, from_right = nbl_ref[...], nbr_ref[...]
    first_id, last_id = own[:, 6:7], own[:, 7:8]
    first = left_ref[:, 0:1, :]
    first = jnp.where(from_left[:, 2:3] == first_id, lse2(first, from_left[:, 0:1]), first)
    first = lse2(first, own[:, 0:1]) * own[:, 1:2]
    last = lse2(right_ref[:, 0:1, :], own[:, 3:4]) * own[:, 4:5]
    last = jnp.where((from_right[:, 2:3] == last_id) | (first_id == last_id), NEG, last)
    which = iota((ny, cats, LANES), 1).astype(F32)
    pq[:, 0:cats, :] = merge(
        [
            part_ref[:, 0:cats, :],
            jnp.where(which == own[:, 2:3], first, NEG),
            jnp.where(which == own[:, 5:6], last, NEG),
        ]
    )
    pq[:, cats:, :] = part_ref[:, cats:, :]

    copies = []
    for k in range(1, ny):
        copies.append(send(pq.at[(y + k) % ny], ybuf.at[k], y_send.at[k], y_recv.at[k], {"sku": along_y[k - 1]}))
    for copy in copies:
        copy.wait_recv()
    rounds += copies
    pieces = [pq[y]] + [ybuf[k] for k in range(1, ny)]
    qbuf[0:cats, :] = merge([piece[0:cats] for piece in pieces])
    qbuf[cats:, :] = sum(piece[cats:] for piece in pieces)

    copies = []
    for k in range(1, nz):
        copies.append(send(qbuf, zbuf.at[k], z_send.at[k], z_recv.at[k], {"sku": along_z[k - 1]}))
    for copy in copies:
        copy.wait_recv()
    rounds += copies
    pieces = [qbuf[...]] + [zbuf[k] for k in range(1, nz)]
    rho = column(rho_ref[...])
    value = rho * merge([piece[0:cats] for piece in pieces])
    cat_cot = sum(piece[cats:] for piece in pieces)
    top = jnp.max(value, axis=0, keepdims=True)
    group = top + jnp.log(jnp.sum(jnp.exp(value - top), axis=0, keepdims=True))
    xsrc[...] = jnp.concatenate(
        [group, jnp.sum(cat_cot, axis=0, keepdims=True), jnp.zeros((6, LANES), F32)], axis=0
    )

    copies = []
    for k in range(1, nx):
        copies.append(send(xsrc, xbuf.at[k], x_send.at[k], x_recv.at[k], {"cat": along_x[k - 1]}))
    for copy in copies:
        copy.wait_recv()
    rounds += copies
    pieces = [xsrc[...]] + [xbuf[k] for k in range(1, nx)]
    inclusive = merge([jnp.zeros((1, LANES), F32)] + [piece[0:1] for piece in pieces])
    all_cot = sum(piece[1:2] for piece in pieces)
    cvs[0:cats, :] = value
    cvs[cats : 2 * cats, :] = (1.0 - 1.0 / rho) * cat_cot - all_cot * jnp.exp(value - inclusive)
    cvs[2 * cats :, :] = jnp.broadcast_to(inclusive, (8, LANES))
    cv_ref[y] = cvs[...]

    copies = []
    for k in range(1, ny):
        copies.append(send(cvs, cv_ref.at[y], g_send.at[k], g_recv.at[k], {"sku": along_y[k - 1]}))
    for k, copy in enumerate(copies):
        copy.wait_recv()
    rounds += copies
    for copy in rounds:
        copy.wait_send()


def slope_kernel(
    wh_ref, wl_ref, lst_ref, r_ref, c_ref, cv_ref, nbl_ref, nbr_ref, own_ref, cg_ref, mem_ref, alpha_ref, size_ref,
    lam_ref, store_ref, rho_ref, par_ref,
    grad_ref, path_ref,
    hs,
):
    subs, cats = lam_ref.shape[1], rho_ref.shape[1]
    blocks = cv_ref.shape[0]
    width = mem_ref.shape[1]
    lam, ilam, _, par, irho = nest_columns(lam_ref, store_ref, rho_ref, par_ref)
    parents = jnp.where((iota((subs, 3 * cats), 1) % cats).astype(F32) == par, 1.0, 0.0).astype(BF16)
    row = iota((subs, LANES), 0).astype(F32)
    for b in range(blocks):
        at = pl.ds(b * LANES, LANES)
        own, from_left, from_right = own_ref[b], nbl_ref[b], nbr_ref[b]
        cv = cv_ref[b]
        left_hit = (row == own[6:7]) & (from_left[2:3] == own[6:7])
        right_hit = (row == own[7:8]) & (from_right[2:3] == own[7:8])
        extra = jnp.where(left_hit, from_left[0:1], jnp.where(right_hit, from_right[0:1], NEG))
        level = lse2(lst_ref[:, at], extra)
        sub_cot = c_ref[:, at] + jnp.where(left_hit, from_left[1:2], jnp.where(right_hit, from_right[1:2], 0.0))
        cat_value = dot(parents, jnp.concatenate(thirds(cv[0:cats]), axis=0))
        d_cat = dot(parents, jnp.concatenate(thirds(cv[cats : 2 * cats]), axis=0))
        inclusive = cv[2 * cats : 2 * cats + 1]
        log_sub = (lam * level - cat_value) * irho
        path = jnp.log(size_ref[:, at]) - level + log_sub + (cat_value - inclusive)
        d_sub = (irho - ilam) * sub_cot + jnp.exp(log_sub) * d_cat
        slope = alpha_ref[:, at] * jnp.exp(r_ref[:, at] - level) * d_sub
        hs[0:subs, at], hs[subs:, at] = halves(slope)
        ph, plo = halves(jnp.transpose(path))
        path_ref[at, 0:subs] = ph
        path_ref[at, subs:] = plo
    for k in range(width // CHUNK):
        at = pl.ds(k * CHUNK, CHUNK)
        both = dot(hs[...], wh_ref[:, at])
        found = both[0:subs] + both[subs:] + dot(hs[0:subs, :], wl_ref[:, at])
        hit = iota((subs, CHUNK), 0) == mem_ref[:, at]
        grad_ref[:, at] = -(jnp.sum(jnp.where(hit, found, 0.0), axis=0, keepdims=True) + cg_ref[:, at])


def demand_kernel(ms_ref, path_ref, mem_ref, out_ref, table):
    width = mem_ref.shape[1]
    depth = path_ref.shape[1]
    tiles = width // LANES
    step = pl.program_id(0)

    @pl.when(step == 0)
    def _():
        for k in range(width // CHUNK):
            at = pl.ds(k * CHUNK, CHUNK)
            hit = iota((depth, CHUNK), 0) % (depth // 2) == mem_ref[:, at]
            table[:, at] = jnp.where(hit, 1.0, 0.0).astype(BF16)

    rows = pl.ds(pl.multiple_of(step * LANES, LANES), LANES)
    path = path_ref[rows, :]
    for k in range(width // CHUNK):
        at = pl.ds(k * CHUNK, CHUNK)
        masked = ms_ref[rows, at]
        value = jnp.where(masked > EMPTY, masked + dot(path, table[:, at]), 0.0)
        for t in range(CHUNK // LANES):
            out_ref[pl.ds(k * (CHUNK // LANES) + t, LANES, stride=tiles), :] = value[:, t * LANES : (t + 1) * LANES]


def whole(shape=None):
    return pl.BlockSpec(memory_space=pltpu.VMEM)


def shards(
    n_sku, n_cat, features, taste, price, alpha, market_size, store_brand, sub_scale, cat_scale, availability,
    sku_subcat, subcat_cat, cotangent,
):
    markets, depth = features.shape
    width = price.shape[1]
    subs, cats = sub_scale.shape[1], cat_scale.shape[1]
    tiles = width // LANES
    blocks = markets // LANES
    ny, nz = blocks, n_sku // blocks
    alpha_row = alpha.reshape(1, markets)
    size_row = market_size.reshape(1, markets)
    avail = availability.reshape(markets * tiles, LANES)
    taste2 = taste.reshape(depth, width)
    cot2 = cotangent.reshape(markets, width)

    def fixed(shape):
        return pl.BlockSpec(shape, lambda i: (0,) * len(shape))

    row_block = pl.BlockSpec((LANES, width), lambda i: (i, 0))
    col_block = pl.BlockSpec((subs, LANES), lambda i: (0, i))
    tile_block = pl.BlockSpec((1, 8, LANES), lambda i: (i, 0, 0))
    sds = jax.ShapeDtypeStruct
    ms, wh, wl, lst, r, c, part, left, right, own, cg = pl.pallas_call(
        local_kernel,
        grid=(blocks,),
        in_specs=[
            pl.BlockSpec((LANES, depth), lambda i: (i, 0)),
            fixed((depth, width)),
            fixed((1, width)),
            pl.BlockSpec((1, LANES), lambda i: (0, i)),
            fixed((1, subs)),
            fixed((1, subs)),
            fixed((1, cats)),
            fixed((1, subs)),
            pl.BlockSpec((LANES * tiles, LANES), lambda i: (i, 0)),
            fixed((1, width)),
            row_block,
        ],
        out_shape=[
            sds((markets, width), F32),
            sds((markets, width), BF16),
            sds((markets, width), BF16),
            sds((subs, markets), F32),
            sds((subs, markets), F32),
            sds((subs, markets), F32),
            sds((blocks, 2 * cats, LANES), F32),
            sds((blocks, 8, LANES), F32),
            sds((blocks, 8, LANES), F32),
            sds((blocks, 8, LANES), F32),
            sds((1, width), F32),
        ],
        out_specs=[
            row_block, row_block, row_block, col_block, col_block, col_block,
            pl.BlockSpec((1, 2 * cats, LANES), lambda i: (i, 0, 0)),
            tile_block, tile_block, tile_block, fixed((1, width)),
        ],
        scratch_shapes=[
            pltpu.VMEM((subs, width), BF16),
            pltpu.VMEM((8, width), F32),
            pltpu.VMEM((4, subs, LANES), F32),
            pltpu.VMEM((16, width), F32),
            pltpu.VMEM((8, LANES), F32),
            pltpu.VMEM((subs, LANES), F32),
        ],
        compiler_params=pltpu.CompilerParams(vmem_limit_bytes=28 * 1024 * 1024),
        name="local_nests",
    )(
        features, taste2, price, alpha_row, sub_scale, store_brand, cat_scale, subcat_cat, avail, sku_subcat, cot2
    )

    cv, nbl, nbr = pl.pallas_call(
        functools.partial(swap_kernel, ny, nz, n_cat),
        in_specs=[whole()] * 5,
        out_specs=[whole()] * 3,
        out_shape=[
            sds((ny, 2 * cats + 8, LANES), F32),
            sds((ny, 8, LANES), F32),
            sds((ny, 8, LANES), F32),
        ],
        scratch_shapes=[
            pltpu.VMEM((ny, 2 * cats, LANES), F32),
            pltpu.VMEM((ny, 2 * cats, LANES), F32),
            pltpu.VMEM((2 * cats, LANES), F32),
            pltpu.VMEM((nz, 2 * cats, LANES), F32),
            pltpu.VMEM((8, LANES), F32),
            pltpu.VMEM((n_cat, 8, LANES), F32),
            pltpu.VMEM((2 * cats + 8, LANES), F32),
        ]
        + [pltpu.SemaphoreType.DMA((count,)) for count in (2, ny, nz, n_cat, ny) for _ in range(2)],
        compiler_params=pltpu.CompilerParams(
            collective_id=0, has_side_effects=True, vmem_limit_bytes=8 * 1024 * 1024
        ),
        name="swap_nests",
    )(part, left, right, own, cat_scale)

    grad, path = pl.pallas_call(
        slope_kernel,
        in_specs=[whole()] * 17,
        out_specs=[whole()] * 2,
        out_shape=[sds((1, width), F32), sds((markets, 2 * subs), BF16)],
        scratch_shapes=[pltpu.VMEM((2 * subs, markets), BF16)],
        compiler_params=pltpu.CompilerParams(vmem_limit_bytes=16 * 1024 * 1024),
        name="price_slope",
    )(
        wh, wl, lst, r, c, cv, nbl, nbr, own, cg, sku_subcat, alpha_row, size_row, sub_scale, store_brand, cat_scale,
        subcat_cat,
    )
    other = lax.ppermute(grad, "mkt", [(0, 1), (1, 0)])

    demand = pl.pallas_call(
        demand_kernel,
        grid=(blocks,),
        in_specs=[whole(), whole(), whole()],
        out_specs=pl.BlockSpec((LANES * tiles, LANES), lambda i: (i, 0)),
        out_shape=sds((markets * tiles, LANES), F32),
        scratch_shapes=[pltpu.VMEM((2 * subs, width), BF16)],
        compiler_params=pltpu.CompilerParams(vmem_limit_bytes=16 * 1024 * 1024),
        cost_estimate=pl.CostEstimate(
            flops=2 * markets * width * 2 * subs, bytes_accessed=8 * markets * width, transcendentals=0
        ),
        name="log_demand",
    )(ms, path, sku_subcat)
    return demand.reshape(markets, 1, width), grad + other


def solution(mesh):
    return jax.shard_map(
        functools.partial(shards, mesh.shape["sku"], mesh.shape["cat"]),
        mesh=mesh,
        in_specs=(
            P("mkt", None),
            P(None, "cat", "sku"),
            P("cat", "sku"),
            P("mkt"),
            P("mkt"),
            P("cat", None),
            P("cat", None),
            P("cat", None),
            P("mkt", "cat", "sku"),
            P("cat", "sku"),
            P("cat", None),
            P("mkt", "cat", "sku"),
        ),
        out_specs=(P("mkt", "cat", "sku"), P("cat", "sku")),
        check_vma=False,
    )
```

```python
import functools

import jax
import jax.numpy as jnp
from jax import lax
from jax.experimental import pallas as pl
from jax.experimental.pallas import tpu as pltpu
from jax.sharding import PartitionSpec as P

F32 = jnp.float32
BF16 = jnp.bfloat16
NEG = -1e30
EMPTY = -1e29
SAFE = 60.0
LANES = 128
CHUNK = 256
MESH = pl.DeviceIdType.MESH
NT = (((1,), (1,)), ((), ()))


def dot(a, b):
    return jnp.dot(a, b, preferred_element_type=F32)


def dot_nt(a, b):
    return lax.dot_general(a, b, NT, preferred_element_type=F32)


def iota(shape, dim):
    return lax.broadcasted_iota(jnp.int32, shape, dim)


def lse2(a, b):
    top = jnp.maximum(a, b)
    return top + jnp.log(1.0 + jnp.exp(jnp.minimum(a, b) - top))


def halves(x):
    high = x.astype(BF16)
    return high, (x - high.astype(F32)).astype(BF16)


def thirds(x):
    high = x.astype(BF16)
    rest = x - high.astype(F32)
    mid = rest.astype(BF16)
    return high, mid, (rest - mid.astype(F32)).astype(BF16)


def column(row):
    n = row.shape[1]
    return jnp.sum(jnp.where(iota((n, n), 0) == iota((n, n), 1), row, 0.0), axis=1, keepdims=True)


def nest_columns(lam_ref, store_ref, rho_ref, par_ref):
    lam = column(lam_ref[...])
    store = column(store_ref[...]) / lam
    par = column(par_ref[...].astype(F32))
    subs, cats = lam_ref.shape[1], rho_ref.shape[1]
    mine = par == iota((subs, cats), 1).astype(F32)
    rho = jnp.sum(jnp.where(mine, rho_ref[...], 0.0), axis=1, keepdims=True)
    return lam, 1.0 / lam, store, par, 1.0 / rho


def pack(low, high):
    left = iota(low.shape, 1) < LANES // 2
    return jnp.where(left, low, turn(high)), jnp.where(left, turn(low), high)


def turn(x):
    return pltpu.roll(x, LANES // 2, 1)


def local_kernel(
    feat_hbm, taste_hbm, price_hbm, alpha_hbm, size_hbm, lam_hbm, store_hbm, rho_hbm, par_hbm, avail_hbm, mem_hbm,
    cot_hbm,
    ms_ref, wh_ref, wl_ref, cotm_ref, sums, peaks, table, table_t, cols, rows_ref, rho_rows, ids_ref, inv_ref,
    feat, taste, price, lam_row, store_row, rho_row, par_row, avail, size, worst,
    small_sem, big_sem, avail_sem, cot_sem,
):
    subs = lam_row.shape[1]
    cats = rho_row.shape[1]
    width = ids_ref.shape[1]
    blocks = ms_ref.shape[0] // LANES
    tiles = width // LANES
    small = [
        (mem_hbm, ids_ref), (lam_hbm, lam_row), (price_hbm, price), (store_hbm, store_row), (rho_hbm, rho_row),
        (par_hbm, par_row), (alpha_hbm, rows_ref.at[0:1]), (size_hbm, size),
    ]
    small = [pltpu.make_async_copy(src, dst, small_sem.at[k]) for k, (src, dst) in enumerate(small)]
    big = [
        pltpu.make_async_copy(src, dst, big_sem.at[k])
        for k, (src, dst) in enumerate([(feat_hbm, feat), (taste_hbm, taste)])
    ]

    def fetch(b):
        rows = pl.ds(pl.multiple_of(b * LANES, LANES), LANES)
        return (
            pltpu.make_async_copy(avail_hbm.at[rows, 0, :], avail.at[rows], avail_sem.at[b]),
            pltpu.make_async_copy(cot_hbm.at[rows], cotm_ref.at[rows], cot_sem.at[b]),
        )

    for copy in small + big:
        copy.start()
    for b in range(blocks):
        for copy in fetch(b):
            copy.start()
    for copy in small:
        copy.wait()

    lam = column(lam_row[...])
    for k in range(width // CHUNK):
        at = pl.ds(k * CHUNK, CHUNK)
        hit = iota((subs, CHUNK), 0) == ids_ref[:, at]
        ones = jnp.where(hit, 1.0, 0.0)
        table[:, at] = ones.astype(BF16)
        table_t[at, :] = jnp.transpose(ones).astype(BF16)
        inv = 1.0 / jnp.sum(jnp.where(hit, lam, 0.0), axis=0, keepdims=True)
        inv_ref[0:1, at] = inv
        inv_ref[1:2, at] = inv * price[:, at]
    _, ilam, store, par, irho = nest_columns(lam_row, store_row, rho_row, par_row)
    for k, col in enumerate((lam, store, par, irho, ilam)):
        cols[k] = jnp.broadcast_to(col, (subs, LANES))
    rho = jnp.broadcast_to(column(rho_row[...]), (cats, LANES))
    rho_rows[0:8, :] = jnp.where(iota((8, LANES), 1) < LANES // 2, rho[0:8], rho[8:16])
    rho_rows[8:24, :] = rho
    rows_ref[1:2, :] = jnp.log(size[...])
    worst[...] = jnp.zeros_like(worst)
    peaks[...] = jnp.zeros_like(peaks)
    for copy in big:
        copy.wait()

    @pl.loop(0, blocks)
    def _(b):
        mine = pl.ds(pl.multiple_of(b * LANES, LANES), LANES)
        for copy in fetch(b):
            copy.wait()
        alpha = jnp.transpose(jnp.broadcast_to(rows_ref[0:1, mine], (LANES, LANES)))
        alpha2 = jnp.concatenate([alpha, alpha], axis=1)
        total = jnp.zeros((2 * LANES, subs), F32)
        most = jnp.zeros((8, CHUNK), F32)
        for k in range(width // CHUNK):
            at = pl.ds(k * CHUNK, CHUNK)
            util = dot(feat[mine, :], taste[:, at])
            scaled = util * inv_ref[0:1, at] - alpha2 * inv_ref[1:2, at]
            open_ = avail[mine, at]
            masked = jnp.where(open_ == 1, scaled, NEG)
            ms_ref[mine, at] = masked
            most = jnp.maximum(most, jnp.max(jnp.abs(scaled).reshape(LANES // 8, 8, CHUNK), axis=0))
            wh, wl = halves(jnp.exp(masked))
            wh_ref[mine, at] = wh
            wl_ref[mine, at] = wl
            cotm_ref[mine, at] = cotm_ref[mine, at] * open_.astype(F32).astype(BF16)
            total = total + dot(jnp.concatenate([wh, wl], axis=0), table_t[at, :])
        sums[:, mine] = jnp.transpose(total[:LANES] + total[LANES:])
        worst[...] = jnp.maximum(worst[...], most)

    @pl.when(jnp.max(worst[...]) > SAFE)
    def _():
        lane = iota((1, LANES), 1)

        @pl.loop(0, blocks)
        def _(b):
            mine = pl.ds(pl.multiple_of(b * LANES, LANES), LANES)
            carry = jnp.full((LANES, 1), NEG, F32)
            carry_id = jnp.full((1, 1), -1, jnp.int32)
            peak = jnp.zeros((LANES, subs), F32)
            for t in range(tiles):
                at = pl.ds(t * LANES, LANES)
                ids = ids_ref[:, at]
                run = ms_ref[mine, at]
                shift = 1
                while shift < LANES:
                    same = (pltpu.roll(ids, shift, 1) == ids) & (lane >= shift)
                    run = jnp.where(same, jnp.maximum(run, pltpu.roll(run, shift, 1)), run)
                    shift *= 2
                run = jnp.where(ids == carry_id, jnp.maximum(run, carry), run)
                carry = run[:, LANES - 1 :]
                carry_id = ids[:, LANES - 1 :]
                if t + 1 < tiles:
                    following = ids_ref[:, pl.ds((t + 1) * LANES, LANES)][:, 0:1]
                else:
                    following = jnp.full((1, 1), -1, jnp.int32)
                nxt = jnp.where(lane == LANES - 1, following, pltpu.roll(ids, LANES - 1, 1))
                ends = jnp.where((iota((subs, LANES), 0) == ids) & (ids != nxt), 1.0, 0.0).astype(BF16)
                peak = peak + dot_nt(run.astype(BF16), ends)
            peak = jnp.where(peak < EMPTY, 0.0, peak)
            peaks[:, mine] = jnp.transpose(peak)
            peak_half = peak.astype(BF16)
            total = jnp.zeros((2 * LANES, subs), F32)
            for t in range(tiles):
                at = pl.ds(t * LANES, LANES)
                wh, wl = halves(jnp.exp(ms_ref[mine, at] - dot(peak_half, table[:, at])))
                wh_ref[mine, at] = wh
                wl_ref[mine, at] = wl
                total = total + dot(jnp.concatenate([wh, wl], axis=0), table_t[at, :])
            sums[:, mine] = jnp.transpose(total[:LANES] + total[LANES:])


def condense(b, sums, peaks, cotm_ref, table_t, cols, ids_ref, part_ref, left_ref, right_ref, lst_ref, c_ref):
    cats = 16
    subs = sums.shape[0]
    width = ids_ref.shape[1]
    mine = pl.ds(b * LANES, LANES)
    total = sums[:, mine]
    raw = jnp.where(total > 0.0, peaks[:, mine] + jnp.log(jnp.where(total > 0.0, total, 1.0)), NEG)
    lam, store, par, irho = cols[0], cols[1], cols[2], cols[3]
    cot_total = jnp.transpose(dot(cotm_ref[mine, :], table_t[...]))
    full = lse2(raw, store)
    lst_ref[:, mine] = full
    c_ref[:, mine] = cot_total
    row = iota((subs, LANES), 0)
    first, last = ids_ref[:, 0:1], ids_ref[:, width - 1 :]
    is_first, is_last = row == first, row == last
    factor = lam * irho
    ratio_all = full * factor
    ratio = jnp.where((row > first) & (row < last), ratio_all, NEG)
    spread = jnp.full((subs, LANES), NEG, F32)
    tops = []
    for c in range(cats):
        hit = par == c
        top = jnp.max(jnp.where(hit, ratio, NEG), axis=0, keepdims=True)
        tops.append(top)
        spread = jnp.where(hit, top, spread)
    tops = jnp.concatenate(tops, axis=0)
    terms = jnp.where(ratio > EMPTY, jnp.exp(ratio - spread), 0.0)
    children = jnp.where(iota((subs, LANES), 1).astype(F32) == par, 1.0, 0.0)
    children = jnp.transpose(children)[0:cats].astype(BF16)
    found = dot(children, jnp.concatenate(halves(terms) + thirds(cot_total), axis=1))
    amount = found[:, 0:LANES] + found[:, LANES : 2 * LANES]
    cat_cot = found[:, 2 * LANES : 3 * LANES] + found[:, 3 * LANES : 4 * LANES] + found[:, 4 * LANES :]
    logs = jnp.where(amount > 0.0, tops + jnp.log(jnp.where(amount > 0.0, amount, 1.0)), NEG)

    def at_row(mask, values):
        return jnp.sum(jnp.where(mask, values, 0.0), axis=0, keepdims=True)

    first_id = jnp.broadcast_to(first.astype(F32), (1, LANES))
    last_id = jnp.broadcast_to(last.astype(F32), (1, LANES))
    blank = jnp.zeros((5, LANES), F32)
    low = at_row(is_first, raw)
    left_ref[b] = jnp.concatenate([low, at_row(is_first, cot_total), first_id, blank], axis=0)
    right_ref[b] = jnp.concatenate([at_row(is_last, raw), at_row(is_last, cot_total), last_id, blank], axis=0)
    ends = jnp.concatenate(
        [
            low, at_row(is_last, full), at_row(is_first, ratio_all), first_id, last_id,
            at_row(is_last, factor), at_row(is_first, par), at_row(is_last, par),
        ],
        axis=0,
    )
    pairs = ((logs[0:8], logs[8:16]), (cat_cot[0:8], cat_cot[8:16]), (ends, pltpu.roll(ends, 4, 0)))
    for k, pair in enumerate(pairs):
        part_ref[2 * b, 8 * k : 8 * k + 8], part_ref[2 * b + 1, 8 * k : 8 * k + 8] = pack(*pair)


ROWS = 20


def unpack_ends(buf, count):
    left = iota((count, LANES), 1) < LANES // 2
    front, back = [], []
    for k in range(4):
        line = jnp.concatenate([buf[d, 16 + k : 17 + k, :] for d in range(count)], axis=0)
        other = turn(line)
        front.append(jnp.where(left, line, other))
        back.append(jnp.where(left, other, line))
    return front + back


def join(buf, count, inner, single):
    low, high, alone, first_id, last_id, factor, first_cat, last_cat = unpack_ends(buf, count)
    place = iota((count, LANES), 0)
    joined = (last_id == pltpu.roll(first_id, count - 1, 0)) & (place < count - 1)
    taken = (first_id == pltpu.roll(last_id, 1, 0)) & (place > 0)
    first = jnp.where(taken, NEG, alone)
    last = jnp.where(joined, lse2(high, pltpu.roll(low, count - 1, 0)), high) * factor
    if single:
        last = jnp.where(first_id == last_id, NEG, last)
    here = iota((8, LANES), 0) + jnp.where(iota((8, LANES), 1) < LANES // 2, 0, 8)
    here = here.astype(F32)
    parts = [buf[d, 0:8, :] for d in range(count)]
    for d in range(count):
        if d > 0 or not inner:
            parts.append(jnp.where(first_cat[d : d + 1] == here, first[d : d + 1], NEG))
        if d < count - 1 or not inner:
            parts.append(jnp.where(last_cat[d : d + 1] == here, last[d : d + 1], NEG))
    top = functools.reduce(jnp.maximum, parts)
    logs = top + jnp.log(sum(jnp.exp(part - top) for part in parts))
    return logs, sum(buf[d, 8:16, :] for d in range(count))


def swap_kernel(
    ny, nz, nx, sums, peaks, cotm_ref, table_t, cols, rows_ref, rho_ref, ids_ref, inv_ref,
    cv_ref, top_ref, nbl_ref, nbr_ref, left_ref, right_ref, lst_ref, c_ref, cg_ref,
    part_ref, zbuf, line, ybuf, xsrc, xbuf, values, tops,
    nb_send, nb_recv, z_send, z_recv, y_send, y_recv, x_send, x_recv, g_send, g_recv, t_send, t_recv,
):
    sku = lax.axis_index("sku")
    cat = lax.axis_index("cat")
    y, z = sku // nz, sku % nz
    n = ny * nz
    to_right, to_left = (sku + 1) % n, (sku + n - 1) % n
    next_z = [(z + k) % nz for k in range(1, nz)]
    along_z = [y * nz + other for other in next_z]
    along_y = [(y + k) % ny * nz + z for k in range(1, ny)]
    along_x = [(cat + k) % nx for k in range(1, nx)]

    barrier = pltpu.get_barrier_semaphore()
    for other in along_z + along_y + [to_right, to_left]:
        pl.semaphore_signal(barrier, inc=1, device_id={"sku": other}, device_id_type=MESH)
    for other in along_x:
        pl.semaphore_signal(barrier, inc=1, device_id={"cat": other}, device_id_type=MESH)
    for b in range(left_ref.shape[0]):
        condense(b, sums, peaks, cotm_ref, table_t, cols, ids_ref, part_ref, left_ref, right_ref, lst_ref, c_ref)
    pl.semaphore_wait(barrier, nz + ny + nx - 1)

    def send(src, dst, send_sem, recv_sem, device):
        copy = pltpu.make_async_remote_copy(
            src_ref=src, dst_ref=dst, send_sem=send_sem, recv_sem=recv_sem, device_id=device, device_id_type=MESH
        )
        copy.start()
        return copy

    used = pl.ds(0, ROWS)
    by_z = [
        send(part_ref.at[next_z[k], used], zbuf.at[z, used], z_send.at[k], z_recv.at[k], {"sku": other})
        for k, other in enumerate(along_z)
    ]
    near = [
        send(right_ref, nbl_ref, nb_send.at[0], nb_recv.at[0], {"sku": to_right}),
        send(left_ref, nbr_ref, nb_send.at[1], nb_recv.at[1], {"sku": to_left}),
    ]
    zbuf[z] = part_ref[z]
    ah, al = halves(rows_ref[0:1, :])
    pick = iota((16, ah.shape[1]), 0)
    weights = jnp.where(pick == 0, ah.astype(F32), jnp.where(pick == 1, al.astype(F32), 0.0)).astype(BF16)
    for k in range(cg_ref.shape[1] // CHUNK):
        at = pl.ds(k * CHUNK, CHUNK)
        cg_ref[:, at] = jnp.sum(dot(weights, cotm_ref[:, at]), axis=0, keepdims=True) * inv_ref[0:1, at]
    for copy in by_z:
        copy.wait_recv()

    line[0:8, :], line[8:16, :] = join(zbuf, nz, True, True)
    begin, end = zbuf[0, 16:24, :], zbuf[nz - 1, 16:24, :]
    row, left = iota((8, LANES), 0), iota((8, LANES), 1) < LANES // 2
    from_begin = (row == 2) | (left & ((row == 0) | (row == 3)))
    one = end[3:4] == turn(end)[0:1]
    end = jnp.where(left & (row == 1) & one, NEG, end)
    line[16:24, :] = jnp.where(from_begin, begin, end)

    by_y = [
        send(line.at[used], ybuf.at[y, used], y_send.at[k], y_recv.at[k], {"sku": other})
        for k, other in enumerate(along_y)
    ]
    ybuf[y] = line[...]
    for copy in by_y:
        copy.wait_recv()
    logs, cot = join(ybuf, ny, False, False)
    value = rho_ref[0:8, :] * logs
    values[0:8, :] = value
    values[8:16, :] = cot
    top = jnp.max(value, axis=0, keepdims=True)
    top = jnp.maximum(top, turn(top))
    total = jnp.sum(jnp.exp(value - top), axis=0, keepdims=True)
    cot = jnp.sum(cot, axis=0, keepdims=True)
    xsrc[0:1, :] = top + jnp.log(total + turn(total))
    xsrc[1:2, :] = cot + turn(cot)
    xsrc[2:8, :] = jnp.zeros((6, LANES), F32)

    by_x = [send(xsrc, xbuf.at[k], x_send.at[k], x_recv.at[k], {"cat": other}) for k, other in enumerate(along_x)]
    gather = [
        send(values, cv_ref.at[z], g_send.at[k], g_recv.at[k], {"sku": other}) for k, other in enumerate(along_z)
    ]
    cv_ref[z] = values[...]
    for copy in by_x:
        copy.wait_recv()
    groups = [xsrc[0:1, :]] + [xbuf[k, 0:1, :] for k in range(nx - 1)]
    top = functools.reduce(jnp.maximum, groups + [jnp.zeros((1, LANES), F32)])
    tops[0:1, :] = top + jnp.log(jnp.exp(-top) + sum(jnp.exp(group - top) for group in groups))
    tops[1:2, :] = xsrc[1:2, :] + sum(xbuf[k, 1:2, :] for k in range(nx - 1))
    tops[2:8, :] = jnp.zeros((6, LANES), F32)
    last = [send(tops, top_ref.at[z], t_send.at[k], t_recv.at[k], {"sku": other}) for k, other in enumerate(along_z)]
    top_ref[z] = tops[...]
    for copy in near + gather + last:
        copy.wait_recv()
    for copy in by_z + near + by_y + by_x + gather + last:
        copy.wait_send()


def slope_kernel(
    wh_ref, wl_ref, lst_ref, r_ref, c_ref, cv_ref, top_ref, nbl_ref, nbr_ref, left_ref, right_ref, cg_ref, ids_ref,
    rows_ref, cols, rho_ref, grad_ref, path_ref, hs,
):
    subs = lst_ref.shape[0]
    blocks = nbl_ref.shape[0]
    width = ids_ref.shape[1]
    lam, par, irho, ilam = cols[0], cols[2], cols[3], cols[4]
    cats = 16
    spot = iota((subs, LANES), 1)
    parents = jnp.where(((spot % cats).astype(F32) == par) & (spot < 3 * cats), 1.0, 0.0).astype(BF16)[:, : 3 * cats]
    row = iota((subs, LANES), 0).astype(F32)
    for b in range(blocks):
        at = pl.ds(b * LANES, LANES)
        from_left, from_right = nbl_ref[b], nbr_ref[b]
        first_id, last_id = left_ref[b, 2:3, :], right_ref[b, 2:3, :]
        values, cots = [
            jnp.concatenate(pack(cv_ref[2 * b, 8 * k : 8 * k + 8, :], cv_ref[2 * b + 1, 8 * k : 8 * k + 8, :]), axis=0)
            for k in range(2)
        ]
        top = jnp.where(iota((8, LANES), 1) < LANES // 2, top_ref[2 * b], top_ref[2 * b + 1])
        inclusive = top[0:1]
        slopes = (1.0 - 1.0 / rho_ref[8:24, :]) * cots - top[1:2] * jnp.exp(values - inclusive)
        left_hit = (row == first_id) & (from_left[2:3] == first_id)
        right_hit = (row == last_id) & (from_right[2:3] == last_id)
        extra = jnp.where(left_hit, from_left[0:1], jnp.where(right_hit, from_right[0:1], NEG))
        level = lse2(lst_ref[:, at], extra)
        sub_cot = c_ref[:, at] + jnp.where(left_hit, from_left[1:2], jnp.where(right_hit, from_right[1:2], 0.0))
        cat_value = dot(parents, jnp.concatenate(thirds(values), axis=0))
        d_cat = dot(parents, jnp.concatenate(thirds(slopes), axis=0))
        log_sub = (lam * level - cat_value) * irho
        path = rows_ref[1:2, at] - level + log_sub + (cat_value - inclusive)
        d_sub = (irho - ilam) * sub_cot + jnp.exp(log_sub) * d_cat
        slope = rows_ref[0:1, at] * jnp.exp(r_ref[:, at] - level) * d_sub
        hs[0:subs, at], hs[subs:, at] = halves(slope)
        ph, plo = halves(jnp.transpose(path))
        path_ref[at, 0:subs] = ph
        path_ref[at, subs:] = plo
    for k in range(width // CHUNK):
        at = pl.ds(k * CHUNK, CHUNK)
        both = dot(hs[...], wh_ref[:, at])
        found = both[0:subs] + both[subs:] + dot(hs[0:subs, :], wl_ref[:, at])
        hit = iota((subs, CHUNK), 0) == ids_ref[:, at]
        grad_ref[:, at] = -(jnp.sum(jnp.where(hit, found, 0.0), axis=0, keepdims=True) + cg_ref[:, at])


def demand_kernel(ms_ref, path_ref, table, out_hbm, value_ref, sem):
    markets, width = ms_ref.shape

    def flush(b):
        rows = pl.ds(b * LANES, LANES)
        return pltpu.make_async_copy(value_ref.at[rows], out_hbm.at[rows, 0, :], sem.at[b])

    for b in range(markets // LANES):
        rows = pl.ds(b * LANES, LANES)
        for k in range(width // CHUNK):
            at = pl.ds(k * CHUNK, CHUNK)
            masked = ms_ref[rows, at]
            hits = table[:, at]
            path = dot(path_ref[rows, :], jnp.concatenate([hits, hits], axis=0))
            value_ref[rows, at] = jnp.where(masked > EMPTY, masked + path, 0.0)
        flush(b).start()
    for b in range(markets // LANES):
        flush(b).wait()


def whole():
    return pl.BlockSpec(memory_space=pltpu.VMEM)


def shards(
    n_sku, n_cat, features, taste, price, alpha, market_size, store_brand, sub_scale, cat_scale, availability,
    sku_subcat, subcat_cat, cotangent,
):
    markets, depth = features.shape
    width = price.shape[1]
    subs, cats = sub_scale.shape[1], cat_scale.shape[1]
    blocks = markets // LANES
    operands = (
        features,
        taste.reshape(depth, width),
        price,
        alpha.reshape(1, markets),
        market_size.reshape(1, markets),
        sub_scale,
        store_brand,
        cat_scale,
        subcat_cat,
        availability,
        sku_subcat,
        cotangent.reshape(markets, width),
    )
    operands = [pltpu.with_memory_space_constraint(x, pltpu.HBM) for x in operands]
    sds = jax.ShapeDtypeStruct
    vmem, dma = pltpu.VMEM, pltpu.SemaphoreType.DMA
    ms, wh, wl, cotm, sums, peaks, table, table_t, cols, rows, rho_rows, ids, inv = pl.pallas_call(
        local_kernel,
        in_specs=[pl.BlockSpec(memory_space=pl.ANY)] * 12,
        out_specs=[whole()] * 13,
        out_shape=[
            sds((markets, width), F32),
            sds((markets, width), BF16),
            sds((markets, width), BF16),
            sds((markets, width), BF16),
            sds((subs, markets), F32),
            sds((subs, markets), F32),
            sds((subs, width), BF16),
            sds((width, subs), BF16),
            sds((5, subs, LANES), F32),
            sds((8, markets), F32),
            sds((24, LANES), F32),
            sds((1, width), jnp.int32),
            sds((8, width), F32),
        ],
        scratch_shapes=[
            vmem((markets, depth), BF16),
            vmem((depth, width), BF16),
            vmem((1, width), F32),
            vmem((1, subs), F32),
            vmem((1, subs), F32),
            vmem((1, cats), F32),
            vmem((1, subs), jnp.int32),
            vmem((markets, width), jnp.int32),
            vmem((1, markets), F32),
            vmem((8, CHUNK), F32),
            dma((8,)),
            dma((2,)),
            dma((blocks,)),
            dma((blocks,)),
        ],
        compiler_params=pltpu.CompilerParams(vmem_limit_bytes=32 * 1024 * 1024),
        name="local_nests",
    )(*operands)

    nz = 2 * blocks
    ny = n_sku // nz
    cv, top, nbl, nbr, left, right, lst, c, cg = pl.pallas_call(
        functools.partial(swap_kernel, ny, nz, n_cat),
        in_specs=[whole()] * 9,
        out_specs=[whole()] * 9,
        out_shape=[sds((nz, 16, LANES), F32), sds((nz, 8, LANES), F32)]
        + [sds((blocks, 8, LANES), F32)] * 4
        + [sds((subs, markets), F32)] * 2
        + [sds((1, width), F32)],
        scratch_shapes=[
            vmem((nz, 24, LANES), F32),
            vmem((nz, 24, LANES), F32),
            vmem((24, LANES), F32),
            vmem((ny, 24, LANES), F32),
            vmem((8, LANES), F32),
            vmem((n_cat - 1, 8, LANES), F32),
            vmem((16, LANES), F32),
            vmem((8, LANES), F32),
        ]
        + [dma((count,)) for count in (2, nz - 1, ny - 1, n_cat - 1, nz - 1, nz - 1) for _ in range(2)],
        compiler_params=pltpu.CompilerParams(
            collective_id=0, has_side_effects=True, vmem_limit_bytes=16 * 1024 * 1024
        ),
        name="swap_nests",
    )(sums, peaks, cotm, table_t, cols, rows, rho_rows, ids, inv)

    grad, path = pl.pallas_call(
        slope_kernel,
        in_specs=[whole()] * 16,
        out_specs=[whole()] * 2,
        out_shape=[sds((1, width), F32), sds((markets, 2 * subs), BF16)],
        scratch_shapes=[vmem((2 * subs, markets), BF16)],
        compiler_params=pltpu.CompilerParams(vmem_limit_bytes=16 * 1024 * 1024),
        name="price_slope",
    )(wh, wl, lst, peaks, c, cv, top, nbl, nbr, left, right, cg, ids, rows, cols, rho_rows)
    other = lax.ppermute(grad, "mkt", [(0, 1), (1, 0)])

    demand = pl.pallas_call(
        demand_kernel,
        in_specs=[whole()] * 3,
        out_specs=pl.BlockSpec(memory_space=pl.ANY),
        out_shape=sds((markets, 1, width), F32),
        scratch_shapes=[vmem((markets, width), F32), dma((blocks,))],
        compiler_params=pltpu.CompilerParams(vmem_limit_bytes=16 * 1024 * 1024),
        cost_estimate=pl.CostEstimate(
            flops=2 * markets * width * 2 * subs, bytes_accessed=8 * markets * width, transcendentals=0
        ),
        name="log_demand",
    )(ms, path, table)
    return demand, grad + other


def solution(mesh):
    return jax.shard_map(
        functools.partial(shards, mesh.shape["sku"], mesh.shape["cat"]),
        mesh=mesh,
        in_specs=(
            P("mkt", None),
            P(None, "cat", "sku"),
            P("cat", "sku"),
            P("mkt"),
            P("mkt"),
            P("cat", None),
            P("cat", None),
            P("cat", None),
            P("mkt", "cat", "sku"),
            P("cat", "sku"),
            P("cat", None),
            P("mkt", "cat", "sku"),
        ),
        out_specs=(P("mkt", "cat", "sku"), P("cat", "sku")),
        check_vma=False,
    )
```

```python
import functools

import jax
import jax.numpy as jnp
from jax import lax
from jax.experimental import pallas as pl
from jax.experimental.pallas import tpu as pltpu
from jax.sharding import PartitionSpec as P

F32 = jnp.float32
BF16 = jnp.bfloat16
NEG = -1e30
EMPTY = -1e29
SAFE = 60.0
LANES = 128
CHUNK = 256
MESH = pl.DeviceIdType.MESH
NT = (((1,), (1,)), ((), ()))


def dot(a, b):
    return jnp.dot(a, b, preferred_element_type=F32)


def dot_nt(a, b):
    return lax.dot_general(a, b, NT, preferred_element_type=F32)


def iota(shape, dim):
    return lax.broadcasted_iota(jnp.int32, shape, dim)


def lse2(a, b):
    top = jnp.maximum(a, b)
    return top + jnp.log(1.0 + jnp.exp(jnp.minimum(a, b) - top))


def halves(x):
    high = x.astype(BF16)
    return high, (x - high.astype(F32)).astype(BF16)


def thirds(x):
    high = x.astype(BF16)
    rest = x - high.astype(F32)
    mid = rest.astype(BF16)
    return high, mid, (rest - mid.astype(F32)).astype(BF16)


def column(row):
    n = row.shape[1]
    return jnp.sum(jnp.where(iota((n, n), 0) == iota((n, n), 1), row, 0.0), axis=1, keepdims=True)


def nest_columns(lam_ref, store_ref, rho_ref, par_ref):
    lam = column(lam_ref[...])
    store = column(store_ref[...]) / lam
    par = column(par_ref[...].astype(F32))
    subs, cats = lam_ref.shape[1], rho_ref.shape[1]
    mine = par == iota((subs, cats), 1).astype(F32)
    rho = jnp.sum(jnp.where(mine, rho_ref[...], 0.0), axis=1, keepdims=True)
    return lam, 1.0 / lam, store, par, 1.0 / rho


def pack(low, high):
    left = iota(low.shape, 1) < LANES // 2
    return jnp.where(left, low, turn(high)), jnp.where(left, turn(low), high)


def turn(x):
    return pltpu.roll(x, LANES // 2, 1)


AHEAD = 3
ROW_BLOCK = 256


def local_kernel(
    feat_hbm, taste_hbm, price_hbm, alpha_hbm, size_hbm, lam_hbm, store_hbm, rho_hbm, par_hbm, avail_hbm, mem_hbm,
    cot_hbm,
    ms_ref, wh_ref, wl_ref, cotm_ref, sums, peaks, table, table_t, cols, rows_ref, rho_rows, ids_ref, inv_ref,
    feat, taste, price, lam_row, store_row, rho_row, par_row, avail, size, worst, alpha, totals,
    small_sem, feat_sem, taste_sem, avail_sem, cot_sem,
):
    subs = lam_row.shape[1]
    cats = rho_row.shape[1]
    markets, width = ms_ref.shape
    blocks = markets // LANES
    tiles = width // LANES
    chunks = width // CHUNK
    small = [
        (mem_hbm, ids_ref), (lam_hbm, lam_row), (price_hbm, price), (alpha_hbm, rows_ref.at[0:1]),
        (store_hbm, store_row), (rho_hbm, rho_row), (par_hbm, par_row), (size_hbm, size),
    ]
    small = [pltpu.make_async_copy(src, dst, small_sem.at[k]) for k, (src, dst) in enumerate(small)]
    whole_feat = pltpu.make_async_copy(feat_hbm, feat, feat_sem)

    def fetch(k):
        at = pl.ds(pl.multiple_of(k * CHUNK, CHUNK), CHUNK)
        return (
            pltpu.make_async_copy(taste_hbm.at[:, at], taste.at[:, at], taste_sem.at[k]),
            pltpu.make_async_copy(avail_hbm.at[:, 0, at], avail.at[:, at], avail_sem.at[k]),
            pltpu.make_async_copy(cot_hbm.at[:, at], cotm_ref.at[:, at], cot_sem.at[k]),
        )

    for copy in small:
        copy.start()
    whole_feat.start()
    for k in range(AHEAD):
        for copy in fetch(k):
            copy.start()
    for copy in small:
        copy.wait()

    lam = column(lam_row[...])
    for b in range(blocks):
        mine = pl.ds(b * LANES, LANES)
        alpha[mine, :] = jnp.transpose(jnp.broadcast_to(rows_ref[0:1, mine], (LANES, LANES)))
    _, ilam, store, par, irho = nest_columns(lam_row, store_row, rho_row, par_row)
    for k, col in enumerate((lam, store, par, irho, ilam)):
        cols[k] = jnp.broadcast_to(col, (subs, LANES))
    rho = jnp.broadcast_to(column(rho_row[...]), (cats, LANES))
    rho_rows[0:8, :] = jnp.where(iota((8, LANES), 1) < LANES // 2, rho[0:8], rho[8:16])
    rho_rows[8:24, :] = rho
    rows_ref[1:2, :] = jnp.log(size[...])
    worst[...] = jnp.zeros_like(worst)
    peaks[...] = jnp.zeros_like(peaks)
    totals[...] = jnp.zeros_like(totals)
    whole_feat.wait()

    @pl.loop(0, chunks)
    def _(k):
        at = pl.ds(pl.multiple_of(k * CHUNK, CHUNK), CHUNK)

        @pl.when(k + AHEAD < chunks)
        def _():
            for copy in fetch(k + AHEAD):
                copy.start()

        scale = jnp.concatenate([cols[0], cols[0]], axis=1)
        hit = iota((subs, CHUNK), 0) == ids_ref[:, at]
        ones = jnp.where(hit, 1.0, 0.0)
        table[:, at] = ones.astype(BF16)
        turned = jnp.transpose(ones).astype(BF16)
        table_t[at, :] = turned
        inv = 1.0 / jnp.sum(jnp.where(hit, scale, 0.0), axis=0, keepdims=True)
        cost = inv * price[:, at]
        inv_ref[0:1, at] = inv
        for copy in fetch(k):
            copy.wait()
        most = worst[...]
        for h in range(markets // ROW_BLOCK):
            rows = pl.ds(h * ROW_BLOCK, ROW_BLOCK)
            util = dot(feat[rows, :], taste[:, at])
            weight = alpha[rows, :]
            scaled = util * inv - jnp.concatenate([weight, weight], axis=1) * cost
            open_ = avail[rows, at]
            masked = jnp.where(open_ == 1, scaled, NEG)
            ms_ref[rows, at] = masked
            most = jnp.maximum(most, jnp.max(jnp.abs(scaled).reshape(ROW_BLOCK // 8, 8, CHUNK), axis=0))
            wh, wl = halves(jnp.exp(masked))
            wh_ref[rows, at] = wh
            wl_ref[rows, at] = wl
            cotm_ref[rows, at] = cotm_ref[rows, at] * open_.astype(F32).astype(BF16)
            both = dot(jnp.concatenate([wh, wl], axis=0), turned)
            totals[rows, :] += both[:ROW_BLOCK] + both[ROW_BLOCK:]
        worst[...] = most

    for b in range(blocks):
        mine = pl.ds(b * LANES, LANES)
        sums[:, mine] = jnp.transpose(totals[mine, :])

    @pl.when(jnp.max(worst[...]) > SAFE)
    def _():
        lane = iota((1, LANES), 1)

        @pl.loop(0, blocks)
        def _(b):
            mine = pl.ds(pl.multiple_of(b * LANES, LANES), LANES)
            carry = jnp.full((LANES, 1), NEG, F32)
            carry_id = jnp.full((1, 1), -1, jnp.int32)
            peak = jnp.zeros((LANES, subs), F32)
            for t in range(tiles):
                at = pl.ds(t * LANES, LANES)
                ids = ids_ref[:, at]
                run = ms_ref[mine, at]
                shift = 1
                while shift < LANES:
                    same = (pltpu.roll(ids, shift, 1) == ids) & (lane >= shift)
                    run = jnp.where(same, jnp.maximum(run, pltpu.roll(run, shift, 1)), run)
                    shift *= 2
                run = jnp.where(ids == carry_id, jnp.maximum(run, carry), run)
                carry = run[:, LANES - 1 :]
                carry_id = ids[:, LANES - 1 :]
                if t + 1 < tiles:
                    following = ids_ref[:, pl.ds((t + 1) * LANES, LANES)][:, 0:1]
                else:
                    following = jnp.full((1, 1), -1, jnp.int32)
                nxt = jnp.where(lane == LANES - 1, following, pltpu.roll(ids, LANES - 1, 1))
                ends = jnp.where((iota((subs, LANES), 0) == ids) & (ids != nxt), 1.0, 0.0).astype(BF16)
                peak = peak + dot_nt(run.astype(BF16), ends)
            peak = jnp.where(peak < EMPTY, 0.0, peak)
            peaks[:, mine] = jnp.transpose(peak)
            peak_half = peak.astype(BF16)
            total = jnp.zeros((2 * LANES, subs), F32)
            for t in range(tiles):
                at = pl.ds(t * LANES, LANES)
                wh, wl = halves(jnp.exp(ms_ref[mine, at] - dot(peak_half, table[:, at])))
                wh_ref[mine, at] = wh
                wl_ref[mine, at] = wl
                total = total + dot(jnp.concatenate([wh, wl], axis=0), table_t[at, :])
            sums[:, mine] = jnp.transpose(total[:LANES] + total[LANES:])


def condense(b, sums, peaks, cotm_ref, table_t, cols, ids_ref, part_ref, left_ref, right_ref, lst_ref, c_ref):
    cats = 16
    subs = sums.shape[0]
    width = ids_ref.shape[1]
    mine = pl.ds(b * LANES, LANES)
    total = sums[:, mine]
    raw = jnp.where(total > 0.0, peaks[:, mine] + jnp.log(jnp.where(total > 0.0, total, 1.0)), NEG)
    lam, store, par, irho = cols[0], cols[1], cols[2], cols[3]
    cot_total = jnp.transpose(dot(cotm_ref[mine, :], table_t[...]))
    full = lse2(raw, store)
    lst_ref[:, mine] = full
    c_ref[:, mine] = cot_total
    row = iota((subs, LANES), 0)
    first, last = ids_ref[:, 0:1], ids_ref[:, width - 1 :]
    is_first, is_last = row == first, row == last
    factor = lam * irho
    ratio_all = full * factor
    ratio = jnp.where((row > first) & (row < last), ratio_all, NEG)
    spread = jnp.full((subs, LANES), NEG, F32)
    tops = []
    for c in range(cats):
        hit = par == c
        top = jnp.max(jnp.where(hit, ratio, NEG), axis=0, keepdims=True)
        tops.append(top)
        spread = jnp.where(hit, top, spread)
    tops = jnp.concatenate(tops, axis=0)
    terms = jnp.where(ratio > EMPTY, jnp.exp(ratio - spread), 0.0)
    children = jnp.where(iota((subs, LANES), 1).astype(F32) == par, 1.0, 0.0)
    children = jnp.transpose(children)[0:cats].astype(BF16)
    found = dot(children, jnp.concatenate(halves(terms) + thirds(cot_total), axis=1))
    amount = found[:, 0:LANES] + found[:, LANES : 2 * LANES]
    cat_cot = found[:, 2 * LANES : 3 * LANES] + found[:, 3 * LANES : 4 * LANES] + found[:, 4 * LANES :]
    logs = jnp.where(amount > 0.0, tops + jnp.log(jnp.where(amount > 0.0, amount, 1.0)), NEG)

    def at_row(mask, values):
        return jnp.sum(jnp.where(mask, values, 0.0), axis=0, keepdims=True)

    first_id = jnp.broadcast_to(first.astype(F32), (1, LANES))
    last_id = jnp.broadcast_to(last.astype(F32), (1, LANES))
    blank = jnp.zeros((5, LANES), F32)
    low = at_row(is_first, raw)
    left_ref[b] = jnp.concatenate([low, at_row(is_first, cot_total), first_id, blank], axis=0)
    right_ref[b] = jnp.concatenate([at_row(is_last, raw), at_row(is_last, cot_total), last_id, blank], axis=0)
    ends = jnp.concatenate(
        [
            low, at_row(is_last, full), at_row(is_first, ratio_all), first_id, last_id,
            at_row(is_last, factor), at_row(is_first, par), at_row(is_last, par),
        ],
        axis=0,
    )
    pairs = ((logs[0:8], logs[8:16]), (cat_cot[0:8], cat_cot[8:16]), (ends, pltpu.roll(ends, 4, 0)))
    for k, pair in enumerate(pairs):
        part_ref[2 * b, 8 * k : 8 * k + 8], part_ref[2 * b + 1, 8 * k : 8 * k + 8] = pack(*pair)


ROWS = 20


def unpack_ends(buf, count):
    left = iota((count, LANES), 1) < LANES // 2
    front, back = [], []
    for k in range(4):
        line = jnp.concatenate([buf[d, 16 + k : 17 + k, :] for d in range(count)], axis=0)
        other = turn(line)
        front.append(jnp.where(left, line, other))
        back.append(jnp.where(left, other, line))
    return front + back


def join(buf, count, inner, single):
    low, high, alone, first_id, last_id, factor, first_cat, last_cat = unpack_ends(buf, count)
    place = iota((count, LANES), 0)
    joined = (last_id == pltpu.roll(first_id, count - 1, 0)) & (place < count - 1)
    taken = (first_id == pltpu.roll(last_id, 1, 0)) & (place > 0)
    first = jnp.where(taken, NEG, alone)
    last = jnp.where(joined, lse2(high, pltpu.roll(low, count - 1, 0)), high) * factor
    if single:
        last = jnp.where(first_id == last_id, NEG, last)
    here = iota((8, LANES), 0) + jnp.where(iota((8, LANES), 1) < LANES // 2, 0, 8)
    here = here.astype(F32)
    parts = [buf[d, 0:8, :] for d in range(count)]
    for d in range(count):
        if d > 0 or not inner:
            parts.append(jnp.where(first_cat[d : d + 1] == here, first[d : d + 1], NEG))
        if d < count - 1 or not inner:
            parts.append(jnp.where(last_cat[d : d + 1] == here, last[d : d + 1], NEG))
    top = functools.reduce(jnp.maximum, parts)
    logs = top + jnp.log(sum(jnp.exp(part - top) for part in parts))
    return logs, sum(buf[d, 8:16, :] for d in range(count))


def swap_kernel(
    ny, nz, nx, sums, peaks, cotm_ref, table_t, cols, rows_ref, rho_ref, ids_ref, inv_ref,
    cv_ref, top_ref, nbl_ref, nbr_ref, left_ref, right_ref, lst_ref, c_ref, cg_ref,
    part_ref, zbuf, line, ybuf, xsrc, xbuf, values, tops,
    nb_send, nb_recv, z_send, z_recv, y_send, y_recv, x_send, x_recv, g_send, g_recv, t_send, t_recv,
):
    sku = lax.axis_index("sku")
    cat = lax.axis_index("cat")
    y, z = sku // nz, sku % nz
    n = ny * nz
    to_right, to_left = (sku + 1) % n, (sku + n - 1) % n
    next_z = [(z + k) % nz for k in range(1, nz)]
    along_z = [y * nz + other for other in next_z]
    along_y = [(y + k) % ny * nz + z for k in range(1, ny)]
    along_x = [(cat + k) % nx for k in range(1, nx)]

    barrier = pltpu.get_barrier_semaphore()
    for other in along_z + along_y + [to_right, to_left]:
        pl.semaphore_signal(barrier, inc=1, device_id={"sku": other}, device_id_type=MESH)
    for other in along_x:
        pl.semaphore_signal(barrier, inc=1, device_id={"cat": other}, device_id_type=MESH)
    for b in range(left_ref.shape[0]):
        condense(b, sums, peaks, cotm_ref, table_t, cols, ids_ref, part_ref, left_ref, right_ref, lst_ref, c_ref)
    pl.semaphore_wait(barrier, nz + ny + nx - 1)

    def send(src, dst, send_sem, recv_sem, device):
        copy = pltpu.make_async_remote_copy(
            src_ref=src, dst_ref=dst, send_sem=send_sem, recv_sem=recv_sem, device_id=device, device_id_type=MESH
        )
        copy.start()
        return copy

    used = pl.ds(0, ROWS)
    by_z = [
        send(part_ref.at[next_z[k], used], zbuf.at[z, used], z_send.at[k], z_recv.at[k], {"sku": other})
        for k, other in enumerate(along_z)
    ]
    near = [
        send(right_ref, nbl_ref, nb_send.at[0], nb_recv.at[0], {"sku": to_right}),
        send(left_ref, nbr_ref, nb_send.at[1], nb_recv.at[1], {"sku": to_left}),
    ]
    zbuf[z] = part_ref[z]
    ah, al = halves(rows_ref[0:1, :])
    pick = iota((16, ah.shape[1]), 0)
    weights = jnp.where(pick == 0, ah.astype(F32), jnp.where(pick == 1, al.astype(F32), 0.0)).astype(BF16)
    for k in range(cg_ref.shape[1] // CHUNK):
        at = pl.ds(k * CHUNK, CHUNK)
        cg_ref[:, at] = jnp.sum(dot(weights, cotm_ref[:, at]), axis=0, keepdims=True) * inv_ref[0:1, at]
    for copy in by_z:
        copy.wait_recv()

    line[0:8, :], line[8:16, :] = join(zbuf, nz, True, True)
    begin, end = zbuf[0, 16:24, :], zbuf[nz - 1, 16:24, :]
    row, left = iota((8, LANES), 0), iota((8, LANES), 1) < LANES // 2
    from_begin = (row == 2) | (left & ((row == 0) | (row == 3)))
    one = end[3:4] == turn(end)[0:1]
    end = jnp.where(left & (row == 1) & one, NEG, end)
    line[16:24, :] = jnp.where(from_begin, begin, end)

    by_y = [
        send(line.at[used], ybuf.at[y, used], y_send.at[k], y_recv.at[k], {"sku": other})
        for k, other in enumerate(along_y)
    ]
    ybuf[y] = line[...]
    for copy in by_y:
        copy.wait_recv()
    logs, cot = join(ybuf, ny, False, False)
    value = rho_ref[0:8, :] * logs
    values[0:8, :] = value
    values[8:16, :] = cot
    top = jnp.max(value, axis=0, keepdims=True)
    top = jnp.maximum(top, turn(top))
    total = jnp.sum(jnp.exp(value - top), axis=0, keepdims=True)
    cot = jnp.sum(cot, axis=0, keepdims=True)
    xsrc[0:1, :] = top + jnp.log(total + turn(total))
    xsrc[1:2, :] = cot + turn(cot)
    xsrc[2:8, :] = jnp.zeros((6, LANES), F32)

    by_x = [send(xsrc, xbuf.at[k], x_send.at[k], x_recv.at[k], {"cat": other}) for k, other in enumerate(along_x)]
    gather = [
        send(values, cv_ref.at[z], g_send.at[k], g_recv.at[k], {"sku": other}) for k, other in enumerate(along_z)
    ]
    cv_ref[z] = values[...]
    for copy in by_x:
        copy.wait_recv()
    groups = [xsrc[0:1, :]] + [xbuf[k, 0:1, :] for k in range(nx - 1)]
    top = functools.reduce(jnp.maximum, groups + [jnp.zeros((1, LANES), F32)])
    tops[0:1, :] = top + jnp.log(jnp.exp(-top) + sum(jnp.exp(group - top) for group in groups))
    tops[1:2, :] = xsrc[1:2, :] + sum(xbuf[k, 1:2, :] for k in range(nx - 1))
    tops[2:8, :] = jnp.zeros((6, LANES), F32)
    last = [send(tops, top_ref.at[z], t_send.at[k], t_recv.at[k], {"sku": other}) for k, other in enumerate(along_z)]
    top_ref[z] = tops[...]
    for copy in near + gather + last:
        copy.wait_recv()
    for copy in by_z + near + by_y + by_x + gather + last:
        copy.wait_send()


def slope_kernel(
    wh_ref, wl_ref, lst_ref, r_ref, c_ref, cv_ref, top_ref, nbl_ref, nbr_ref, left_ref, right_ref, cg_ref, ids_ref,
    rows_ref, cols, rho_ref, grad_ref, path_ref, hs,
):
    subs = lst_ref.shape[0]
    blocks = nbl_ref.shape[0]
    width = ids_ref.shape[1]
    lam, par, irho, ilam = cols[0], cols[2], cols[3], cols[4]
    cats = 16
    spot = iota((subs, LANES), 1)
    parents = jnp.where(((spot % cats).astype(F32) == par) & (spot < 3 * cats), 1.0, 0.0).astype(BF16)[:, : 3 * cats]
    row = iota((subs, LANES), 0).astype(F32)
    for b in range(blocks):
        at = pl.ds(b * LANES, LANES)
        from_left, from_right = nbl_ref[b], nbr_ref[b]
        first_id, last_id = left_ref[b, 2:3, :], right_ref[b, 2:3, :]
        values, cots = [
            jnp.concatenate(pack(cv_ref[2 * b, 8 * k : 8 * k + 8, :], cv_ref[2 * b + 1, 8 * k : 8 * k + 8, :]), axis=0)
            for k in range(2)
        ]
        top = jnp.where(iota((8, LANES), 1) < LANES // 2, top_ref[2 * b], top_ref[2 * b + 1])
        inclusive = top[0:1]
        slopes = (1.0 - 1.0 / rho_ref[8:24, :]) * cots - top[1:2] * jnp.exp(values - inclusive)
        left_hit = (row == first_id) & (from_left[2:3] == first_id)
        right_hit = (row == last_id) & (from_right[2:3] == last_id)
        extra = jnp.where(left_hit, from_left[0:1], jnp.where(right_hit, from_right[0:1], NEG))
        level = lse2(lst_ref[:, at], extra)
        sub_cot = c_ref[:, at] + jnp.where(left_hit, from_left[1:2], jnp.where(right_hit, from_right[1:2], 0.0))
        cat_value = dot(parents, jnp.concatenate(thirds(values), axis=0))
        d_cat = dot(parents, jnp.concatenate(thirds(slopes), axis=0))
        log_sub = (lam * level - cat_value) * irho
        path = rows_ref[1:2, at] - level + log_sub + (cat_value - inclusive)
        d_sub = (irho - ilam) * sub_cot + jnp.exp(log_sub) * d_cat
        slope = rows_ref[0:1, at] * jnp.exp(r_ref[:, at] - level) * d_sub
        hs[0:subs, at], hs[subs:, at] = halves(slope)
        ph, plo = halves(jnp.transpose(path))
        path_ref[at, 0:subs] = ph
        path_ref[at, subs:] = plo
    for k in range(width // CHUNK):
        at = pl.ds(k * CHUNK, CHUNK)
        both = dot(hs[...], wh_ref[:, at])
        found = both[0:subs] + both[subs:] + dot(hs[0:subs, :], wl_ref[:, at])
        hit = iota((subs, CHUNK), 0) == ids_ref[:, at]
        grad_ref[:, at] = -(jnp.sum(jnp.where(hit, found, 0.0), axis=0, keepdims=True) + cg_ref[:, at])


def demand_kernel(ms_ref, path_ref, table, out_hbm, value_ref, sem):
    markets, width = ms_ref.shape

    def flush(k):
        at = pl.ds(k * CHUNK, CHUNK)
        return pltpu.make_async_copy(value_ref.at[:, at], out_hbm.at[:, 0, at], sem.at[k])

    for k in range(width // CHUNK):
        at = pl.ds(k * CHUNK, CHUNK)
        hits = table[:, at]
        hits = jnp.concatenate([hits, hits], axis=0)
        for h in range(markets // ROW_BLOCK):
            rows = pl.ds(h * ROW_BLOCK, ROW_BLOCK)
            masked = ms_ref[rows, at]
            value_ref[rows, at] = jnp.where(masked > EMPTY, masked + dot(path_ref[rows, :], hits), 0.0)
        flush(k).start()
    for k in range(width // CHUNK):
        flush(k).wait()


def whole():
    return pl.BlockSpec(memory_space=pltpu.VMEM)


def shards(
    n_sku, n_cat, features, taste, price, alpha, market_size, store_brand, sub_scale, cat_scale, availability,
    sku_subcat, subcat_cat, cotangent,
):
    markets, depth = features.shape
    width = price.shape[1]
    subs, cats = sub_scale.shape[1], cat_scale.shape[1]
    blocks = markets // LANES
    operands = (
        features,
        taste.reshape(depth, width),
        price,
        alpha.reshape(1, markets),
        market_size.reshape(1, markets),
        sub_scale,
        store_brand,
        cat_scale,
        subcat_cat,
        availability,
        sku_subcat,
        cotangent.reshape(markets, width),
    )
    operands = [pltpu.with_memory_space_constraint(x, pltpu.HBM) for x in operands]
    sds = jax.ShapeDtypeStruct
    vmem, dma = pltpu.VMEM, pltpu.SemaphoreType.DMA
    ms, wh, wl, cotm, sums, peaks, table, table_t, cols, rows, rho_rows, ids, inv = pl.pallas_call(
        local_kernel,
        in_specs=[pl.BlockSpec(memory_space=pl.ANY)] * 12,
        out_specs=[whole()] * 13,
        out_shape=[
            sds((markets, width), F32),
            sds((markets, width), BF16),
            sds((markets, width), BF16),
            sds((markets, width), BF16),
            sds((subs, markets), F32),
            sds((subs, markets), F32),
            sds((subs, width), BF16),
            sds((width, subs), BF16),
            sds((5, subs, LANES), F32),
            sds((8, markets), F32),
            sds((24, LANES), F32),
            sds((1, width), jnp.int32),
            sds((8, width), F32),
        ],
        scratch_shapes=[
            vmem((markets, depth), BF16),
            vmem((depth, width), BF16),
            vmem((1, width), F32),
            vmem((1, subs), F32),
            vmem((1, subs), F32),
            vmem((1, cats), F32),
            vmem((1, subs), jnp.int32),
            vmem((markets, width), jnp.int32),
            vmem((1, markets), F32),
            vmem((8, CHUNK), F32),
            vmem((markets, LANES), F32),
            vmem((markets, subs), F32),
            dma((8,)),
            dma,
            dma((width // CHUNK,)),
            dma((width // CHUNK,)),
            dma((width // CHUNK,)),
        ],
        compiler_params=pltpu.CompilerParams(vmem_limit_bytes=32 * 1024 * 1024),
        name="local_nests",
    )(*operands)

    nz = 2 * blocks
    ny = n_sku // nz
    cv, top, nbl, nbr, left, right, lst, c, cg = pl.pallas_call(
        functools.partial(swap_kernel, ny, nz, n_cat),
        in_specs=[whole()] * 9,
        out_specs=[whole()] * 9,
        out_shape=[sds((nz, 16, LANES), F32), sds((nz, 8, LANES), F32)]
        + [sds((blocks, 8, LANES), F32)] * 4
        + [sds((subs, markets), F32)] * 2
        + [sds((1, width), F32)],
        scratch_shapes=[
            vmem((nz, 24, LANES), F32),
            vmem((nz, 24, LANES), F32),
            vmem((24, LANES), F32),
            vmem((ny, 24, LANES), F32),
            vmem((8, LANES), F32),
            vmem((n_cat - 1, 8, LANES), F32),
            vmem((16, LANES), F32),
            vmem((8, LANES), F32),
        ]
        + [dma((count,)) for count in (2, nz - 1, ny - 1, n_cat - 1, nz - 1, nz - 1) for _ in range(2)],
        compiler_params=pltpu.CompilerParams(
            collective_id=0, has_side_effects=True, vmem_limit_bytes=16 * 1024 * 1024
        ),
        name="swap_nests",
    )(sums, peaks, cotm, table_t, cols, rows, rho_rows, ids, inv)

    grad, path = pl.pallas_call(
        slope_kernel,
        in_specs=[whole()] * 16,
        out_specs=[whole()] * 2,
        out_shape=[sds((1, width), F32), sds((markets, 2 * subs), BF16)],
        scratch_shapes=[vmem((2 * subs, markets), BF16)],
        compiler_params=pltpu.CompilerParams(vmem_limit_bytes=16 * 1024 * 1024),
        name="price_slope",
    )(wh, wl, lst, peaks, c, cv, top, nbl, nbr, left, right, cg, ids, rows, cols, rho_rows)
    other = lax.ppermute(grad, "mkt", [(0, 1), (1, 0)])

    demand = pl.pallas_call(
        demand_kernel,
        in_specs=[whole()] * 3,
        out_specs=pl.BlockSpec(memory_space=pl.ANY),
        out_shape=sds((markets, 1, width), F32),
        scratch_shapes=[vmem((markets, width), F32), dma((width // CHUNK,))],
        compiler_params=pltpu.CompilerParams(vmem_limit_bytes=16 * 1024 * 1024),
        cost_estimate=pl.CostEstimate(
            flops=2 * markets * width * 2 * subs, bytes_accessed=8 * markets * width, transcendentals=0
        ),
        name="log_demand",
    )(ms, path, table)
    return demand, grad + other


def solution(mesh):
    return jax.shard_map(
        functools.partial(shards, mesh.shape["sku"], mesh.shape["cat"]),
        mesh=mesh,
        in_specs=(
            P("mkt", None),
            P(None, "cat", "sku"),
            P("cat", "sku"),
            P("mkt"),
            P("mkt"),
            P("cat", None),
            P("cat", None),
            P("cat", None),
            P("mkt", "cat", "sku"),
            P("cat", "sku"),
            P("cat", None),
            P("mkt", "cat", "sku"),
        ),
        out_specs=(P("mkt", "cat", "sku"), P("cat", "sku")),
        check_vma=False,
    )
```

```python
import functools

import jax
import jax.numpy as jnp
from jax import lax
from jax.experimental import pallas as pl
from jax.experimental.pallas import tpu as pltpu
from jax.sharding import PartitionSpec as P

F32 = jnp.float32
BF16 = jnp.bfloat16
NEG = -1e30
EMPTY = -1e29
SAFE = 60.0
LANES = 128
CHUNK = 256
MESH = pl.DeviceIdType.MESH
NT = (((1,), (1,)), ((), ()))


def dot(a, b):
    return jnp.dot(a, b, preferred_element_type=F32)


def dot_nt(a, b):
    return lax.dot_general(a, b, NT, preferred_element_type=F32)


def iota(shape, dim):
    return lax.broadcasted_iota(jnp.int32, shape, dim)


def lse2(a, b):
    top = jnp.maximum(a, b)
    return top + jnp.log(1.0 + jnp.exp(jnp.minimum(a, b) - top))


def halves(x):
    high = x.astype(BF16)
    return high, (x - high.astype(F32)).astype(BF16)


def thirds(x):
    high = x.astype(BF16)
    rest = x - high.astype(F32)
    mid = rest.astype(BF16)
    return high, mid, (rest - mid.astype(F32)).astype(BF16)


def column(row):
    n = row.shape[1]
    return jnp.sum(jnp.where(iota((n, n), 0) == iota((n, n), 1), row, 0.0), axis=1, keepdims=True)


def nest_columns(lam_ref, store_ref, rho_ref, par_ref):
    lam = column(lam_ref[...])
    store = column(store_ref[...]) / lam
    par = column(par_ref[...].astype(F32))
    subs, cats = lam_ref.shape[1], rho_ref.shape[1]
    mine = par == iota((subs, cats), 1).astype(F32)
    rho = jnp.sum(jnp.where(mine, rho_ref[...], 0.0), axis=1, keepdims=True)
    return lam, 1.0 / lam, store, par, 1.0 / rho


def pack(low, high):
    left = iota(low.shape, 1) < LANES // 2
    return jnp.where(left, low, turn(high)), jnp.where(left, turn(low), high)


def turn(x):
    return pltpu.roll(x, LANES // 2, 1)


def local_kernel(
    feat_hbm, taste_hbm, price_hbm, alpha_hbm, size_hbm, lam_hbm, store_hbm, rho_hbm, par_hbm, avail_hbm, mem_hbm,
    cot_hbm,
    ms_ref, wh_ref, wl_ref, cot_ref, sums, peaks, table, table_t, cols, rows_ref, rho_rows, ids_ref, inv_ref,
    feat, taste, price, lam_row, store_row, rho_row, par_row, avail, size, worst,
    small_sem, feat_sem, taste_sem, avail_sem, cot_sem,
):
    subs = lam_row.shape[1]
    cats = rho_row.shape[1]
    width = ids_ref.shape[1]
    blocks = ms_ref.shape[0] // LANES
    tiles = width // LANES
    chunks = width // CHUNK
    small = [
        (mem_hbm, ids_ref), (lam_hbm, lam_row), (price_hbm, price), (alpha_hbm, rows_ref.at[0:1]),
        (store_hbm, store_row), (rho_hbm, rho_row), (par_hbm, par_row), (size_hbm, size),
    ]
    small = [pltpu.make_async_copy(src, dst, small_sem.at[k]) for k, (src, dst) in enumerate(small)]
    whole_feat = pltpu.make_async_copy(feat_hbm, feat, feat_sem)
    whole_cot = pltpu.make_async_copy(cot_hbm, cot_ref, cot_sem)
    tastes = []
    for k in range(chunks):
        at = pl.ds(k * CHUNK, CHUNK)
        tastes.append(pltpu.make_async_copy(taste_hbm.at[:, at], taste.at[:, at], taste_sem.at[k]))

    def fetch(b):
        rows = pl.ds(pl.multiple_of(b * LANES, LANES), LANES)
        return pltpu.make_async_copy(avail_hbm.at[rows, 0, :], avail.at[rows], avail_sem.at[b])

    for copy in small:
        copy.start()
    whole_feat.start()
    tastes[0].start()
    fetch(0).start()
    for copy in tastes[1:]:
        copy.start()
    for b in range(1, blocks):
        fetch(b).start()
    whole_cot.start()
    for copy in small:
        copy.wait()

    lam = column(lam_row[...])
    for k in range(chunks):
        at = pl.ds(k * CHUNK, CHUNK)
        hit = iota((subs, CHUNK), 0) == ids_ref[:, at]
        ones = jnp.where(hit, 1.0, 0.0)
        table[:, at] = ones.astype(BF16)
        table_t[at, :] = jnp.transpose(ones).astype(BF16)
        inv = 1.0 / jnp.sum(jnp.where(hit, lam, 0.0), axis=0, keepdims=True)
        inv_ref[0:1, at] = inv
        inv_ref[1:2, at] = inv * price[:, at]
    worst[...] = jnp.zeros_like(worst)

    def block(b, mine, arrive):
        fetch(b).wait()
        alpha = jnp.transpose(jnp.broadcast_to(rows_ref[0:1, mine], (LANES, LANES)))
        alpha2 = jnp.concatenate([alpha, alpha], axis=1)
        total = jnp.zeros((LANES, subs), F32)
        most = jnp.zeros((8, CHUNK), F32)
        for k in range(chunks):
            at = pl.ds(k * CHUNK, CHUNK)
            if arrive:
                tastes[k].wait()
            util = dot(feat[mine, :], taste[:, at])
            scaled = util * inv_ref[0:1, at] - alpha2 * inv_ref[1:2, at]
            masked = jnp.where(avail[mine, at] == 1, scaled, NEG)
            ms_ref[mine, at] = masked
            most = jnp.maximum(most, jnp.max(jnp.abs(scaled).reshape(LANES // 8, 8, CHUNK), axis=0))
            wh, wl = halves(jnp.exp(masked))
            wh_ref[mine, at] = wh
            wl_ref[mine, at] = wl
            hits = table_t[at, :]
            total = total + dot(jnp.concatenate([wh, wl], axis=1), jnp.concatenate([hits, hits], axis=0))
        sums[:, mine] = jnp.transpose(total)
        worst[...] = jnp.maximum(worst[...], most)

    whole_feat.wait()
    block(0, pl.ds(0, LANES), True)

    @pl.loop(1, blocks)
    def _(b):
        block(b, pl.ds(pl.multiple_of(b * LANES, LANES), LANES), False)

    peaks[...] = jnp.zeros_like(peaks)
    _, ilam, store, par, irho = nest_columns(lam_row, store_row, rho_row, par_row)
    for k, col in enumerate((lam, store, par, irho, ilam)):
        cols[k] = jnp.broadcast_to(col, (subs, LANES))
    rho = jnp.broadcast_to(column(rho_row[...]), (cats, LANES))
    rho_rows[0:8, :] = jnp.where(iota((8, LANES), 1) < LANES // 2, rho[0:8], rho[8:16])
    rho_rows[8:24, :] = rho
    rows_ref[1:2, :] = jnp.log(size[...])
    whole_cot.wait()

    @pl.when(jnp.max(worst[...]) > SAFE)
    def _():
        lane = iota((1, LANES), 1)

        @pl.loop(0, blocks)
        def _(b):
            mine = pl.ds(pl.multiple_of(b * LANES, LANES), LANES)
            carry = jnp.full((LANES, 1), NEG, F32)
            carry_id = jnp.full((1, 1), -1, jnp.int32)
            peak = jnp.zeros((LANES, subs), F32)
            for t in range(tiles):
                at = pl.ds(t * LANES, LANES)
                ids = ids_ref[:, at]
                run = ms_ref[mine, at]
                shift = 1
                while shift < LANES:
                    same = (pltpu.roll(ids, shift, 1) == ids) & (lane >= shift)
                    run = jnp.where(same, jnp.maximum(run, pltpu.roll(run, shift, 1)), run)
                    shift *= 2
                run = jnp.where(ids == carry_id, jnp.maximum(run, carry), run)
                carry = run[:, LANES - 1 :]
                carry_id = ids[:, LANES - 1 :]
                if t + 1 < tiles:
                    following = ids_ref[:, pl.ds((t + 1) * LANES, LANES)][:, 0:1]
                else:
                    following = jnp.full((1, 1), -1, jnp.int32)
                nxt = jnp.where(lane == LANES - 1, following, pltpu.roll(ids, LANES - 1, 1))
                ends = jnp.where((iota((subs, LANES), 0) == ids) & (ids != nxt), 1.0, 0.0).astype(BF16)
                peak = peak + dot_nt(run.astype(BF16), ends)
            peak = jnp.where(peak < EMPTY, 0.0, peak)
            peaks[:, mine] = jnp.transpose(peak)
            peak_half = peak.astype(BF16)
            total = jnp.zeros((2 * LANES, subs), F32)
            for t in range(tiles):
                at = pl.ds(t * LANES, LANES)
                wh, wl = halves(jnp.exp(ms_ref[mine, at] - dot(peak_half, table[:, at])))
                wh_ref[mine, at] = wh
                wl_ref[mine, at] = wl
                total = total + dot(jnp.concatenate([wh, wl], axis=0), table_t[at, :])
            sums[:, mine] = jnp.transpose(total[:LANES] + total[LANES:])


def condense(b, sums, peaks, ms_ref, cot_ref, cotm_ref, table_t, cols, ids_ref, part_ref, left_ref, right_ref, lst_ref, c_ref):
    cats = 16
    subs = sums.shape[0]
    width = ids_ref.shape[1]
    mine = pl.ds(b * LANES, LANES)
    for k in range(width // CHUNK):
        at = pl.ds(k * CHUNK, CHUNK)
        cotm_ref[mine, at] = cot_ref[mine, at] * jnp.where(ms_ref[mine, at] > EMPTY, 1.0, 0.0).astype(BF16)
    total = sums[:, mine]
    raw = jnp.where(total > 0.0, peaks[:, mine] + jnp.log(jnp.where(total > 0.0, total, 1.0)), NEG)
    lam, store, par, irho = cols[0], cols[1], cols[2], cols[3]
    cot_total = jnp.transpose(dot(cotm_ref[mine, :], table_t[...]))
    full = lse2(raw, store)
    lst_ref[:, mine] = full
    c_ref[:, mine] = cot_total
    row = iota((subs, LANES), 0)
    first, last = ids_ref[:, 0:1], ids_ref[:, width - 1 :]
    is_first, is_last = row == first, row == last
    factor = lam * irho
    ratio_all = full * factor
    ratio = jnp.where((row > first) & (row < last), ratio_all, NEG)
    spread = jnp.full((subs, LANES), NEG, F32)
    tops = []
    for c in range(cats):
        hit = par == c
        top = jnp.max(jnp.where(hit, ratio, NEG), axis=0, keepdims=True)
        tops.append(top)
        spread = jnp.where(hit, top, spread)
    tops = jnp.concatenate(tops, axis=0)
    terms = jnp.where(ratio > EMPTY, jnp.exp(ratio - spread), 0.0)
    children = jnp.where(iota((subs, LANES), 1).astype(F32) == par, 1.0, 0.0)
    children = jnp.transpose(children)[0:cats].astype(BF16)
    found = dot(children, jnp.concatenate(halves(terms) + thirds(cot_total), axis=1))
    amount = found[:, 0:LANES] + found[:, LANES : 2 * LANES]
    cat_cot = found[:, 2 * LANES : 3 * LANES] + found[:, 3 * LANES : 4 * LANES] + found[:, 4 * LANES :]
    logs = jnp.where(amount > 0.0, tops + jnp.log(jnp.where(amount > 0.0, amount, 1.0)), NEG)

    def at_row(mask, values):
        return jnp.sum(jnp.where(mask, values, 0.0), axis=0, keepdims=True)

    first_id = jnp.broadcast_to(first.astype(F32), (1, LANES))
    last_id = jnp.broadcast_to(last.astype(F32), (1, LANES))
    blank = jnp.zeros((5, LANES), F32)
    low = at_row(is_first, raw)
    left_ref[b] = jnp.concatenate([low, at_row(is_first, cot_total), first_id, blank], axis=0)
    right_ref[b] = jnp.concatenate([at_row(is_last, raw), at_row(is_last, cot_total), last_id, blank], axis=0)
    ends = jnp.concatenate(
        [
            low, at_row(is_last, full), at_row(is_first, ratio_all), first_id, last_id,
            at_row(is_last, factor), at_row(is_first, par), at_row(is_last, par),
        ],
        axis=0,
    )
    pairs = ((logs[0:8], logs[8:16]), (cat_cot[0:8], cat_cot[8:16]), (ends, pltpu.roll(ends, 4, 0)))
    for k, pair in enumerate(pairs):
        part_ref[2 * b, 8 * k : 8 * k + 8], part_ref[2 * b + 1, 8 * k : 8 * k + 8] = pack(*pair)


ROWS = 20


def unpack_ends(buf, count):
    left = iota((count, LANES), 1) < LANES // 2
    front, back = [], []
    for k in range(4):
        line = buf[pl.ds(16 + k, count, stride=24), :]
        other = turn(line)
        front.append(jnp.where(left, line, other))
        back.append(jnp.where(left, other, line))
    return front + back


def join(buf, count, inner, single):
    low, high, alone, first_id, last_id, factor, first_cat, last_cat = unpack_ends(buf, count)
    place = iota((count, LANES), 0)
    joined = (last_id == pltpu.roll(first_id, count - 1, 0)) & (place < count - 1)
    taken = (first_id == pltpu.roll(last_id, 1, 0)) & (place > 0)
    first = jnp.where(taken, NEG, alone)
    last = jnp.where(joined, lse2(high, pltpu.roll(low, count - 1, 0)), high) * factor
    if single:
        last = jnp.where(first_id == last_id, NEG, last)
    here = iota((8, LANES), 0) + jnp.where(iota((8, LANES), 1) < LANES // 2, 0, 8)
    here = here.astype(F32)
    parts = [buf[24 * d : 24 * d + 8, :] for d in range(count)]
    for d in range(count):
        if d > 0 or not inner:
            parts.append(jnp.where(first_cat[d : d + 1] == here, first[d : d + 1], NEG))
        if d < count - 1 or not inner:
            parts.append(jnp.where(last_cat[d : d + 1] == here, last[d : d + 1], NEG))
    top = functools.reduce(jnp.maximum, parts)
    logs = top + jnp.log(sum(jnp.exp(part - top) for part in parts))
    return logs, sum(buf[24 * d + 8 : 24 * d + 16, :] for d in range(count))


def swap_kernel(
    ny, nz, nx, sums, peaks, ms_ref, cot_ref, table_t, cols, rows_ref, rho_ref, ids_ref, inv_ref,
    cv_ref, top_ref, nbl_ref, nbr_ref, left_ref, right_ref, lst_ref, c_ref, cg_ref,
    cotm_ref, part_ref, zbuf, line, ybuf, xsrc, xbuf, values, tops,
    nb_send, nb_recv, z_send, z_recv, y_send, y_recv, x_send, x_recv, g_send, g_recv, t_send, t_recv,
):
    sku = lax.axis_index("sku")
    cat = lax.axis_index("cat")
    y, z = sku // nz, sku % nz
    n = ny * nz
    to_right, to_left = (sku + 1) % n, (sku + n - 1) % n
    next_z = [(z + k) % nz for k in range(1, nz)]
    along_z = [y * nz + other for other in next_z]
    along_y = [(y + k) % ny * nz + z for k in range(1, ny)]
    along_x = [(cat + k) % nx for k in range(1, nx)]

    barrier = pltpu.get_barrier_semaphore()
    for other in along_z + along_y + [to_right, to_left]:
        pl.semaphore_signal(barrier, inc=1, device_id={"sku": other}, device_id_type=MESH)
    for other in along_x:
        pl.semaphore_signal(barrier, inc=1, device_id={"cat": other}, device_id_type=MESH)
    for b in range(left_ref.shape[0]):
        condense(
            b, sums, peaks, ms_ref, cot_ref, cotm_ref, table_t, cols, ids_ref, part_ref, left_ref, right_ref, lst_ref,
            c_ref,
        )
    pl.semaphore_wait(barrier, nz + ny + nx - 1)

    def send(src, dst, send_sem, recv_sem, device):
        copy = pltpu.make_async_remote_copy(
            src_ref=src, dst_ref=dst, send_sem=send_sem, recv_sem=recv_sem, device_id=device, device_id_type=MESH
        )
        copy.start()
        return copy

    used = pl.ds(0, ROWS)

    def slot(k, size):
        return pl.ds(pl.multiple_of(k * 24, 8), size)

    by_z = [
        send(part_ref.at[next_z[k], used], zbuf.at[slot(z, ROWS)], z_send.at[k], z_recv.at[k], {"sku": other})
        for k, other in enumerate(along_z)
    ]
    near = [
        send(right_ref, nbl_ref, nb_send.at[0], nb_recv.at[0], {"sku": to_right}),
        send(left_ref, nbr_ref, nb_send.at[1], nb_recv.at[1], {"sku": to_left}),
    ]
    zbuf[slot(z, 24), :] = part_ref[z]
    ah, al = halves(rows_ref[0:1, :])
    pick = iota((16, ah.shape[1]), 0)
    weights = jnp.where(pick == 0, ah.astype(F32), jnp.where(pick == 1, al.astype(F32), 0.0)).astype(BF16)
    for k in range(cg_ref.shape[1] // CHUNK):
        at = pl.ds(k * CHUNK, CHUNK)
        cg_ref[:, at] = jnp.sum(dot(weights, cotm_ref[:, at]), axis=0, keepdims=True) * inv_ref[0:1, at]
    for copy in by_z:
        copy.wait_recv()

    line[0:8, :], line[8:16, :] = join(zbuf, nz, True, True)
    begin, end = zbuf[16:24, :], zbuf[24 * nz - 8 : 24 * nz, :]
    row, left = iota((8, LANES), 0), iota((8, LANES), 1) < LANES // 2
    from_begin = (row == 2) | (left & ((row == 0) | (row == 3)))
    one = end[3:4] == turn(end)[0:1]
    end = jnp.where(left & (row == 1) & one, NEG, end)
    line[16:24, :] = jnp.where(from_begin, begin, end)

    by_y = [
        send(line.at[used], ybuf.at[slot(y, ROWS)], y_send.at[k], y_recv.at[k], {"sku": other})
        for k, other in enumerate(along_y)
    ]
    ybuf[slot(y, 24), :] = line[...]
    for copy in by_y:
        copy.wait_recv()
    logs, cot = join(ybuf, ny, False, False)
    value = rho_ref[0:8, :] * logs
    values[0:8, :] = value
    values[8:16, :] = cot
    top = jnp.max(value, axis=0, keepdims=True)
    top = jnp.maximum(top, turn(top))
    total = jnp.sum(jnp.exp(value - top), axis=0, keepdims=True)
    cot = jnp.sum(cot, axis=0, keepdims=True)
    xsrc[0:1, :] = top + jnp.log(total + turn(total))
    xsrc[1:2, :] = cot + turn(cot)
    xsrc[2:8, :] = jnp.zeros((6, LANES), F32)

    by_x = [send(xsrc, xbuf.at[k], x_send.at[k], x_recv.at[k], {"cat": other}) for k, other in enumerate(along_x)]
    gather = [
        send(values, cv_ref.at[z], g_send.at[k], g_recv.at[k], {"sku": other}) for k, other in enumerate(along_z)
    ]
    cv_ref[z] = values[...]
    for copy in by_x:
        copy.wait_recv()
    groups = [xsrc[0:1, :]] + [xbuf[k, 0:1, :] for k in range(nx - 1)]
    top = functools.reduce(jnp.maximum, groups + [jnp.zeros((1, LANES), F32)])
    tops[0:1, :] = top + jnp.log(jnp.exp(-top) + sum(jnp.exp(group - top) for group in groups))
    tops[1:2, :] = xsrc[1:2, :] + sum(xbuf[k, 1:2, :] for k in range(nx - 1))
    tops[2:8, :] = jnp.zeros((6, LANES), F32)
    last = [send(tops, top_ref.at[z], t_send.at[k], t_recv.at[k], {"sku": other}) for k, other in enumerate(along_z)]
    top_ref[z] = tops[...]
    for copy in near + gather + last:
        copy.wait_recv()
    for copy in by_z + near + by_y + by_x + gather + last:
        copy.wait_send()


def slope_kernel(
    wh_ref, wl_ref, lst_ref, r_ref, c_ref, cv_ref, top_ref, nbl_ref, nbr_ref, left_ref, right_ref, cg_ref, ids_ref,
    rows_ref, cols, rho_ref, grad_ref, path_ref, hs,
):
    subs = lst_ref.shape[0]
    blocks = nbl_ref.shape[0]
    width = ids_ref.shape[1]
    lam, par, irho, ilam = cols[0], cols[2], cols[3], cols[4]
    cats = 16
    spot = iota((subs, LANES), 1)
    parents = jnp.where(((spot % cats).astype(F32) == par) & (spot < 3 * cats), 1.0, 0.0).astype(BF16)[:, : 3 * cats]
    row = iota((subs, LANES), 0).astype(F32)
    for b in range(blocks):
        at = pl.ds(b * LANES, LANES)
        from_left, from_right = nbl_ref[b], nbr_ref[b]
        first_id, last_id = left_ref[b, 2:3, :], right_ref[b, 2:3, :]
        values, cots = [
            jnp.concatenate(pack(cv_ref[2 * b, 8 * k : 8 * k + 8, :], cv_ref[2 * b + 1, 8 * k : 8 * k + 8, :]), axis=0)
            for k in range(2)
        ]
        top = jnp.where(iota((8, LANES), 1) < LANES // 2, top_ref[2 * b], top_ref[2 * b + 1])
        inclusive = top[0:1]
        slopes = (1.0 - 1.0 / rho_ref[8:24, :]) * cots - top[1:2] * jnp.exp(values - inclusive)
        left_hit = (row == first_id) & (from_left[2:3] == first_id)
        right_hit = (row == last_id) & (from_right[2:3] == last_id)
        extra = jnp.where(left_hit, from_left[0:1], jnp.where(right_hit, from_right[0:1], NEG))
        level = lse2(lst_ref[:, at], extra)
        sub_cot = c_ref[:, at] + jnp.where(left_hit, from_left[1:2], jnp.where(right_hit, from_right[1:2], 0.0))
        cat_value = dot(parents, jnp.concatenate(thirds(values), axis=0))
        d_cat = dot(parents, jnp.concatenate(thirds(slopes), axis=0))
        log_sub = (lam * level - cat_value) * irho
        path = rows_ref[1:2, at] - level + log_sub + (cat_value - inclusive)
        d_sub = (irho - ilam) * sub_cot + jnp.exp(log_sub) * d_cat
        slope = rows_ref[0:1, at] * jnp.exp(r_ref[:, at] - level) * d_sub
        hs[0:subs, at], hs[subs:, at] = halves(slope)
        ph, plo = halves(jnp.transpose(path))
        path_ref[at, 0:subs] = ph
        path_ref[at, subs:] = plo
    for k in range(width // CHUNK):
        at = pl.ds(k * CHUNK, CHUNK)
        both = dot(hs[...], wh_ref[:, at])
        found = both[0:subs] + both[subs:] + dot(hs[0:subs, :], wl_ref[:, at])
        hit = iota((subs, CHUNK), 0) == ids_ref[:, at]
        grad_ref[:, at] = -(jnp.sum(jnp.where(hit, found, 0.0), axis=0, keepdims=True) + cg_ref[:, at])


ROW_BLOCK = 64


def demand_kernel(ms_ref, path_ref, table, out_hbm, value_ref, sem):
    markets, width = ms_ref.shape

    def flush(b):
        rows = pl.ds(b * ROW_BLOCK, ROW_BLOCK)
        return pltpu.make_async_copy(value_ref.at[rows], out_hbm.at[rows, 0, :], sem.at[b])

    for b in range(markets // ROW_BLOCK):
        rows = pl.ds(b * ROW_BLOCK, ROW_BLOCK)
        for k in range(width // CHUNK):
            at = pl.ds(k * CHUNK, CHUNK)
            masked = ms_ref[rows, at]
            hits = table[:, at]
            path = dot(path_ref[rows, :], jnp.concatenate([hits, hits], axis=0))
            value_ref[rows, at] = jnp.where(masked > EMPTY, masked + path, 0.0)
        flush(b).start()
    for b in range(markets // ROW_BLOCK):
        flush(b).wait()


def whole():
    return pl.BlockSpec(memory_space=pltpu.VMEM)


def shards(
    n_sku, n_cat, features, taste, price, alpha, market_size, store_brand, sub_scale, cat_scale, availability,
    sku_subcat, subcat_cat, cotangent,
):
    markets, depth = features.shape
    width = price.shape[1]
    subs, cats = sub_scale.shape[1], cat_scale.shape[1]
    blocks = markets // LANES
    operands = (
        features,
        taste.reshape(depth, width),
        price,
        alpha.reshape(1, markets),
        market_size.reshape(1, markets),
        sub_scale,
        store_brand,
        cat_scale,
        subcat_cat,
        availability,
        sku_subcat,
        cotangent.reshape(markets, width),
    )
    operands = [pltpu.with_memory_space_constraint(x, pltpu.HBM) for x in operands]
    sds = jax.ShapeDtypeStruct
    vmem, dma = pltpu.VMEM, pltpu.SemaphoreType.DMA
    ms, wh, wl, cot, sums, peaks, table, table_t, cols, rows, rho_rows, ids, inv = pl.pallas_call(
        local_kernel,
        in_specs=[pl.BlockSpec(memory_space=pl.ANY)] * 12,
        out_specs=[whole()] * 13,
        out_shape=[
            sds((markets, width), F32),
            sds((markets, width), BF16),
            sds((markets, width), BF16),
            sds((markets, width), BF16),
            sds((subs, markets), F32),
            sds((subs, markets), F32),
            sds((subs, width), BF16),
            sds((width, subs), BF16),
            sds((5, subs, LANES), F32),
            sds((8, markets), F32),
            sds((24, LANES), F32),
            sds((1, width), jnp.int32),
            sds((8, width), F32),
        ],
        scratch_shapes=[
            vmem((markets, depth), BF16),
            vmem((depth, width), BF16),
            vmem((1, width), F32),
            vmem((1, subs), F32),
            vmem((1, subs), F32),
            vmem((1, cats), F32),
            vmem((1, subs), jnp.int32),
            vmem((markets, width), jnp.int32),
            vmem((1, markets), F32),
            vmem((8, CHUNK), F32),
            dma((8,)),
            dma,
            dma((width // CHUNK,)),
            dma((blocks,)),
            dma,
        ],
        compiler_params=pltpu.CompilerParams(vmem_limit_bytes=32 * 1024 * 1024),
        name="local_nests",
    )(*operands)

    nz = 2 * blocks
    ny = n_sku // nz
    cv, top, nbl, nbr, left, right, lst, c, cg = pl.pallas_call(
        functools.partial(swap_kernel, ny, nz, n_cat),
        in_specs=[whole()] * 10,
        out_specs=[whole()] * 9,
        out_shape=[sds((nz, 16, LANES), F32), sds((nz, 8, LANES), F32)]
        + [sds((blocks, 8, LANES), F32)] * 4
        + [sds((subs, markets), F32)] * 2
        + [sds((1, width), F32)],
        scratch_shapes=[
            vmem((markets, width), BF16),
            vmem((nz, 24, LANES), F32),
            vmem((nz * 24, LANES), F32),
            vmem((24, LANES), F32),
            vmem((ny * 24, LANES), F32),
            vmem((8, LANES), F32),
            vmem((n_cat - 1, 8, LANES), F32),
            vmem((16, LANES), F32),
            vmem((8, LANES), F32),
        ]
        + [dma((count,)) for count in (2, nz - 1, ny - 1, n_cat - 1, nz - 1, nz - 1) for _ in range(2)],
        compiler_params=pltpu.CompilerParams(
            collective_id=0, has_side_effects=True, vmem_limit_bytes=16 * 1024 * 1024
        ),
        name="swap_nests",
    )(sums, peaks, ms, cot, table_t, cols, rows, rho_rows, ids, inv)

    grad, path = pl.pallas_call(
        slope_kernel,
        in_specs=[whole()] * 16,
        out_specs=[whole()] * 2,
        out_shape=[sds((1, width), F32), sds((markets, 2 * subs), BF16)],
        scratch_shapes=[vmem((2 * subs, markets), BF16)],
        compiler_params=pltpu.CompilerParams(vmem_limit_bytes=16 * 1024 * 1024),
        name="price_slope",
    )(wh, wl, lst, peaks, c, cv, top, nbl, nbr, left, right, cg, ids, rows, cols, rho_rows)
    other = lax.ppermute(grad, "mkt", [(0, 1), (1, 0)])

    demand = pl.pallas_call(
        demand_kernel,
        in_specs=[whole()] * 3,
        out_specs=pl.BlockSpec(memory_space=pl.ANY),
        out_shape=sds((markets, 1, width), F32),
        scratch_shapes=[vmem((markets, width), F32), dma((markets // ROW_BLOCK,))],
        compiler_params=pltpu.CompilerParams(vmem_limit_bytes=16 * 1024 * 1024),
        cost_estimate=pl.CostEstimate(
            flops=2 * markets * width * 2 * subs, bytes_accessed=8 * markets * width, transcendentals=0
        ),
        name="log_demand",
    )(ms, path, table)
    return demand, grad + other


def solution(mesh):
    return jax.shard_map(
        functools.partial(shards, mesh.shape["sku"], mesh.shape["cat"]),
        mesh=mesh,
        in_specs=(
            P("mkt", None),
            P(None, "cat", "sku"),
            P("cat", "sku"),
            P("mkt"),
            P("mkt"),
            P("cat", None),
            P("cat", None),
            P("cat", None),
            P("mkt", "cat", "sku"),
            P("cat", "sku"),
            P("cat", None),
            P("mkt", "cat", "sku"),
        ),
        out_specs=(P("mkt", "cat", "sku"), P("cat", "sku")),
        check_vma=False,
    )
```

```python
import functools

import jax
import jax.numpy as jnp
from jax import lax
from jax.experimental import pallas as pl
from jax.experimental.pallas import tpu as pltpu
from jax.sharding import PartitionSpec as P

F32 = jnp.float32
BF16 = jnp.bfloat16
NEG = -1e30
EMPTY = -1e29
SAFE = 60.0
LANES = 128
CHUNK = 256
MESH = pl.DeviceIdType.MESH
NT = (((1,), (1,)), ((), ()))


def dot(a, b):
    return jnp.dot(a, b, preferred_element_type=F32)


def dot_nt(a, b):
    return lax.dot_general(a, b, NT, preferred_element_type=F32)


def iota(shape, dim):
    return lax.broadcasted_iota(jnp.int32, shape, dim)


def lse2(a, b):
    top = jnp.maximum(a, b)
    return top + jnp.log(1.0 + jnp.exp(jnp.minimum(a, b) - top))


def halves(x):
    high = x.astype(BF16)
    return high, (x - high.astype(F32)).astype(BF16)


def thirds(x):
    high = x.astype(BF16)
    rest = x - high.astype(F32)
    mid = rest.astype(BF16)
    return high, mid, (rest - mid.astype(F32)).astype(BF16)


def column(row):
    n = row.shape[1]
    return jnp.sum(jnp.where(iota((n, n), 0) == iota((n, n), 1), row, 0.0), axis=1, keepdims=True)


def nest_columns(lam_ref, store_ref, rho_ref, par_ref):
    lam = column(lam_ref[...])
    store = column(store_ref[...]) / lam
    par = column(par_ref[...].astype(F32))
    subs, cats = lam_ref.shape[1], rho_ref.shape[1]
    mine = par == iota((subs, cats), 1).astype(F32)
    rho = jnp.sum(jnp.where(mine, rho_ref[...], 0.0), axis=1, keepdims=True)
    return lam, 1.0 / lam, store, par, 1.0 / rho


def pack(low, high):
    left = iota(low.shape, 1) < LANES // 2
    return jnp.where(left, low, turn(high)), jnp.where(left, turn(low), high)


def turn(x):
    return pltpu.roll(x, LANES // 2, 1)


def local_kernel(
    feat_hbm, taste_hbm, price_hbm, alpha_hbm, size_hbm, lam_hbm, store_hbm, rho_hbm, par_hbm, avail_hbm, mem_hbm,
    cot_hbm,
    ms_ref, wh_ref, wl_ref, cot_ref, sums, peaks, table, table_t, cols, rows_ref, rho_rows, ids_ref, inv_ref,
    feat, taste, price, lam_row, store_row, rho_row, par_row, avail, size, worst,
    small_sem, feat_sem, taste_sem, avail_sem, cot_sem,
):
    subs = lam_row.shape[1]
    cats = rho_row.shape[1]
    width = ids_ref.shape[1]
    blocks = ms_ref.shape[0] // LANES
    tiles = width // LANES
    chunks = width // CHUNK
    small = [
        (mem_hbm, ids_ref), (lam_hbm, lam_row), (price_hbm, price), (alpha_hbm, rows_ref.at[0:1]),
        (store_hbm, store_row), (rho_hbm, rho_row), (par_hbm, par_row), (size_hbm, size),
    ]
    small = [pltpu.make_async_copy(src, dst, small_sem.at[k]) for k, (src, dst) in enumerate(small)]
    whole_feat = pltpu.make_async_copy(feat_hbm, feat, feat_sem)
    whole_cot = pltpu.make_async_copy(cot_hbm, cot_ref, cot_sem)
    tastes = []
    for k in range(chunks):
        at = pl.ds(k * CHUNK, CHUNK)
        tastes.append(pltpu.make_async_copy(taste_hbm.at[:, at], taste.at[:, at], taste_sem.at[k]))

    def fetch(b):
        rows = pl.ds(pl.multiple_of(b * LANES, LANES), LANES)
        return pltpu.make_async_copy(avail_hbm.at[rows, 0, :], avail.at[rows], avail_sem.at[b])

    for copy in small:
        copy.start()
    whole_feat.start()
    tastes[0].start()
    fetch(0).start()
    for copy in tastes[1:]:
        copy.start()
    for b in range(1, blocks):
        fetch(b).start()
    whole_cot.start()
    for copy in small:
        copy.wait()

    lam = column(lam_row[...])
    for k in range(chunks):
        at = pl.ds(k * CHUNK, CHUNK)
        hit = iota((subs, CHUNK), 0) == ids_ref[:, at]
        ones = jnp.where(hit, 1.0, 0.0)
        table[:, at] = ones.astype(BF16)
        table_t[at, :] = jnp.transpose(ones).astype(BF16)
        inv = 1.0 / jnp.sum(jnp.where(hit, lam, 0.0), axis=0, keepdims=True)
        inv_ref[0:1, at] = inv
        inv_ref[1:2, at] = inv * price[:, at]
    worst[...] = jnp.zeros_like(worst)

    whole_feat.wait()
    for k in range(chunks):
        at = pl.ds(k * CHUNK, CHUNK)
        tastes[k].wait()
        ms_ref[:, at] = dot(feat[...], taste[:, at])

    @pl.loop(0, blocks)
    def _(b):
        mine = pl.ds(pl.multiple_of(b * LANES, LANES), LANES)
        fetch(b).wait()
        alpha = jnp.transpose(jnp.broadcast_to(rows_ref[0:1, mine], (LANES, LANES)))
        alpha2 = jnp.concatenate([alpha, alpha], axis=1)
        total = jnp.zeros((2 * LANES, subs), F32)
        most = jnp.zeros((8, CHUNK), F32)
        for k in range(chunks):
            at = pl.ds(k * CHUNK, CHUNK)
            scaled = ms_ref[mine, at] * inv_ref[0:1, at] - alpha2 * inv_ref[1:2, at]
            masked = jnp.where(avail[mine, at] == 1, scaled, NEG)
            ms_ref[mine, at] = masked
            most = jnp.maximum(most, jnp.max(jnp.abs(scaled).reshape(LANES // 8, 8, CHUNK), axis=0))
            wh, wl = halves(jnp.exp(masked))
            wh_ref[mine, at] = wh
            wl_ref[mine, at] = wl
            total = total + dot(jnp.concatenate([wh, wl], axis=0), table_t[at, :])
        sums[:, mine] = jnp.transpose(total[:LANES] + total[LANES:])
        worst[...] = jnp.maximum(worst[...], most)

    peaks[...] = jnp.zeros_like(peaks)
    _, ilam, store, par, irho = nest_columns(lam_row, store_row, rho_row, par_row)
    for k, col in enumerate((lam, store, par, irho, ilam)):
        cols[k] = jnp.broadcast_to(col, (subs, LANES))
    rho = jnp.broadcast_to(column(rho_row[...]), (cats, LANES))
    rho_rows[0:8, :] = jnp.where(iota((8, LANES), 1) < LANES // 2, rho[0:8], rho[8:16])
    rho_rows[8:24, :] = rho
    rows_ref[1:2, :] = jnp.log(size[...])
    whole_cot.wait()

    @pl.when(jnp.max(worst[...]) > SAFE)
    def _():
        lane = iota((1, LANES), 1)

        @pl.loop(0, blocks)
        def _(b):
            mine = pl.ds(pl.multiple_of(b * LANES, LANES), LANES)
            carry = jnp.full((LANES, 1), NEG, F32)
            carry_id = jnp.full((1, 1), -1, jnp.int32)
            peak = jnp.zeros((LANES, subs), F32)
            for t in range(tiles):
                at = pl.ds(t * LANES, LANES)
                ids = ids_ref[:, at]
                run = ms_ref[mine, at]
                shift = 1
                while shift < LANES:
                    same = (pltpu.roll(ids, shift, 1) == ids) & (lane >= shift)
                    run = jnp.where(same, jnp.maximum(run, pltpu.roll(run, shift, 1)), run)
                    shift *= 2
                run = jnp.where(ids == carry_id, jnp.maximum(run, carry), run)
                carry = run[:, LANES - 1 :]
                carry_id = ids[:, LANES - 1 :]
                if t + 1 < tiles:
                    following = ids_ref[:, pl.ds((t + 1) * LANES, LANES)][:, 0:1]
                else:
                    following = jnp.full((1, 1), -1, jnp.int32)
                nxt = jnp.where(lane == LANES - 1, following, pltpu.roll(ids, LANES - 1, 1))
                ends = jnp.where((iota((subs, LANES), 0) == ids) & (ids != nxt), 1.0, 0.0).astype(BF16)
                peak = peak + dot_nt(run.astype(BF16), ends)
            peak = jnp.where(peak < EMPTY, 0.0, peak)
            peaks[:, mine] = jnp.transpose(peak)
            peak_half = peak.astype(BF16)
            total = jnp.zeros((2 * LANES, subs), F32)
            for t in range(tiles):
                at = pl.ds(t * LANES, LANES)
                wh, wl = halves(jnp.exp(ms_ref[mine, at] - dot(peak_half, table[:, at])))
                wh_ref[mine, at] = wh
                wl_ref[mine, at] = wl
                total = total + dot(jnp.concatenate([wh, wl], axis=0), table_t[at, :])
            sums[:, mine] = jnp.transpose(total[:LANES] + total[LANES:])


def condense(b, sums, peaks, ms_ref, cot_ref, cotm_ref, table_t, cols, ids_ref, part_ref, left_ref, right_ref, lst_ref, c_ref):
    cats = 16
    subs = sums.shape[0]
    width = ids_ref.shape[1]
    mine = pl.ds(b * LANES, LANES)
    for k in range(width // CHUNK):
        at = pl.ds(k * CHUNK, CHUNK)
        cotm_ref[mine, at] = cot_ref[mine, at] * jnp.where(ms_ref[mine, at] > EMPTY, 1.0, 0.0).astype(BF16)
    total = sums[:, mine]
    raw = jnp.where(total > 0.0, peaks[:, mine] + jnp.log(jnp.where(total > 0.0, total, 1.0)), NEG)
    lam, store, par, irho = cols[0], cols[1], cols[2], cols[3]
    cot_total = jnp.transpose(dot(cotm_ref[mine, :], table_t[...]))
    full = lse2(raw, store)
    lst_ref[:, mine] = full
    c_ref[:, mine] = cot_total
    row = iota((subs, LANES), 0)
    first, last = ids_ref[:, 0:1], ids_ref[:, width - 1 :]
    is_first, is_last = row == first, row == last
    factor = lam * irho
    ratio_all = full * factor
    ratio = jnp.where((row > first) & (row < last), ratio_all, NEG)
    spread = jnp.full((subs, LANES), NEG, F32)
    tops = []
    for c in range(cats):
        hit = par == c
        top = jnp.max(jnp.where(hit, ratio, NEG), axis=0, keepdims=True)
        tops.append(top)
        spread = jnp.where(hit, top, spread)
    tops = jnp.concatenate(tops, axis=0)
    terms = jnp.where(ratio > EMPTY, jnp.exp(ratio - spread), 0.0)
    children = jnp.where(iota((subs, LANES), 1).astype(F32) == par, 1.0, 0.0)
    children = jnp.transpose(children)[0:cats].astype(BF16)
    found = dot(children, jnp.concatenate(halves(terms) + thirds(cot_total), axis=1))
    amount = found[:, 0:LANES] + found[:, LANES : 2 * LANES]
    cat_cot = found[:, 2 * LANES : 3 * LANES] + found[:, 3 * LANES : 4 * LANES] + found[:, 4 * LANES :]
    logs = jnp.where(amount > 0.0, tops + jnp.log(jnp.where(amount > 0.0, amount, 1.0)), NEG)

    def at_row(mask, values):
        return jnp.sum(jnp.where(mask, values, 0.0), axis=0, keepdims=True)

    first_id = jnp.broadcast_to(first.astype(F32), (1, LANES))
    last_id = jnp.broadcast_to(last.astype(F32), (1, LANES))
    blank = jnp.zeros((5, LANES), F32)
    low = at_row(is_first, raw)
    left_ref[b] = jnp.concatenate([low, at_row(is_first, cot_total), first_id, blank], axis=0)
    right_ref[b] = jnp.concatenate([at_row(is_last, raw), at_row(is_last, cot_total), last_id, blank], axis=0)
    ends = jnp.concatenate(
        [
            low, at_row(is_last, full), at_row(is_first, ratio_all), first_id, last_id,
            at_row(is_last, factor), at_row(is_first, par), at_row(is_last, par),
        ],
        axis=0,
    )
    pairs = ((logs[0:8], logs[8:16]), (cat_cot[0:8], cat_cot[8:16]), (ends, pltpu.roll(ends, 4, 0)))
    for k, pair in enumerate(pairs):
        part_ref[2 * b, 8 * k : 8 * k + 8], part_ref[2 * b + 1, 8 * k : 8 * k + 8] = pack(*pair)


ROWS = 20


def unpack_ends(buf, count):
    left = iota((count, LANES), 1) < LANES // 2
    front, back = [], []
    for k in range(4):
        line = buf[pl.ds(16 + k, count, stride=24), :]
        other = turn(line)
        front.append(jnp.where(left, line, other))
        back.append(jnp.where(left, other, line))
    return front + back


def join(buf, count, inner, single):
    low, high, alone, first_id, last_id, factor, first_cat, last_cat = unpack_ends(buf, count)
    place = iota((count, LANES), 0)
    joined = (last_id == pltpu.roll(first_id, count - 1, 0)) & (place < count - 1)
    taken = (first_id == pltpu.roll(last_id, 1, 0)) & (place > 0)
    first = jnp.where(taken, NEG, alone)
    last = jnp.where(joined, lse2(high, pltpu.roll(low, count - 1, 0)), high) * factor
    if single:
        last = jnp.where(first_id == last_id, NEG, last)
    here = iota((8, LANES), 0) + jnp.where(iota((8, LANES), 1) < LANES // 2, 0, 8)
    here = here.astype(F32)
    parts = [buf[24 * d : 24 * d + 8, :] for d in range(count)]
    for d in range(count):
        if d > 0 or not inner:
            parts.append(jnp.where(first_cat[d : d + 1] == here, first[d : d + 1], NEG))
        if d < count - 1 or not inner:
            parts.append(jnp.where(last_cat[d : d + 1] == here, last[d : d + 1], NEG))
    top = functools.reduce(jnp.maximum, parts)
    logs = top + jnp.log(sum(jnp.exp(part - top) for part in parts))
    return logs, sum(buf[24 * d + 8 : 24 * d + 16, :] for d in range(count))


def swap_kernel(
    ny, nz, nx, sums, peaks, ms_ref, cot_ref, table_t, cols, rows_ref, rho_ref, ids_ref, inv_ref,
    cv_ref, top_ref, nbl_ref, nbr_ref, left_ref, right_ref, lst_ref, c_ref, cg_ref,
    cotm_ref, part_ref, zbuf, line, ybuf, xsrc, xbuf, values, tops,
    nb_send, nb_recv, z_send, z_recv, y_send, y_recv, x_send, x_recv, g_send, g_recv, t_send, t_recv,
):
    sku = lax.axis_index("sku")
    cat = lax.axis_index("cat")
    y, z = sku // nz, sku % nz
    n = ny * nz
    to_right, to_left = (sku + 1) % n, (sku + n - 1) % n
    next_z = [(z + k) % nz for k in range(1, nz)]
    along_z = [y * nz + other for other in next_z]
    along_y = [(y + k) % ny * nz + z for k in range(1, ny)]
    along_x = [(cat + k) % nx for k in range(1, nx)]

    barrier = pltpu.get_barrier_semaphore()
    for other in along_z + along_y + [to_right, to_left]:
        pl.semaphore_signal(barrier, inc=1, device_id={"sku": other}, device_id_type=MESH)
    for other in along_x:
        pl.semaphore_signal(barrier, inc=1, device_id={"cat": other}, device_id_type=MESH)
    for b in range(left_ref.shape[0]):
        condense(
            b, sums, peaks, ms_ref, cot_ref, cotm_ref, table_t, cols, ids_ref, part_ref, left_ref, right_ref, lst_ref,
            c_ref,
        )
    pl.semaphore_wait(barrier, nz + ny + nx - 1)

    def send(src, dst, send_sem, recv_sem, device):
        copy = pltpu.make_async_remote_copy(
            src_ref=src, dst_ref=dst, send_sem=send_sem, recv_sem=recv_sem, device_id=device, device_id_type=MESH
        )
        copy.start()
        return copy

    used = pl.ds(0, ROWS)

    def slot(k, size):
        return pl.ds(pl.multiple_of(k * 24, 8), size)

    by_z = [
        send(part_ref.at[next_z[k], used], zbuf.at[slot(z, ROWS)], z_send.at[k], z_recv.at[k], {"sku": other})
        for k, other in enumerate(along_z)
    ]
    near = [
        send(right_ref, nbl_ref, nb_send.at[0], nb_recv.at[0], {"sku": to_right}),
        send(left_ref, nbr_ref, nb_send.at[1], nb_recv.at[1], {"sku": to_left}),
    ]
    zbuf[slot(z, 24), :] = part_ref[z]
    ah, al = halves(rows_ref[0:1, :])
    pick = iota((16, ah.shape[1]), 0)
    weights = jnp.where(pick == 0, ah.astype(F32), jnp.where(pick == 1, al.astype(F32), 0.0)).astype(BF16)
    for k in range(cg_ref.shape[1] // CHUNK):
        at = pl.ds(k * CHUNK, CHUNK)
        cg_ref[:, at] = jnp.sum(dot(weights, cotm_ref[:, at]), axis=0, keepdims=True) * inv_ref[0:1, at]
    for copy in by_z:
        copy.wait_recv()

    line[0:8, :], line[8:16, :] = join(zbuf, nz, True, True)
    begin, end = zbuf[16:24, :], zbuf[24 * nz - 8 : 24 * nz, :]
    row, left = iota((8, LANES), 0), iota((8, LANES), 1) < LANES // 2
    from_begin = (row == 2) | (left & ((row == 0) | (row == 3)))
    one = end[3:4] == turn(end)[0:1]
    end = jnp.where(left & (row == 1) & one, NEG, end)
    line[16:24, :] = jnp.where(from_begin, begin, end)

    by_y = [
        send(line.at[used], ybuf.at[slot(y, ROWS)], y_send.at[k], y_recv.at[k], {"sku": other})
        for k, other in enumerate(along_y)
    ]
    ybuf[slot(y, 24), :] = line[...]
    for copy in by_y:
        copy.wait_recv()
    logs, cot = join(ybuf, ny, False, False)
    value = rho_ref[0:8, :] * logs
    values[0:8, :] = value
    values[8:16, :] = cot
    top = jnp.max(value, axis=0, keepdims=True)
    top = jnp.maximum(top, turn(top))
    total = jnp.sum(jnp.exp(value - top), axis=0, keepdims=True)
    cot = jnp.sum(cot, axis=0, keepdims=True)
    xsrc[0:1, :] = top + jnp.log(total + turn(total))
    xsrc[1:2, :] = cot + turn(cot)
    xsrc[2:8, :] = jnp.zeros((6, LANES), F32)

    by_x = [send(xsrc, xbuf.at[k], x_send.at[k], x_recv.at[k], {"cat": other}) for k, other in enumerate(along_x)]
    gather = [
        send(values, cv_ref.at[z], g_send.at[k], g_recv.at[k], {"sku": other}) for k, other in enumerate(along_z)
    ]
    cv_ref[z] = values[...]
    for copy in by_x:
        copy.wait_recv()
    groups = [xsrc[0:1, :]] + [xbuf[k, 0:1, :] for k in range(nx - 1)]
    top = functools.reduce(jnp.maximum, groups + [jnp.zeros((1, LANES), F32)])
    tops[0:1, :] = top + jnp.log(jnp.exp(-top) + sum(jnp.exp(group - top) for group in groups))
    tops[1:2, :] = xsrc[1:2, :] + sum(xbuf[k, 1:2, :] for k in range(nx - 1))
    tops[2:8, :] = jnp.zeros((6, LANES), F32)
    last = [send(tops, top_ref.at[z], t_send.at[k], t_recv.at[k], {"sku": other}) for k, other in enumerate(along_z)]
    top_ref[z] = tops[...]
    for copy in near + gather + last:
        copy.wait_recv()
    for copy in by_z + near + by_y + by_x + gather + last:
        copy.wait_send()


def slope_kernel(
    wh_ref, wl_ref, lst_ref, r_ref, c_ref, cv_ref, top_ref, nbl_ref, nbr_ref, left_ref, right_ref, cg_ref, ids_ref,
    rows_ref, cols, rho_ref, grad_ref, path_ref, hs,
):
    subs = lst_ref.shape[0]
    blocks = nbl_ref.shape[0]
    width = ids_ref.shape[1]
    lam, par, irho, ilam = cols[0], cols[2], cols[3], cols[4]
    cats = 16
    spot = iota((subs, LANES), 1)
    parents = jnp.where(((spot % cats).astype(F32) == par) & (spot < 3 * cats), 1.0, 0.0).astype(BF16)[:, : 3 * cats]
    row = iota((subs, LANES), 0).astype(F32)
    for b in range(blocks):
        at = pl.ds(b * LANES, LANES)
        from_left, from_right = nbl_ref[b], nbr_ref[b]
        first_id, last_id = left_ref[b, 2:3, :], right_ref[b, 2:3, :]
        values, cots = [
            jnp.concatenate(pack(cv_ref[2 * b, 8 * k : 8 * k + 8, :], cv_ref[2 * b + 1, 8 * k : 8 * k + 8, :]), axis=0)
            for k in range(2)
        ]
        top = jnp.where(iota((8, LANES), 1) < LANES // 2, top_ref[2 * b], top_ref[2 * b + 1])
        inclusive = top[0:1]
        slopes = (1.0 - 1.0 / rho_ref[8:24, :]) * cots - top[1:2] * jnp.exp(values - inclusive)
        left_hit = (row == first_id) & (from_left[2:3] == first_id)
        right_hit = (row == last_id) & (from_right[2:3] == last_id)
        extra = jnp.where(left_hit, from_left[0:1], jnp.where(right_hit, from_right[0:1], NEG))
        level = lse2(lst_ref[:, at], extra)
        sub_cot = c_ref[:, at] + jnp.where(left_hit, from_left[1:2], jnp.where(right_hit, from_right[1:2], 0.0))
        cat_value = dot(parents, jnp.concatenate(thirds(values), axis=0))
        d_cat = dot(parents, jnp.concatenate(thirds(slopes), axis=0))
        log_sub = (lam * level - cat_value) * irho
        path = rows_ref[1:2, at] - level + log_sub + (cat_value - inclusive)
        d_sub = (irho - ilam) * sub_cot + jnp.exp(log_sub) * d_cat
        slope = rows_ref[0:1, at] * jnp.exp(r_ref[:, at] - level) * d_sub
        hs[0:subs, at], hs[subs:, at] = halves(slope)
        ph, plo = halves(jnp.transpose(path))
        path_ref[at, 0:subs] = ph
        path_ref[at, subs:] = plo
    for k in range(width // CHUNK):
        at = pl.ds(k * CHUNK, CHUNK)
        both = dot(hs[...], wh_ref[:, at])
        found = both[0:subs] + both[subs:] + dot(hs[0:subs, :], wl_ref[:, at])
        hit = iota((subs, CHUNK), 0) == ids_ref[:, at]
        grad_ref[:, at] = -(jnp.sum(jnp.where(hit, found, 0.0), axis=0, keepdims=True) + cg_ref[:, at])


ROW_BLOCK = 128


def demand_kernel(ms_ref, path_ref, table, out_hbm, value_ref, sem):
    markets, width = ms_ref.shape

    def flush(b):
        rows = pl.ds(b * ROW_BLOCK, ROW_BLOCK)
        return pltpu.make_async_copy(value_ref.at[rows], out_hbm.at[rows, 0, :], sem.at[b])

    for b in range(markets // ROW_BLOCK):
        rows = pl.ds(b * ROW_BLOCK, ROW_BLOCK)
        for k in range(width // CHUNK):
            at = pl.ds(k * CHUNK, CHUNK)
            masked = ms_ref[rows, at]
            hits = table[:, at]
            path = dot(path_ref[rows, :], jnp.concatenate([hits, hits], axis=0))
            value_ref[rows, at] = jnp.where(masked > EMPTY, masked + path, 0.0)
        flush(b).start()
    for b in range(markets // ROW_BLOCK):
        flush(b).wait()


def whole():
    return pl.BlockSpec(memory_space=pltpu.VMEM)


def shards(
    n_sku, n_cat, features, taste, price, alpha, market_size, store_brand, sub_scale, cat_scale, availability,
    sku_subcat, subcat_cat, cotangent,
):
    markets, depth = features.shape
    width = price.shape[1]
    subs, cats = sub_scale.shape[1], cat_scale.shape[1]
    blocks = markets // LANES
    operands = (
        features,
        taste.reshape(depth, width),
        price,
        alpha.reshape(1, markets),
        market_size.reshape(1, markets),
        sub_scale,
        store_brand,
        cat_scale,
        subcat_cat,
        availability,
        sku_subcat,
        cotangent.reshape(markets, width),
    )
    operands = [pltpu.with_memory_space_constraint(x, pltpu.HBM) for x in operands]
    sds = jax.ShapeDtypeStruct
    vmem, dma = pltpu.VMEM, pltpu.SemaphoreType.DMA
    ms, wh, wl, cot, sums, peaks, table, table_t, cols, rows, rho_rows, ids, inv = pl.pallas_call(
        local_kernel,
        in_specs=[pl.BlockSpec(memory_space=pl.ANY)] * 12,
        out_specs=[whole()] * 13,
        out_shape=[
            sds((markets, width), F32),
            sds((markets, width), BF16),
            sds((markets, width), BF16),
            sds((markets, width), BF16),
            sds((subs, markets), F32),
            sds((subs, markets), F32),
            sds((subs, width), BF16),
            sds((width, subs), BF16),
            sds((5, subs, LANES), F32),
            sds((8, markets), F32),
            sds((24, LANES), F32),
            sds((1, width), jnp.int32),
            sds((8, width), F32),
        ],
        scratch_shapes=[
            vmem((markets, depth), BF16),
            vmem((depth, width), BF16),
            vmem((1, width), F32),
            vmem((1, subs), F32),
            vmem((1, subs), F32),
            vmem((1, cats), F32),
            vmem((1, subs), jnp.int32),
            vmem((markets, width), jnp.int32),
            vmem((1, markets), F32),
            vmem((8, CHUNK), F32),
            dma((8,)),
            dma,
            dma((width // CHUNK,)),
            dma((blocks,)),
            dma,
        ],
        compiler_params=pltpu.CompilerParams(vmem_limit_bytes=32 * 1024 * 1024),
        name="local_nests",
    )(*operands)

    nz = 2 * blocks
    ny = n_sku // nz
    cv, top, nbl, nbr, left, right, lst, c, cg = pl.pallas_call(
        functools.partial(swap_kernel, ny, nz, n_cat),
        in_specs=[whole()] * 10,
        out_specs=[whole()] * 9,
        out_shape=[sds((nz, 16, LANES), F32), sds((nz, 8, LANES), F32)]
        + [sds((blocks, 8, LANES), F32)] * 4
        + [sds((subs, markets), F32)] * 2
        + [sds((1, width), F32)],
        scratch_shapes=[
            vmem((markets, width), BF16),
            vmem((nz, 24, LANES), F32),
            vmem((nz * 24, LANES), F32),
            vmem((24, LANES), F32),
            vmem((ny * 24, LANES), F32),
            vmem((8, LANES), F32),
            vmem((n_cat - 1, 8, LANES), F32),
            vmem((16, LANES), F32),
            vmem((8, LANES), F32),
        ]
        + [dma((count,)) for count in (2, nz - 1, ny - 1, n_cat - 1, nz - 1, nz - 1) for _ in range(2)],
        compiler_params=pltpu.CompilerParams(
            collective_id=0, has_side_effects=True, vmem_limit_bytes=16 * 1024 * 1024
        ),
        name="swap_nests",
    )(sums, peaks, ms, cot, table_t, cols, rows, rho_rows, ids, inv)

    grad, path = pl.pallas_call(
        slope_kernel,
        in_specs=[whole()] * 16,
        out_specs=[whole()] * 2,
        out_shape=[sds((1, width), F32), sds((markets, 2 * subs), BF16)],
        scratch_shapes=[vmem((2 * subs, markets), BF16)],
        compiler_params=pltpu.CompilerParams(vmem_limit_bytes=16 * 1024 * 1024),
        name="price_slope",
    )(wh, wl, lst, peaks, c, cv, top, nbl, nbr, left, right, cg, ids, rows, cols, rho_rows)
    other = lax.ppermute(grad, "mkt", [(0, 1), (1, 0)])

    demand = pl.pallas_call(
        demand_kernel,
        in_specs=[whole()] * 3,
        out_specs=pl.BlockSpec(memory_space=pl.ANY),
        out_shape=sds((markets, 1, width), F32),
        scratch_shapes=[vmem((markets, width), F32), dma((markets // ROW_BLOCK,))],
        compiler_params=pltpu.CompilerParams(vmem_limit_bytes=16 * 1024 * 1024),
        cost_estimate=pl.CostEstimate(
            flops=2 * markets * width * 2 * subs, bytes_accessed=8 * markets * width, transcendentals=0
        ),
        name="log_demand",
    )(ms, path, table)
    return demand, grad + other


def solution(mesh):
    return jax.shard_map(
        functools.partial(shards, mesh.shape["sku"], mesh.shape["cat"]),
        mesh=mesh,
        in_specs=(
            P("mkt", None),
            P(None, "cat", "sku"),
            P("cat", "sku"),
            P("mkt"),
            P("mkt"),
            P("cat", None),
            P("cat", None),
            P("cat", None),
            P("mkt", "cat", "sku"),
            P("cat", "sku"),
            P("cat", None),
            P("mkt", "cat", "sku"),
        ),
        out_specs=(P("mkt", "cat", "sku"), P("cat", "sku")),
        check_vma=False,
    )
```

```python
import functools

import jax
import jax.numpy as jnp
from jax import lax
from jax.experimental import pallas as pl
from jax.experimental.pallas import tpu as pltpu
from jax.sharding import PartitionSpec as P

F32 = jnp.float32
BF16 = jnp.bfloat16
NEG = -1e30
EMPTY = -1e29
SAFE = 60.0
LANES = 128
CHUNK = 256
MESH = pl.DeviceIdType.MESH
NT = (((1,), (1,)), ((), ()))


def dot(a, b):
    return jnp.dot(a, b, preferred_element_type=F32)


def dot_nt(a, b):
    return lax.dot_general(a, b, NT, preferred_element_type=F32)


def iota(shape, dim):
    return lax.broadcasted_iota(jnp.int32, shape, dim)


def lse2(a, b):
    top = jnp.maximum(a, b)
    return top + jnp.log(1.0 + jnp.exp(jnp.minimum(a, b) - top))


def halves(x):
    high = x.astype(BF16)
    return high, (x - high.astype(F32)).astype(BF16)


def thirds(x):
    high = x.astype(BF16)
    rest = x - high.astype(F32)
    mid = rest.astype(BF16)
    return high, mid, (rest - mid.astype(F32)).astype(BF16)


def column(row):
    n = row.shape[1]
    return jnp.sum(jnp.where(iota((n, n), 0) == iota((n, n), 1), row, 0.0), axis=1, keepdims=True)


def nest_columns(lam_ref, store_ref, rho_ref, par_ref):
    lam = column(lam_ref[...])
    store = column(store_ref[...]) / lam
    par = column(par_ref[...].astype(F32))
    subs, cats = lam_ref.shape[1], rho_ref.shape[1]
    mine = par == iota((subs, cats), 1).astype(F32)
    rho = jnp.sum(jnp.where(mine, rho_ref[...], 0.0), axis=1, keepdims=True)
    return lam, 1.0 / lam, store, par, 1.0 / rho


def pack(low, high):
    left = iota(low.shape, 1) < LANES // 2
    return jnp.where(left, low, turn(high)), jnp.where(left, turn(low), high)


def turn(x):
    return pltpu.roll(x, LANES // 2, 1)


WINDOW = 32


def reach(ids):
    ends = ids.astype(F32)
    first = jnp.min(ends[:, :LANES]).astype(jnp.int32)
    last = jnp.max(ends[:, ends.shape[1] - LANES :]).astype(jnp.int32)
    base = jnp.minimum(first // 8 * 8, LANES - WINDOW)
    return pl.multiple_of(base, 8), last < base + WINDOW


def local_kernel(
    feat_hbm, taste_hbm, price_hbm, alpha_hbm, size_hbm, lam_hbm, store_hbm, rho_hbm, par_hbm, avail_hbm, mem_hbm,
    cot_hbm,
    ms_ref, wh_ref, wl_ref, cot_ref, sums, peaks, table, cols, rows_ref, rho_rows, ids_ref, inv_ref,
    feat, taste, price, lam_row, store_row, rho_row, par_row, avail, size, worst, near,
    small_sem, big_sem, avail_sem, cot_sem,
):
    subs = lam_row.shape[1]
    cats = rho_row.shape[1]
    width = ids_ref.shape[1]
    blocks = ms_ref.shape[0] // LANES
    tiles = width // LANES
    chunks = width // CHUNK
    small = [
        (mem_hbm, ids_ref), (lam_hbm, lam_row), (price_hbm, price), (alpha_hbm, rows_ref.at[0:1]),
        (store_hbm, store_row), (rho_hbm, rho_row), (par_hbm, par_row), (size_hbm, size),
    ]
    small = [pltpu.make_async_copy(src, dst, small_sem.at[k]) for k, (src, dst) in enumerate(small)]
    big = [
        pltpu.make_async_copy(src, dst, big_sem.at[k])
        for k, (src, dst) in enumerate([(taste_hbm, taste), (feat_hbm, feat)])
    ]
    whole_cot = pltpu.make_async_copy(cot_hbm, cot_ref, cot_sem)

    def fetch(b):
        rows = pl.ds(pl.multiple_of(b * LANES, LANES), LANES)
        return pltpu.make_async_copy(avail_hbm.at[rows, 0, :], avail.at[rows], avail_sem.at[b])

    for copy in small[:3] + big + [fetch(0)] + small[3:]:
        copy.start()
    for b in range(1, blocks):
        fetch(b).start()
    whole_cot.start()
    for copy in small:
        copy.wait()

    base, narrow = reach(ids_ref[...])
    lam = column(lam_row[...])
    for k in range(chunks):
        at = pl.ds(k * CHUNK, CHUNK)
        hit = iota((subs, CHUNK), 0) == ids_ref[:, at]
        table[:, at] = jnp.where(hit, 1.0, 0.0).astype(BF16)
        near[:, at] = jnp.where(iota((WINDOW, CHUNK), 0) + base == ids_ref[:, at], 1.0, 0.0).astype(BF16)
        inv = 1.0 / jnp.sum(jnp.where(hit, lam, 0.0), axis=0, keepdims=True)
        inv_ref[0:1, at] = inv
        inv_ref[1:2, at] = inv * price[:, at]
    worst[...] = jnp.zeros_like(worst)
    sums[...] = jnp.zeros_like(sums)
    peaks[...] = jnp.zeros_like(peaks)
    _, ilam, store, par, irho = nest_columns(lam_row, store_row, rho_row, par_row)
    for k, col in enumerate((lam, store, par, irho, ilam)):
        cols[k] = jnp.broadcast_to(col, (subs, LANES))
    rho = jnp.broadcast_to(column(rho_row[...]), (cats, LANES))
    rho_rows[0:8, :] = jnp.where(iota((8, LANES), 1) < LANES // 2, rho[0:8], rho[8:16])
    rho_rows[8:24, :] = rho
    rows_ref[1:2, :] = jnp.log(size[...])
    for copy in big:
        copy.wait()

    @pl.loop(0, blocks)
    def _(b):
        mine = pl.ds(pl.multiple_of(b * LANES, LANES), LANES)
        fetch(b).wait()
        alpha = jnp.transpose(jnp.broadcast_to(rows_ref[0:1, mine], (LANES, LANES)))
        alpha2 = jnp.concatenate([alpha, alpha], axis=1)
        total = jnp.zeros((WINDOW, 2 * LANES), F32)
        most = jnp.zeros((8, CHUNK), F32)
        for k in range(chunks):
            at = pl.ds(k * CHUNK, CHUNK)
            util = dot(feat[mine, :], taste[:, at])
            scaled = util * inv_ref[0:1, at] - alpha2 * inv_ref[1:2, at]
            masked = jnp.where(avail[mine, at] == 1, scaled, NEG)
            ms_ref[mine, at] = masked
            most = jnp.maximum(most, jnp.max(jnp.abs(scaled).reshape(LANES // 8, 8, CHUNK), axis=0))
            wh, wl = halves(jnp.exp(masked))
            wh_ref[mine, at] = wh
            wl_ref[mine, at] = wl
            total = total + dot_nt(near[:, at], jnp.concatenate([wh, wl], axis=0))
        sums[pl.ds(base, WINDOW), mine] = total[:, :LANES] + total[:, LANES:]
        worst[...] = jnp.maximum(worst[...], most)

    @pl.when(jnp.logical_not(narrow))
    def _():
        @pl.loop(0, blocks)
        def _(b):
            mine = pl.ds(pl.multiple_of(b * LANES, LANES), LANES)
            sums[:, mine] = dot_nt(table[...], wh_ref[mine, :]) + dot_nt(table[...], wl_ref[mine, :])

    whole_cot.wait()

    @pl.when(jnp.max(worst[...]) > SAFE)
    def _():
        lane = iota((1, LANES), 1)

        @pl.loop(0, blocks)
        def _(b):
            mine = pl.ds(pl.multiple_of(b * LANES, LANES), LANES)
            carry = jnp.full((LANES, 1), NEG, F32)
            carry_id = jnp.full((1, 1), -1, jnp.int32)
            peak = jnp.zeros((LANES, subs), F32)
            for t in range(tiles):
                at = pl.ds(t * LANES, LANES)
                ids = ids_ref[:, at]
                run = ms_ref[mine, at]
                shift = 1
                while shift < LANES:
                    same = (pltpu.roll(ids, shift, 1) == ids) & (lane >= shift)
                    run = jnp.where(same, jnp.maximum(run, pltpu.roll(run, shift, 1)), run)
                    shift *= 2
                run = jnp.where(ids == carry_id, jnp.maximum(run, carry), run)
                carry = run[:, LANES - 1 :]
                carry_id = ids[:, LANES - 1 :]
                if t + 1 < tiles:
                    following = ids_ref[:, pl.ds((t + 1) * LANES, LANES)][:, 0:1]
                else:
                    following = jnp.full((1, 1), -1, jnp.int32)
                nxt = jnp.where(lane == LANES - 1, following, pltpu.roll(ids, LANES - 1, 1))
                ends = jnp.where((iota((subs, LANES), 0) == ids) & (ids != nxt), 1.0, 0.0).astype(BF16)
                peak = peak + dot_nt(run.astype(BF16), ends)
            peak = jnp.where(peak < EMPTY, 0.0, peak)
            peaks[:, mine] = jnp.transpose(peak)
            peak_half = peak.astype(BF16)
            total = jnp.zeros((subs, 2 * LANES), F32)
            for t in range(tiles):
                at = pl.ds(t * LANES, LANES)
                wh, wl = halves(jnp.exp(ms_ref[mine, at] - dot(peak_half, table[:, at])))
                wh_ref[mine, at] = wh
                wl_ref[mine, at] = wl
                total = total + dot_nt(table[:, at], jnp.concatenate([wh, wl], axis=0))
            sums[:, mine] = total[:, :LANES] + total[:, LANES:]


def condense(b, sums, peaks, ms_ref, cot_ref, cotm_ref, table, cols, ids_ref, part_ref, left_ref, right_ref, lst_ref, c_ref):
    cats = 16
    subs = sums.shape[0]
    width = ids_ref.shape[1]
    mine = pl.ds(b * LANES, LANES)
    for k in range(width // CHUNK):
        at = pl.ds(k * CHUNK, CHUNK)
        cotm_ref[mine, at] = cot_ref[mine, at] * jnp.where(ms_ref[mine, at] > EMPTY, 1.0, 0.0).astype(BF16)
    total = sums[:, mine]
    raw = jnp.where(total > 0.0, peaks[:, mine] + jnp.log(jnp.where(total > 0.0, total, 1.0)), NEG)
    lam, store, par, irho = cols[0], cols[1], cols[2], cols[3]
    cot_total = dot_nt(table[...], cotm_ref[mine, :])
    full = lse2(raw, store)
    lst_ref[:, mine] = full
    c_ref[:, mine] = cot_total
    row = iota((subs, LANES), 0)
    first, last = ids_ref[:, 0:1], ids_ref[:, width - 1 :]
    is_first, is_last = row == first, row == last
    factor = lam * irho
    ratio_all = full * factor
    ratio = jnp.where((row > first) & (row < last), ratio_all, NEG)
    spread = jnp.full((subs, LANES), NEG, F32)
    tops = []
    for c in range(cats):
        hit = par == c
        top = jnp.max(jnp.where(hit, ratio, NEG), axis=0, keepdims=True)
        tops.append(top)
        spread = jnp.where(hit, top, spread)
    tops = jnp.concatenate(tops, axis=0)
    terms = jnp.where(ratio > EMPTY, jnp.exp(ratio - spread), 0.0)
    children = jnp.where(iota((subs, LANES), 1).astype(F32) == par, 1.0, 0.0)
    children = jnp.transpose(children)[0:cats].astype(BF16)
    found = dot(children, jnp.concatenate(halves(terms) + thirds(cot_total), axis=1))
    amount = found[:, 0:LANES] + found[:, LANES : 2 * LANES]
    cat_cot = found[:, 2 * LANES : 3 * LANES] + found[:, 3 * LANES : 4 * LANES] + found[:, 4 * LANES :]
    logs = jnp.where(amount > 0.0, tops + jnp.log(jnp.where(amount > 0.0, amount, 1.0)), NEG)

    def at_row(mask, values):
        return jnp.sum(jnp.where(mask, values, 0.0), axis=0, keepdims=True)

    first_id = jnp.broadcast_to(first.astype(F32), (1, LANES))
    last_id = jnp.broadcast_to(last.astype(F32), (1, LANES))
    blank = jnp.zeros((5, LANES), F32)
    low = at_row(is_first, raw)
    left_ref[b] = jnp.concatenate([low, at_row(is_first, cot_total), first_id, blank], axis=0)
    right_ref[b] = jnp.concatenate([at_row(is_last, raw), at_row(is_last, cot_total), last_id, blank], axis=0)
    ends = jnp.concatenate(
        [
            low, at_row(is_last, full), at_row(is_first, ratio_all), first_id, last_id,
            at_row(is_last, factor), at_row(is_first, par), at_row(is_last, par),
        ],
        axis=0,
    )
    pairs = ((logs[0:8], logs[8:16]), (cat_cot[0:8], cat_cot[8:16]), (ends, pltpu.roll(ends, 4, 0)))
    for k, pair in enumerate(pairs):
        part_ref[2 * b, 8 * k : 8 * k + 8], part_ref[2 * b + 1, 8 * k : 8 * k + 8] = pack(*pair)


ROWS = 20


def unpack_ends(buf, count):
    left = iota((count, LANES), 1) < LANES // 2
    front, back = [], []
    for k in range(4):
        line = buf[pl.ds(16 + k, count, stride=24), :]
        other = turn(line)
        front.append(jnp.where(left, line, other))
        back.append(jnp.where(left, other, line))
    return front + back


def join(buf, count, inner, single):
    low, high, alone, first_id, last_id, factor, first_cat, last_cat = unpack_ends(buf, count)
    place = iota((count, LANES), 0)
    joined = (last_id == pltpu.roll(first_id, count - 1, 0)) & (place < count - 1)
    taken = (first_id == pltpu.roll(last_id, 1, 0)) & (place > 0)
    first = jnp.where(taken, NEG, alone)
    last = jnp.where(joined, lse2(high, pltpu.roll(low, count - 1, 0)), high) * factor
    if single:
        last = jnp.where(first_id == last_id, NEG, last)
    here = iota((8, LANES), 0) + jnp.where(iota((8, LANES), 1) < LANES // 2, 0, 8)
    here = here.astype(F32)
    parts = [buf[24 * d : 24 * d + 8, :] for d in range(count)]
    for d in range(count):
        if d > 0 or not inner:
            parts.append(jnp.where(first_cat[d : d + 1] == here, first[d : d + 1], NEG))
        if d < count - 1 or not inner:
            parts.append(jnp.where(last_cat[d : d + 1] == here, last[d : d + 1], NEG))
    top = functools.reduce(jnp.maximum, parts)
    logs = top + jnp.log(sum(jnp.exp(part - top) for part in parts))
    return logs, sum(buf[24 * d + 8 : 24 * d + 16, :] for d in range(count))


def swap_kernel(
    ny, nz, nx, sums, peaks, ms_ref, cot_ref, table, cols, rows_ref, rho_ref, ids_ref, inv_ref,
    cv_ref, top_ref, nbl_ref, nbr_ref, left_ref, right_ref, lst_ref, c_ref, cg_ref,
    cotm_ref, part_ref, zbuf, line, ybuf, xsrc, xbuf, values, tops,
    nb_send, nb_recv, z_send, z_recv, y_send, y_recv, x_send, x_recv, g_send, g_recv, t_send, t_recv,
):
    sku = lax.axis_index("sku")
    cat = lax.axis_index("cat")
    y, z = sku // nz, sku % nz
    n = ny * nz
    to_right, to_left = (sku + 1) % n, (sku + n - 1) % n
    next_z = [(z + k) % nz for k in range(1, nz)]
    along_z = [y * nz + other for other in next_z]
    along_y = [(y + k) % ny * nz + z for k in range(1, ny)]
    along_x = [(cat + k) % nx for k in range(1, nx)]

    barrier = pltpu.get_barrier_semaphore()
    for other in along_z + along_y + [to_right, to_left]:
        pl.semaphore_signal(barrier, inc=1, device_id={"sku": other}, device_id_type=MESH)
    for other in along_x:
        pl.semaphore_signal(barrier, inc=1, device_id={"cat": other}, device_id_type=MESH)
    for b in range(left_ref.shape[0]):
        condense(
            b, sums, peaks, ms_ref, cot_ref, cotm_ref, table, cols, ids_ref, part_ref, left_ref, right_ref, lst_ref,
            c_ref,
        )
    pl.semaphore_wait(barrier, nz + ny + nx - 1)

    def send(src, dst, send_sem, recv_sem, device):
        copy = pltpu.make_async_remote_copy(
            src_ref=src, dst_ref=dst, send_sem=send_sem, recv_sem=recv_sem, device_id=device, device_id_type=MESH
        )
        copy.start()
        return copy

    used = pl.ds(0, ROWS)

    def slot(k, size):
        return pl.ds(pl.multiple_of(k * 24, 8), size)

    by_z = [
        send(part_ref.at[next_z[k], used], zbuf.at[slot(z, ROWS)], z_send.at[k], z_recv.at[k], {"sku": other})
        for k, other in enumerate(along_z)
    ]
    near = [
        send(right_ref, nbl_ref, nb_send.at[0], nb_recv.at[0], {"sku": to_right}),
        send(left_ref, nbr_ref, nb_send.at[1], nb_recv.at[1], {"sku": to_left}),
    ]
    zbuf[slot(z, 24), :] = part_ref[z]
    ah, al = halves(rows_ref[0:1, :])
    pick = iota((16, ah.shape[1]), 0)
    weights = jnp.where(pick == 0, ah.astype(F32), jnp.where(pick == 1, al.astype(F32), 0.0)).astype(BF16)
    for k in range(cg_ref.shape[1] // CHUNK):
        at = pl.ds(k * CHUNK, CHUNK)
        cg_ref[:, at] = jnp.sum(dot(weights, cotm_ref[:, at]), axis=0, keepdims=True) * inv_ref[0:1, at]
    for copy in by_z:
        copy.wait_recv()

    line[0:8, :], line[8:16, :] = join(zbuf, nz, True, True)
    begin, end = zbuf[16:24, :], zbuf[24 * nz - 8 : 24 * nz, :]
    row, left = iota((8, LANES), 0), iota((8, LANES), 1) < LANES // 2
    from_begin = (row == 2) | (left & ((row == 0) | (row == 3)))
    one = end[3:4] == turn(end)[0:1]
    end = jnp.where(left & (row == 1) & one, NEG, end)
    line[16:24, :] = jnp.where(from_begin, begin, end)

    by_y = [
        send(line.at[used], ybuf.at[slot(y, ROWS)], y_send.at[k], y_recv.at[k], {"sku": other})
        for k, other in enumerate(along_y)
    ]
    ybuf[slot(y, 24), :] = line[...]
    for copy in by_y:
        copy.wait_recv()
    logs, cot = join(ybuf, ny, False, False)
    value = rho_ref[0:8, :] * logs
    values[0:8, :] = value
    values[8:16, :] = cot
    top = jnp.max(value, axis=0, keepdims=True)
    top = jnp.maximum(top, turn(top))
    total = jnp.sum(jnp.exp(value - top), axis=0, keepdims=True)
    cot = jnp.sum(cot, axis=0, keepdims=True)
    xsrc[0:1, :] = top + jnp.log(total + turn(total))
    xsrc[1:2, :] = cot + turn(cot)
    xsrc[2:8, :] = jnp.zeros((6, LANES), F32)

    by_x = [send(xsrc, xbuf.at[k], x_send.at[k], x_recv.at[k], {"cat": other}) for k, other in enumerate(along_x)]
    gather = [
        send(values, cv_ref.at[z], g_send.at[k], g_recv.at[k], {"sku": other}) for k, other in enumerate(along_z)
    ]
    cv_ref[z] = values[...]
    for copy in by_x:
        copy.wait_recv()
    groups = [xsrc[0:1, :]] + [xbuf[k, 0:1, :] for k in range(nx - 1)]
    top = functools.reduce(jnp.maximum, groups + [jnp.zeros((1, LANES), F32)])
    tops[0:1, :] = top + jnp.log(jnp.exp(-top) + sum(jnp.exp(group - top) for group in groups))
    tops[1:2, :] = xsrc[1:2, :] + sum(xbuf[k, 1:2, :] for k in range(nx - 1))
    tops[2:8, :] = jnp.zeros((6, LANES), F32)
    last = [send(tops, top_ref.at[z], t_send.at[k], t_recv.at[k], {"sku": other}) for k, other in enumerate(along_z)]
    top_ref[z] = tops[...]
    for copy in near + gather + last:
        copy.wait_recv()
    for copy in by_z + near + by_y + by_x + gather + last:
        copy.wait_send()


def slope_kernel(
    wh_ref, wl_ref, lst_ref, r_ref, c_ref, cv_ref, top_ref, nbl_ref, nbr_ref, left_ref, right_ref, cg_ref, ids_ref,
    rows_ref, cols, rho_ref, grad_ref, path_ref, hs, paths,
):
    subs = lst_ref.shape[0]
    blocks = nbl_ref.shape[0]
    width = ids_ref.shape[1]
    cats = 16
    base, narrow = reach(ids_ref[...])
    paths[...] = jnp.zeros_like(paths)

    def fill(base, count):
        stretch = pl.ds(base, count)
        lam, par, irho, ilam = cols[0, stretch, :], cols[2, stretch, :], cols[3, stretch, :], cols[4, stretch, :]
        spot = iota((count, LANES), 1)
        parents = jnp.where(((spot % cats).astype(F32) == par) & (spot < 3 * cats), 1.0, 0.0).astype(BF16)
        parents = parents[:, : 3 * cats]
        row = (iota((count, LANES), 0) + base).astype(F32)
        for b in range(blocks):
            at = pl.ds(b * LANES, LANES)
            from_left, from_right = nbl_ref[b], nbr_ref[b]
            first_id, last_id = left_ref[b, 2:3, :], right_ref[b, 2:3, :]
            values, cots = [
                jnp.concatenate(
                    pack(cv_ref[2 * b, 8 * k : 8 * k + 8, :], cv_ref[2 * b + 1, 8 * k : 8 * k + 8, :]), axis=0
                )
                for k in range(2)
            ]
            top = jnp.where(iota((8, LANES), 1) < LANES // 2, top_ref[2 * b], top_ref[2 * b + 1])
            inclusive = top[0:1]
            slopes = (1.0 - 1.0 / rho_ref[8:24, :]) * cots - top[1:2] * jnp.exp(values - inclusive)
            left_hit = (row == first_id) & (from_left[2:3] == first_id)
            right_hit = (row == last_id) & (from_right[2:3] == last_id)
            extra = jnp.where(left_hit, from_left[0:1], jnp.where(right_hit, from_right[0:1], NEG))
            level = lse2(lst_ref[stretch, at], extra)
            other_cot = jnp.where(left_hit, from_left[1:2], jnp.where(right_hit, from_right[1:2], 0.0))
            sub_cot = c_ref[stretch, at] + other_cot
            cat_value = dot(parents, jnp.concatenate(thirds(values), axis=0))
            d_cat = dot(parents, jnp.concatenate(thirds(slopes), axis=0))
            log_sub = (lam * level - cat_value) * irho
            paths[stretch, at] = rows_ref[1:2, at] - level + log_sub + (cat_value - inclusive)
            d_sub = (irho - ilam) * sub_cot + jnp.exp(log_sub) * d_cat
            slope = rows_ref[0:1, at] * jnp.exp(r_ref[stretch, at] - level) * d_sub
            hs[0:count, at], hs[count : 2 * count, at] = halves(slope)
        for k in range(width // CHUNK):
            at = pl.ds(k * CHUNK, CHUNK)
            both = dot(hs[0 : 2 * count, :], wh_ref[:, at])
            found = both[0:count] + both[count:] + dot(hs[0:count, :], wl_ref[:, at])
            hit = iota((count, CHUNK), 0) + base == ids_ref[:, at]
            grad_ref[:, at] = -(jnp.sum(jnp.where(hit, found, 0.0), axis=0, keepdims=True) + cg_ref[:, at])

    @pl.when(narrow)
    def _():
        fill(base, WINDOW)

    @pl.when(jnp.logical_not(narrow))
    def _():
        fill(0, subs)

    for b in range(blocks):
        at = pl.ds(b * LANES, LANES)
        path_ref[at, 0:subs], path_ref[at, subs:] = halves(jnp.transpose(paths[:, at]))


ROW_BLOCK = 128


def demand_kernel(ms_ref, path_ref, table, out_hbm, value_ref, sem):
    markets, width = ms_ref.shape

    def flush(b):
        rows = pl.ds(b * ROW_BLOCK, ROW_BLOCK)
        return pltpu.make_async_copy(value_ref.at[rows], out_hbm.at[rows, 0, :], sem.at[b])

    for b in range(markets // ROW_BLOCK):
        rows = pl.ds(b * ROW_BLOCK, ROW_BLOCK)
        for k in range(width // CHUNK):
            at = pl.ds(k * CHUNK, CHUNK)
            masked = ms_ref[rows, at]
            hits = table[:, at]
            path = dot(path_ref[rows, :], jnp.concatenate([hits, hits], axis=0))
            value_ref[rows, at] = jnp.where(masked > EMPTY, masked + path, 0.0)
        flush(b).start()
    for b in range(markets // ROW_BLOCK):
        flush(b).wait()


def whole():
    return pl.BlockSpec(memory_space=pltpu.VMEM)


def shards(
    n_sku, n_cat, features, taste, price, alpha, market_size, store_brand, sub_scale, cat_scale, availability,
    sku_subcat, subcat_cat, cotangent,
):
    markets, depth = features.shape
    width = price.shape[1]
    subs, cats = sub_scale.shape[1], cat_scale.shape[1]
    blocks = markets // LANES
    operands = (
        features,
        taste.reshape(depth, width),
        price,
        alpha.reshape(1, markets),
        market_size.reshape(1, markets),
        sub_scale,
        store_brand,
        cat_scale,
        subcat_cat,
        availability,
        sku_subcat,
        cotangent.reshape(markets, width),
    )
    operands = [pltpu.with_memory_space_constraint(x, pltpu.HBM) for x in operands]
    sds = jax.ShapeDtypeStruct
    vmem, dma = pltpu.VMEM, pltpu.SemaphoreType.DMA
    ms, wh, wl, cot, sums, peaks, table, cols, rows, rho_rows, ids, inv = pl.pallas_call(
        local_kernel,
        in_specs=[pl.BlockSpec(memory_space=pl.ANY)] * 12,
        out_specs=[whole()] * 12,
        out_shape=[
            sds((markets, width), F32),
            sds((markets, width), BF16),
            sds((markets, width), BF16),
            sds((markets, width), BF16),
            sds((subs, markets), F32),
            sds((subs, markets), F32),
            sds((subs, width), BF16),
            sds((5, subs, LANES), F32),
            sds((8, markets), F32),
            sds((24, LANES), F32),
            sds((1, width), jnp.int32),
            sds((8, width), F32),
        ],
        scratch_shapes=[
            vmem((markets, depth), BF16),
            vmem((depth, width), BF16),
            vmem((1, width), F32),
            vmem((1, subs), F32),
            vmem((1, subs), F32),
            vmem((1, cats), F32),
            vmem((1, subs), jnp.int32),
            vmem((markets, width), jnp.int32),
            vmem((1, markets), F32),
            vmem((8, CHUNK), F32),
            vmem((WINDOW, width), BF16),
            dma((8,)),
            dma((2,)),
            dma((blocks,)),
            dma,
        ],
        compiler_params=pltpu.CompilerParams(vmem_limit_bytes=32 * 1024 * 1024),
        name="local_nests",
    )(*operands)

    nz = 2 * blocks
    ny = n_sku // nz
    cv, top, nbl, nbr, left, right, lst, c, cg = pl.pallas_call(
        functools.partial(swap_kernel, ny, nz, n_cat),
        in_specs=[whole()] * 10,
        out_specs=[whole()] * 9,
        out_shape=[sds((nz, 16, LANES), F32), sds((nz, 8, LANES), F32)]
        + [sds((blocks, 8, LANES), F32)] * 4
        + [sds((subs, markets), F32)] * 2
        + [sds((1, width), F32)],
        scratch_shapes=[
            vmem((markets, width), BF16),
            vmem((nz, 24, LANES), F32),
            vmem((nz * 24, LANES), F32),
            vmem((24, LANES), F32),
            vmem((ny * 24, LANES), F32),
            vmem((8, LANES), F32),
            vmem((n_cat - 1, 8, LANES), F32),
            vmem((16, LANES), F32),
            vmem((8, LANES), F32),
        ]
        + [dma((count,)) for count in (2, nz - 1, ny - 1, n_cat - 1, nz - 1, nz - 1) for _ in range(2)],
        compiler_params=pltpu.CompilerParams(
            collective_id=0, has_side_effects=True, vmem_limit_bytes=16 * 1024 * 1024
        ),
        name="swap_nests",
    )(sums, peaks, ms, cot, table, cols, rows, rho_rows, ids, inv)

    grad, path = pl.pallas_call(
        slope_kernel,
        in_specs=[whole()] * 16,
        out_specs=[whole()] * 2,
        out_shape=[sds((1, width), F32), sds((markets, 2 * subs), BF16)],
        scratch_shapes=[vmem((2 * subs, markets), BF16), vmem((subs, markets), F32)],
        compiler_params=pltpu.CompilerParams(vmem_limit_bytes=16 * 1024 * 1024),
        name="price_slope",
    )(wh, wl, lst, peaks, c, cv, top, nbl, nbr, left, right, cg, ids, rows, cols, rho_rows)
    other = lax.ppermute(grad, "mkt", [(0, 1), (1, 0)])

    demand = pl.pallas_call(
        demand_kernel,
        in_specs=[whole()] * 3,
        out_specs=pl.BlockSpec(memory_space=pl.ANY),
        out_shape=sds((markets, 1, width), F32),
        scratch_shapes=[vmem((markets, width), F32), dma((markets // ROW_BLOCK,))],
        compiler_params=pltpu.CompilerParams(vmem_limit_bytes=16 * 1024 * 1024),
        cost_estimate=pl.CostEstimate(
            flops=2 * markets * width * 2 * subs, bytes_accessed=8 * markets * width, transcendentals=0
        ),
        name="log_demand",
    )(ms, path, table)
    return demand, grad + other


def solution(mesh):
    return jax.shard_map(
        functools.partial(shards, mesh.shape["sku"], mesh.shape["cat"]),
        mesh=mesh,
        in_specs=(
            P("mkt", None),
            P(None, "cat", "sku"),
            P("cat", "sku"),
            P("mkt"),
            P("mkt"),
            P("cat", None),
            P("cat", None),
            P("cat", None),
            P("mkt", "cat", "sku"),
            P("cat", "sku"),
            P("cat", None),
            P("mkt", "cat", "sku"),
        ),
        out_specs=(P("mkt", "cat", "sku"), P("cat", "sku")),
        check_vma=False,
    )
```

```python
import functools

import jax
import jax.numpy as jnp
from jax import lax
from jax.experimental import pallas as pl
from jax.experimental.pallas import tpu as pltpu
from jax.sharding import PartitionSpec as P

F32 = jnp.float32
BF16 = jnp.bfloat16
NEG = -1e30
EMPTY = -1e29
SAFE = 60.0
LANES = 128
CHUNK = 256
MESH = pl.DeviceIdType.MESH
NT = (((1,), (1,)), ((), ()))


def dot(a, b):
    return jnp.dot(a, b, preferred_element_type=F32)


def dot_nt(a, b):
    return lax.dot_general(a, b, NT, preferred_element_type=F32)


def iota(shape, dim):
    return lax.broadcasted_iota(jnp.int32, shape, dim)


def lse2(a, b):
    top = jnp.maximum(a, b)
    return top + jnp.log(1.0 + jnp.exp(jnp.minimum(a, b) - top))


def halves(x):
    high = x.astype(BF16)
    return high, (x - high.astype(F32)).astype(BF16)


def thirds(x):
    high = x.astype(BF16)
    rest = x - high.astype(F32)
    mid = rest.astype(BF16)
    return high, mid, (rest - mid.astype(F32)).astype(BF16)


def column(row):
    n = row.shape[1]
    return jnp.sum(jnp.where(iota((n, n), 0) == iota((n, n), 1), row, 0.0), axis=1, keepdims=True)


def nest_columns(lam_ref, store_ref, rho_ref, par_ref):
    lam = column(lam_ref[...])
    store = column(store_ref[...]) / lam
    par = column(par_ref[...].astype(F32))
    subs, cats = lam_ref.shape[1], rho_ref.shape[1]
    mine = par == iota((subs, cats), 1).astype(F32)
    rho = jnp.sum(jnp.where(mine, rho_ref[...], 0.0), axis=1, keepdims=True)
    return lam, 1.0 / lam, store, par, 1.0 / rho


def pack(low, high):
    left = iota(low.shape, 1) < LANES // 2
    return jnp.where(left, low, turn(high)), jnp.where(left, turn(low), high)


def turn(x):
    return pltpu.roll(x, LANES // 2, 1)


WINDOW = 32


def reach(ids):
    ends = ids.astype(F32)
    first = jnp.min(ends[:, :LANES]).astype(jnp.int32)
    last = jnp.max(ends[:, ends.shape[1] - LANES :]).astype(jnp.int32)
    base = jnp.minimum(first // 8 * 8, LANES - WINDOW)
    return pl.multiple_of(base, 8), last < base + WINDOW


def local_kernel(
    feat_hbm, taste_hbm, price_hbm, alpha_hbm, size_hbm, lam_hbm, store_hbm, rho_hbm, par_hbm, avail_hbm, mem_hbm,
    cot_hbm,
    ms_ref, wh_ref, wl_ref, cotm_ref, sums, cot_sums, peaks, table, cols, rows_ref, rho_rows, ids_ref, inv_ref,
    feat, taste, price, lam_row, store_row, rho_row, par_row, avail, size, worst, near,
    small_sem, big_sem, avail_sem, cot_sem,
):
    subs = lam_row.shape[1]
    cats = rho_row.shape[1]
    width = ids_ref.shape[1]
    blocks = ms_ref.shape[0] // LANES
    tiles = width // LANES
    chunks = width // CHUNK
    small = [
        (mem_hbm, ids_ref), (lam_hbm, lam_row), (price_hbm, price), (alpha_hbm, rows_ref.at[0:1]),
        (store_hbm, store_row), (rho_hbm, rho_row), (par_hbm, par_row), (size_hbm, size),
    ]
    small = [pltpu.make_async_copy(src, dst, small_sem.at[k]) for k, (src, dst) in enumerate(small)]
    big = [
        pltpu.make_async_copy(src, dst, big_sem.at[k])
        for k, (src, dst) in enumerate([(taste_hbm, taste), (feat_hbm, feat)])
    ]

    def fetch(b):
        rows = pl.ds(pl.multiple_of(b * LANES, LANES), LANES)
        return (
            pltpu.make_async_copy(avail_hbm.at[rows, 0, :], avail.at[rows], avail_sem.at[b]),
            pltpu.make_async_copy(cot_hbm.at[rows], cotm_ref.at[rows], cot_sem.at[b]),
        )

    for copy in small[:3] + big + list(fetch(0)) + small[3:]:
        copy.start()
    for b in range(1, blocks):
        for copy in fetch(b):
            copy.start()
    for copy in small:
        copy.wait()

    base, narrow = reach(ids_ref[...])
    lam = column(lam_row[...])
    for k in range(chunks):
        at = pl.ds(k * CHUNK, CHUNK)
        hit = iota((subs, CHUNK), 0) == ids_ref[:, at]
        table[:, at] = jnp.where(hit, 1.0, 0.0).astype(BF16)
        near[:, at] = jnp.where(iota((WINDOW, CHUNK), 0) + base == ids_ref[:, at], 1.0, 0.0).astype(BF16)
        inv = 1.0 / jnp.sum(jnp.where(hit, lam, 0.0), axis=0, keepdims=True)
        inv_ref[0:1, at] = inv
        inv_ref[1:2, at] = inv * price[:, at]
    worst[...] = jnp.zeros_like(worst)
    sums[...] = jnp.zeros_like(sums)
    cot_sums[...] = jnp.zeros_like(cot_sums)
    peaks[...] = jnp.zeros_like(peaks)
    _, ilam, store, par, irho = nest_columns(lam_row, store_row, rho_row, par_row)
    for k, col in enumerate((lam, store, par, irho, ilam)):
        cols[k] = jnp.broadcast_to(col, (subs, LANES))
    rho = jnp.broadcast_to(column(rho_row[...]), (cats, LANES))
    rho_rows[0:8, :] = jnp.where(iota((8, LANES), 1) < LANES // 2, rho[0:8], rho[8:16])
    rho_rows[8:24, :] = rho
    rows_ref[1:2, :] = jnp.log(size[...])
    for copy in big:
        copy.wait()

    @pl.loop(0, blocks)
    def _(b):
        mine = pl.ds(pl.multiple_of(b * LANES, LANES), LANES)
        for copy in fetch(b):
            copy.wait()
        alpha = jnp.transpose(jnp.broadcast_to(rows_ref[0:1, mine], (LANES, LANES)))
        alpha2 = jnp.concatenate([alpha, alpha], axis=1)
        total = jnp.zeros((WINDOW, 3 * LANES), F32)
        most = jnp.zeros((8, CHUNK), F32)
        for k in range(chunks):
            at = pl.ds(k * CHUNK, CHUNK)
            util = dot(feat[mine, :], taste[:, at])
            scaled = util * inv_ref[0:1, at] - alpha2 * inv_ref[1:2, at]
            open_ = avail[mine, at]
            masked = jnp.where(open_ == 1, scaled, NEG)
            ms_ref[mine, at] = masked
            most = jnp.maximum(most, jnp.max(jnp.abs(scaled).reshape(LANES // 8, 8, CHUNK), axis=0))
            wh, wl = halves(jnp.exp(masked))
            wh_ref[mine, at] = wh
            wl_ref[mine, at] = wl
            cotm = cotm_ref[mine, at] * open_.astype(F32).astype(BF16)
            cotm_ref[mine, at] = cotm
            total = total + dot_nt(near[:, at], jnp.concatenate([wh, wl, cotm], axis=0))
        sums[pl.ds(base, WINDOW), mine] = total[:, :LANES] + total[:, LANES : 2 * LANES]
        cot_sums[pl.ds(base, WINDOW), mine] = total[:, 2 * LANES :]
        worst[...] = jnp.maximum(worst[...], most)

    @pl.when(jnp.logical_not(narrow))
    def _():
        @pl.loop(0, blocks)
        def _(b):
            mine = pl.ds(pl.multiple_of(b * LANES, LANES), LANES)
            sums[:, mine] = dot_nt(table[...], wh_ref[mine, :]) + dot_nt(table[...], wl_ref[mine, :])
            cot_sums[:, mine] = dot_nt(table[...], cotm_ref[mine, :])

    @pl.when(jnp.max(worst[...]) > SAFE)
    def _():
        lane = iota((1, LANES), 1)

        @pl.loop(0, blocks)
        def _(b):
            mine = pl.ds(pl.multiple_of(b * LANES, LANES), LANES)
            carry = jnp.full((LANES, 1), NEG, F32)
            carry_id = jnp.full((1, 1), -1, jnp.int32)
            peak = jnp.zeros((LANES, subs), F32)
            for t in range(tiles):
                at = pl.ds(t * LANES, LANES)
                ids = ids_ref[:, at]
                run = ms_ref[mine, at]
                shift = 1
                while shift < LANES:
                    same = (pltpu.roll(ids, shift, 1) == ids) & (lane >= shift)
                    run = jnp.where(same, jnp.maximum(run, pltpu.roll(run, shift, 1)), run)
                    shift *= 2
                run = jnp.where(ids == carry_id, jnp.maximum(run, carry), run)
                carry = run[:, LANES - 1 :]
                carry_id = ids[:, LANES - 1 :]
                if t + 1 < tiles:
                    following = ids_ref[:, pl.ds((t + 1) * LANES, LANES)][:, 0:1]
                else:
                    following = jnp.full((1, 1), -1, jnp.int32)
                nxt = jnp.where(lane == LANES - 1, following, pltpu.roll(ids, LANES - 1, 1))
                ends = jnp.where((iota((subs, LANES), 0) == ids) & (ids != nxt), 1.0, 0.0).astype(BF16)
                peak = peak + dot_nt(run.astype(BF16), ends)
            peak = jnp.where(peak < EMPTY, 0.0, peak)
            peaks[:, mine] = jnp.transpose(peak)
            peak_half = peak.astype(BF16)
            total = jnp.zeros((subs, 2 * LANES), F32)
            for t in range(tiles):
                at = pl.ds(t * LANES, LANES)
                wh, wl = halves(jnp.exp(ms_ref[mine, at] - dot(peak_half, table[:, at])))
                wh_ref[mine, at] = wh
                wl_ref[mine, at] = wl
                total = total + dot_nt(table[:, at], jnp.concatenate([wh, wl], axis=0))
            sums[:, mine] = total[:, :LANES] + total[:, LANES:]


def condense(b, sums, cot_sums, peaks, cols, ids_ref, part_ref, left_ref, right_ref, lst_ref):
    cats = 16
    subs = sums.shape[0]
    width = ids_ref.shape[1]
    mine = pl.ds(b * LANES, LANES)
    total = sums[:, mine]
    raw = jnp.where(total > 0.0, peaks[:, mine] + jnp.log(jnp.where(total > 0.0, total, 1.0)), NEG)
    lam, store, par, irho = cols[0], cols[1], cols[2], cols[3]
    cot_total = cot_sums[:, mine]
    full = lse2(raw, store)
    lst_ref[:, mine] = full
    row = iota((subs, LANES), 0)
    first, last = ids_ref[:, 0:1], ids_ref[:, width - 1 :]
    is_first, is_last = row == first, row == last
    factor = lam * irho
    ratio_all = full * factor
    ratio = jnp.where((row > first) & (row < last), ratio_all, NEG)
    spread = jnp.full((subs, LANES), NEG, F32)
    tops = []
    for c in range(cats):
        hit = par == c
        top = jnp.max(jnp.where(hit, ratio, NEG), axis=0, keepdims=True)
        tops.append(top)
        spread = jnp.where(hit, top, spread)
    tops = jnp.concatenate(tops, axis=0)
    terms = jnp.where(ratio > EMPTY, jnp.exp(ratio - spread), 0.0)
    children = jnp.where(iota((subs, LANES), 1).astype(F32) == par, 1.0, 0.0)
    children = jnp.transpose(children)[0:cats].astype(BF16)
    found = dot(children, jnp.concatenate(halves(terms) + thirds(cot_total), axis=1))
    amount = found[:, 0:LANES] + found[:, LANES : 2 * LANES]
    cat_cot = found[:, 2 * LANES : 3 * LANES] + found[:, 3 * LANES : 4 * LANES] + found[:, 4 * LANES :]
    logs = jnp.where(amount > 0.0, tops + jnp.log(jnp.where(amount > 0.0, amount, 1.0)), NEG)

    def at_row(mask, values):
        return jnp.sum(jnp.where(mask, values, 0.0), axis=0, keepdims=True)

    first_id = jnp.broadcast_to(first.astype(F32), (1, LANES))
    last_id = jnp.broadcast_to(last.astype(F32), (1, LANES))
    blank = jnp.zeros((5, LANES), F32)
    low = at_row(is_first, raw)
    left_ref[b] = jnp.concatenate([low, at_row(is_first, cot_total), first_id, blank], axis=0)
    right_ref[b] = jnp.concatenate([at_row(is_last, raw), at_row(is_last, cot_total), last_id, blank], axis=0)
    ends = jnp.concatenate(
        [
            low, at_row(is_last, full), at_row(is_first, ratio_all), first_id, last_id,
            at_row(is_last, factor), at_row(is_first, par), at_row(is_last, par),
        ],
        axis=0,
    )
    pairs = ((logs[0:8], logs[8:16]), (cat_cot[0:8], cat_cot[8:16]), (ends, pltpu.roll(ends, 4, 0)))
    for k, pair in enumerate(pairs):
        part_ref[2 * b, 8 * k : 8 * k + 8], part_ref[2 * b + 1, 8 * k : 8 * k + 8] = pack(*pair)


ROWS = 20


def unpack_ends(buf, count):
    left = iota((count, LANES), 1) < LANES // 2
    front, back = [], []
    for k in range(4):
        line = buf[pl.ds(16 + k, count, stride=24), :]
        other = turn(line)
        front.append(jnp.where(left, line, other))
        back.append(jnp.where(left, other, line))
    return front + back


def join(buf, count, inner, single):
    low, high, alone, first_id, last_id, factor, first_cat, last_cat = unpack_ends(buf, count)
    place = iota((count, LANES), 0)
    joined = (last_id == pltpu.roll(first_id, count - 1, 0)) & (place < count - 1)
    taken = (first_id == pltpu.roll(last_id, 1, 0)) & (place > 0)
    first = jnp.where(taken, NEG, alone)
    last = jnp.where(joined, lse2(high, pltpu.roll(low, count - 1, 0)), high) * factor
    if single:
        last = jnp.where(first_id == last_id, NEG, last)
    here = iota((8, LANES), 0) + jnp.where(iota((8, LANES), 1) < LANES // 2, 0, 8)
    here = here.astype(F32)
    parts = [buf[24 * d : 24 * d + 8, :] for d in range(count)]
    for d in range(count):
        if d > 0 or not inner:
            parts.append(jnp.where(first_cat[d : d + 1] == here, first[d : d + 1], NEG))
        if d < count - 1 or not inner:
            parts.append(jnp.where(last_cat[d : d + 1] == here, last[d : d + 1], NEG))
    top = functools.reduce(jnp.maximum, parts)
    logs = top + jnp.log(sum(jnp.exp(part - top) for part in parts))
    return logs, sum(buf[24 * d + 8 : 24 * d + 16, :] for d in range(count))


def swap_kernel(
    ny, nz, nx, sums, cot_sums, peaks, cotm_ref, cols, rows_ref, rho_ref, ids_ref, inv_ref,
    cv_ref, top_ref, nbl_ref, nbr_ref, left_ref, right_ref, lst_ref, cg_ref,
    part_ref, zbuf, line, ybuf, xsrc, xbuf, values, tops,
    nb_send, nb_recv, z_send, z_recv, y_send, y_recv, x_send, x_recv, g_send, g_recv, t_send, t_recv,
):
    sku = lax.axis_index("sku")
    cat = lax.axis_index("cat")
    y, z = lax.div(sku, nz), lax.rem(sku, nz)
    n = ny * nz
    to_right, to_left = lax.rem(sku + 1, n), lax.rem(sku + n - 1, n)
    next_z = [lax.rem(z + k, nz) for k in range(1, nz)]
    along_z = [y * nz + other for other in next_z]
    along_y = [lax.rem(y + k, ny) * nz + z for k in range(1, ny)]
    along_x = [lax.rem(cat + k, nx) for k in range(1, nx)]

    barrier = pltpu.get_barrier_semaphore()
    for other in along_z + along_y + [to_right, to_left]:
        pl.semaphore_signal(barrier, inc=1, device_id={"sku": other}, device_id_type=MESH)
    for other in along_x:
        pl.semaphore_signal(barrier, inc=1, device_id={"cat": other}, device_id_type=MESH)
    for b in range(left_ref.shape[0]):
        condense(b, sums, cot_sums, peaks, cols, ids_ref, part_ref, left_ref, right_ref, lst_ref)
    pl.semaphore_wait(barrier, nz + ny + nx - 1)

    def send(src, dst, send_sem, recv_sem, device):
        copy = pltpu.make_async_remote_copy(
            src_ref=src, dst_ref=dst, send_sem=send_sem, recv_sem=recv_sem, device_id=device, device_id_type=MESH
        )
        copy.start()
        return copy

    used = pl.ds(0, ROWS)

    def slot(k, size):
        return pl.ds(pl.multiple_of(k * 24, 8), size)

    by_z = [
        send(part_ref.at[next_z[k], used], zbuf.at[slot(z, ROWS)], z_send.at[k], z_recv.at[k], {"sku": other})
        for k, other in enumerate(along_z)
    ]
    near = [
        send(right_ref, nbl_ref, nb_send.at[0], nb_recv.at[0], {"sku": to_right}),
        send(left_ref, nbr_ref, nb_send.at[1], nb_recv.at[1], {"sku": to_left}),
    ]
    zbuf[slot(z, 24), :] = part_ref[z]
    ah, al = halves(rows_ref[0:1, :])
    pick = iota((16, ah.shape[1]), 0)
    weights = jnp.where(pick == 0, ah.astype(F32), jnp.where(pick == 1, al.astype(F32), 0.0)).astype(BF16)
    for k in range(cg_ref.shape[1] // CHUNK):
        at = pl.ds(k * CHUNK, CHUNK)
        cg_ref[:, at] = jnp.sum(dot(weights, cotm_ref[:, at]), axis=0, keepdims=True) * inv_ref[0:1, at]
    for copy in by_z:
        copy.wait_recv()

    line[0:8, :], line[8:16, :] = join(zbuf, nz, True, True)
    begin, end = zbuf[16:24, :], zbuf[24 * nz - 8 : 24 * nz, :]
    row, left = iota((8, LANES), 0), iota((8, LANES), 1) < LANES // 2
    from_begin = (row == 2) | (left & ((row == 0) | (row == 3)))
    one = end[3:4] == turn(end)[0:1]
    end = jnp.where(left & (row == 1) & one, NEG, end)
    line[16:24, :] = jnp.where(from_begin, begin, end)

    by_y = [
        send(line.at[used], ybuf.at[slot(y, ROWS)], y_send.at[k], y_recv.at[k], {"sku": other})
        for k, other in enumerate(along_y)
    ]
    ybuf[slot(y, 24), :] = line[...]
    for copy in by_y:
        copy.wait_recv()
    logs, cot = join(ybuf, ny, False, False)
    value = rho_ref[0:8, :] * logs
    values[0:8, :] = value
    values[8:16, :] = cot
    top = jnp.max(value, axis=0, keepdims=True)
    top = jnp.maximum(top, turn(top))
    total = jnp.sum(jnp.exp(value - top), axis=0, keepdims=True)
    cot = jnp.sum(cot, axis=0, keepdims=True)
    xsrc[0:1, :] = top + jnp.log(total + turn(total))
    xsrc[1:2, :] = cot + turn(cot)
    xsrc[2:8, :] = jnp.zeros((6, LANES), F32)

    by_x = [send(xsrc, xbuf.at[k], x_send.at[k], x_recv.at[k], {"cat": other}) for k, other in enumerate(along_x)]
    gather = [
        send(values, cv_ref.at[z], g_send.at[k], g_recv.at[k], {"sku": other}) for k, other in enumerate(along_z)
    ]
    cv_ref[z] = values[...]
    for copy in by_x:
        copy.wait_recv()
    groups = [xsrc[0:1, :]] + [xbuf[k, 0:1, :] for k in range(nx - 1)]
    top = functools.reduce(jnp.maximum, groups + [jnp.zeros((1, LANES), F32)])
    tops[0:1, :] = top + jnp.log(jnp.exp(-top) + sum(jnp.exp(group - top) for group in groups))
    tops[1:2, :] = xsrc[1:2, :] + sum(xbuf[k, 1:2, :] for k in range(nx - 1))
    tops[2:8, :] = jnp.zeros((6, LANES), F32)
    last = [send(tops, top_ref.at[z], t_send.at[k], t_recv.at[k], {"sku": other}) for k, other in enumerate(along_z)]
    top_ref[z] = tops[...]
    for copy in near + gather + last:
        copy.wait_recv()
    for copy in by_z + near + by_y + by_x + gather + last:
        copy.wait_send()


def slope_kernel(
    wh_ref, wl_ref, lst_ref, r_ref, c_ref, cv_ref, top_ref, nbl_ref, nbr_ref, left_ref, right_ref, cg_ref, ids_ref,
    rows_ref, cols, rho_ref, grad_ref, path_ref, hs, paths,
):
    subs = lst_ref.shape[0]
    blocks = nbl_ref.shape[0]
    width = ids_ref.shape[1]
    cats = 16
    base, narrow = reach(ids_ref[...])
    paths[...] = jnp.zeros_like(paths)

    def fill(base, count):
        stretch = pl.ds(base, count)
        lam, par, irho, ilam = cols[0, stretch, :], cols[2, stretch, :], cols[3, stretch, :], cols[4, stretch, :]
        spot = iota((count, LANES), 1)
        parents = jnp.where(((spot % cats).astype(F32) == par) & (spot < 3 * cats), 1.0, 0.0).astype(BF16)
        parents = parents[:, : 3 * cats]
        row = (iota((count, LANES), 0) + base).astype(F32)
        for b in range(blocks):
            at = pl.ds(b * LANES, LANES)
            from_left, from_right = nbl_ref[b], nbr_ref[b]
            first_id, last_id = left_ref[b, 2:3, :], right_ref[b, 2:3, :]
            values, cots = [
                jnp.concatenate(
                    pack(cv_ref[2 * b, 8 * k : 8 * k + 8, :], cv_ref[2 * b + 1, 8 * k : 8 * k + 8, :]), axis=0
                )
                for k in range(2)
            ]
            top = jnp.where(iota((8, LANES), 1) < LANES // 2, top_ref[2 * b], top_ref[2 * b + 1])
            inclusive = top[0:1]
            slopes = (1.0 - 1.0 / rho_ref[8:24, :]) * cots - top[1:2] * jnp.exp(values - inclusive)
            left_hit = (row == first_id) & (from_left[2:3] == first_id)
            right_hit = (row == last_id) & (from_right[2:3] == last_id)
            extra = jnp.where(left_hit, from_left[0:1], jnp.where(right_hit, from_right[0:1], NEG))
            level = lse2(lst_ref[stretch, at], extra)
            other_cot = jnp.where(left_hit, from_left[1:2], jnp.where(right_hit, from_right[1:2], 0.0))
            sub_cot = c_ref[stretch, at] + other_cot
            cat_value = dot(parents, jnp.concatenate(thirds(values), axis=0))
            d_cat = dot(parents, jnp.concatenate(thirds(slopes), axis=0))
            log_sub = (lam * level - cat_value) * irho
            paths[stretch, at] = rows_ref[1:2, at] - level + log_sub + (cat_value - inclusive)
            d_sub = (irho - ilam) * sub_cot + jnp.exp(log_sub) * d_cat
            slope = rows_ref[0:1, at] * jnp.exp(r_ref[stretch, at] - level) * d_sub
            hs[0:count, at], hs[count : 2 * count, at] = halves(slope)
        for k in range(width // CHUNK):
            at = pl.ds(k * CHUNK, CHUNK)
            both = dot(hs[0 : 2 * count, :], wh_ref[:, at])
            found = both[0:count] + both[count:] + dot(hs[0:count, :], wl_ref[:, at])
            hit = iota((count, CHUNK), 0) + base == ids_ref[:, at]
            grad_ref[:, at] = -(jnp.sum(jnp.where(hit, found, 0.0), axis=0, keepdims=True) + cg_ref[:, at])

    @pl.when(narrow)
    def _():
        fill(base, WINDOW)

    @pl.when(jnp.logical_not(narrow))
    def _():
        fill(0, subs)

    for b in range(blocks):
        at = pl.ds(b * LANES, LANES)
        path_ref[at, 0:subs], path_ref[at, subs:] = halves(jnp.transpose(paths[:, at]))


ROW_BLOCK = 128


def demand_kernel(ms_ref, path_ref, table, out_hbm, value_ref, sem):
    markets, width = ms_ref.shape

    def flush(b):
        rows = pl.ds(b * ROW_BLOCK, ROW_BLOCK)
        return pltpu.make_async_copy(value_ref.at[rows], out_hbm.at[rows, 0, :], sem.at[b])

    for b in range(markets // ROW_BLOCK):
        rows = pl.ds(b * ROW_BLOCK, ROW_BLOCK)
        for k in range(width // CHUNK):
            at = pl.ds(k * CHUNK, CHUNK)
            masked = ms_ref[rows, at]
            hits = table[:, at]
            path = dot(path_ref[rows, :], jnp.concatenate([hits, hits], axis=0))
            value_ref[rows, at] = jnp.where(masked > EMPTY, masked + path, 0.0)
        flush(b).start()
    for b in range(markets // ROW_BLOCK):
        flush(b).wait()


def whole():
    return pl.BlockSpec(memory_space=pltpu.VMEM)


def shards(
    n_sku, n_cat, features, taste, price, alpha, market_size, store_brand, sub_scale, cat_scale, availability,
    sku_subcat, subcat_cat, cotangent,
):
    markets, depth = features.shape
    width = price.shape[1]
    subs, cats = sub_scale.shape[1], cat_scale.shape[1]
    blocks = markets // LANES
    operands = (
        features,
        taste.reshape(depth, width),
        price,
        alpha.reshape(1, markets),
        market_size.reshape(1, markets),
        sub_scale,
        store_brand,
        cat_scale,
        subcat_cat,
        availability,
        sku_subcat,
        cotangent.reshape(markets, width),
    )
    operands = [pltpu.with_memory_space_constraint(x, pltpu.HBM) for x in operands]
    sds = jax.ShapeDtypeStruct
    vmem, dma = pltpu.VMEM, pltpu.SemaphoreType.DMA
    ms, wh, wl, cotm, sums, c, peaks, table, cols, rows, rho_rows, ids, inv = pl.pallas_call(
        local_kernel,
        in_specs=[pl.BlockSpec(memory_space=pl.ANY)] * 12,
        out_specs=[whole()] * 13,
        out_shape=[
            sds((markets, width), F32),
            sds((markets, width), BF16),
            sds((markets, width), BF16),
            sds((markets, width), BF16),
            sds((subs, markets), F32),
            sds((subs, markets), F32),
            sds((subs, markets), F32),
            sds((subs, width), BF16),
            sds((5, subs, LANES), F32),
            sds((8, markets), F32),
            sds((24, LANES), F32),
            sds((1, width), jnp.int32),
            sds((8, width), F32),
        ],
        scratch_shapes=[
            vmem((markets, depth), BF16),
            vmem((depth, width), BF16),
            vmem((1, width), F32),
            vmem((1, subs), F32),
            vmem((1, subs), F32),
            vmem((1, cats), F32),
            vmem((1, subs), jnp.int32),
            vmem((markets, width), jnp.int32),
            vmem((1, markets), F32),
            vmem((8, CHUNK), F32),
            vmem((WINDOW, width), BF16),
            dma((8,)),
            dma((2,)),
            dma((blocks,)),
            dma((blocks,)),
        ],
        compiler_params=pltpu.CompilerParams(vmem_limit_bytes=32 * 1024 * 1024),
        name="local_nests",
    )(*operands)

    nz = 2 * blocks
    ny = n_sku // nz
    cv, top, nbl, nbr, left, right, lst, cg = pl.pallas_call(
        functools.partial(swap_kernel, ny, nz, n_cat),
        in_specs=[whole()] * 9,
        out_specs=[whole()] * 8,
        out_shape=[sds((nz, 16, LANES), F32), sds((nz, 8, LANES), F32)]
        + [sds((blocks, 8, LANES), F32)] * 4
        + [sds((subs, markets), F32)]
        + [sds((1, width), F32)],
        scratch_shapes=[
            vmem((nz, 24, LANES), F32),
            vmem((nz * 24, LANES), F32),
            vmem((24, LANES), F32),
            vmem((ny * 24, LANES), F32),
            vmem((8, LANES), F32),
            vmem((n_cat - 1, 8, LANES), F32),
            vmem((16, LANES), F32),
            vmem((8, LANES), F32),
        ]
        + [dma((count,)) for count in (2, nz - 1, ny - 1, n_cat - 1, nz - 1, nz - 1) for _ in range(2)],
        compiler_params=pltpu.CompilerParams(
            collective_id=0, has_side_effects=True, vmem_limit_bytes=16 * 1024 * 1024
        ),
        name="swap_nests",
    )(sums, c, peaks, cotm, cols, rows, rho_rows, ids, inv)

    grad, path = pl.pallas_call(
        slope_kernel,
        in_specs=[whole()] * 16,
        out_specs=[whole()] * 2,
        out_shape=[sds((1, width), F32), sds((markets, 2 * subs), BF16)],
        scratch_shapes=[vmem((2 * subs, markets), BF16), vmem((subs, markets), F32)],
        compiler_params=pltpu.CompilerParams(vmem_limit_bytes=16 * 1024 * 1024),
        name="price_slope",
    )(wh, wl, lst, peaks, c, cv, top, nbl, nbr, left, right, cg, ids, rows, cols, rho_rows)
    other = lax.ppermute(grad, "mkt", [(0, 1), (1, 0)])

    demand = pl.pallas_call(
        demand_kernel,
        in_specs=[whole()] * 3,
        out_specs=pl.BlockSpec(memory_space=pl.ANY),
        out_shape=sds((markets, 1, width), F32),
        scratch_shapes=[vmem((markets, width), F32), dma((markets // ROW_BLOCK,))],
        compiler_params=pltpu.CompilerParams(vmem_limit_bytes=16 * 1024 * 1024),
        cost_estimate=pl.CostEstimate(
            flops=2 * markets * width * 2 * subs, bytes_accessed=8 * markets * width, transcendentals=0
        ),
        name="log_demand",
    )(ms, path, table)
    return demand, grad + other


def solution(mesh):
    return jax.shard_map(
        functools.partial(shards, mesh.shape["sku"], mesh.shape["cat"]),
        mesh=mesh,
        in_specs=(
            P("mkt", None),
            P(None, "cat", "sku"),
            P("cat", "sku"),
            P("mkt"),
            P("mkt"),
            P("cat", None),
            P("cat", None),
            P("cat", None),
            P("mkt", "cat", "sku"),
            P("cat", "sku"),
            P("cat", None),
            P("mkt", "cat", "sku"),
        ),
        out_specs=(P("mkt", "cat", "sku"), P("cat", "sku")),
        check_vma=False,
    )
```

```python
import functools

import jax
import jax.numpy as jnp
from jax import lax
from jax.experimental import pallas as pl
from jax.experimental.pallas import tpu as pltpu
from jax.sharding import PartitionSpec as P

F32 = jnp.float32
BF16 = jnp.bfloat16
NEG = -1e30
EMPTY = -1e29
SAFE = 60.0
LANES = 128
CHUNK = 256
MESH = pl.DeviceIdType.MESH
NT = (((1,), (1,)), ((), ()))


def dot(a, b):
    return jnp.dot(a, b, preferred_element_type=F32)


def dot_nt(a, b):
    return lax.dot_general(a, b, NT, preferred_element_type=F32)


def iota(shape, dim):
    return lax.broadcasted_iota(jnp.int32, shape, dim)


def lse2(a, b):
    top = jnp.maximum(a, b)
    return top + jnp.log(1.0 + jnp.exp(jnp.minimum(a, b) - top))


def halves(x):
    high = x.astype(BF16)
    return high, (x - high.astype(F32)).astype(BF16)


def thirds(x):
    high = x.astype(BF16)
    rest = x - high.astype(F32)
    mid = rest.astype(BF16)
    return high, mid, (rest - mid.astype(F32)).astype(BF16)


def column(row):
    n = row.shape[1]
    return jnp.sum(jnp.where(iota((n, n), 0) == iota((n, n), 1), row, 0.0), axis=1, keepdims=True)


def nest_columns(lam_ref, store_ref, rho_ref, par_ref):
    lam = column(lam_ref[...])
    store = column(store_ref[...]) / lam
    par = column(par_ref[...].astype(F32))
    subs, cats = lam_ref.shape[1], rho_ref.shape[1]
    mine = par == iota((subs, cats), 1).astype(F32)
    rho = jnp.sum(jnp.where(mine, rho_ref[...], 0.0), axis=1, keepdims=True)
    return lam, 1.0 / lam, store, par, 1.0 / rho


def pack(low, high):
    left = iota(low.shape, 1) < LANES // 2
    return jnp.where(left, low, turn(high)), jnp.where(left, turn(low), high)


def turn(x):
    return pltpu.roll(x, LANES // 2, 1)


WINDOW = 32


def reach(ids):
    ends = ids.astype(F32)
    first = jnp.min(ends[:, :LANES]).astype(jnp.int32)
    last = jnp.max(ends[:, ends.shape[1] - LANES :]).astype(jnp.int32)
    base = jnp.minimum(first // 8 * 8, LANES - WINDOW)
    return pl.multiple_of(base, 8), last < base + WINDOW


def local_kernel(
    feat_hbm, taste_hbm, price_hbm, alpha_hbm, size_hbm, lam_hbm, store_hbm, rho_hbm, par_hbm, avail_hbm, mem_hbm,
    cot_hbm,
    ms_ref, wh_ref, wl_ref, cot_ref, sums, peaks, table, cols, rows_ref, rho_rows, ids_ref, inv_ref,
    feat, taste, price, lam_row, store_row, rho_row, par_row, avail, size, worst, near,
    small_sem, big_sem, avail_sem, cot_sem,
):
    subs = lam_row.shape[1]
    cats = rho_row.shape[1]
    width = ids_ref.shape[1]
    blocks = ms_ref.shape[0] // LANES
    tiles = width // LANES
    chunks = width // CHUNK
    small = [
        (mem_hbm, ids_ref), (lam_hbm, lam_row), (price_hbm, price), (alpha_hbm, rows_ref.at[0:1]),
        (store_hbm, store_row), (rho_hbm, rho_row), (par_hbm, par_row), (size_hbm, size),
    ]
    small = [pltpu.make_async_copy(src, dst, small_sem.at[k]) for k, (src, dst) in enumerate(small)]
    big = [
        pltpu.make_async_copy(src, dst, big_sem.at[k])
        for k, (src, dst) in enumerate([(taste_hbm, taste), (feat_hbm, feat)])
    ]
    whole_cot = pltpu.make_async_copy(cot_hbm, cot_ref, cot_sem)

    def fetch(b):
        rows = pl.ds(pl.multiple_of(b * LANES, LANES), LANES)
        return pltpu.make_async_copy(avail_hbm.at[rows, 0, :], avail.at[rows], avail_sem.at[b])

    for copy in small[:3] + big + small[3:] + [fetch(0)]:
        copy.start()
    for b in range(1, blocks):
        fetch(b).start()
    whole_cot.start()
    for copy in small[:3]:
        copy.wait()

    base, narrow = reach(ids_ref[...])
    lam = column(lam_row[...])
    for k in range(chunks):
        at = pl.ds(k * CHUNK, CHUNK)
        hit = iota((subs, CHUNK), 0) == ids_ref[:, at]
        table[:, at] = jnp.where(hit, 1.0, 0.0).astype(BF16)
        near[:, at] = jnp.where(iota((WINDOW, CHUNK), 0) + base == ids_ref[:, at], 1.0, 0.0).astype(BF16)
        inv = 1.0 / jnp.sum(jnp.where(hit, lam, 0.0), axis=0, keepdims=True)
        inv_ref[0:1, at] = inv
        inv_ref[1:2, at] = inv * price[:, at]
    worst[...] = jnp.zeros_like(worst)
    sums[...] = jnp.zeros_like(sums)
    peaks[...] = jnp.zeros_like(peaks)
    for copy in small[3:]:
        copy.wait()
    _, ilam, store, par, irho = nest_columns(lam_row, store_row, rho_row, par_row)
    for k, col in enumerate((lam, store, par, irho, ilam)):
        cols[k] = jnp.broadcast_to(col, (subs, LANES))
    rho = jnp.broadcast_to(column(rho_row[...]), (cats, LANES))
    rho_rows[0:8, :] = jnp.where(iota((8, LANES), 1) < LANES // 2, rho[0:8], rho[8:16])
    rho_rows[8:24, :] = rho
    rows_ref[1:2, :] = jnp.log(size[...])
    for copy in big:
        copy.wait()

    @pl.loop(0, blocks)
    def _(b):
        mine = pl.ds(pl.multiple_of(b * LANES, LANES), LANES)
        fetch(b).wait()
        alpha = jnp.transpose(jnp.broadcast_to(rows_ref[0:1, mine], (LANES, LANES)))
        alpha2 = jnp.concatenate([alpha, alpha], axis=1)
        total = jnp.zeros((WINDOW, 2 * LANES), F32)
        most = jnp.zeros((8, CHUNK), F32)
        for k in range(chunks):
            at = pl.ds(k * CHUNK, CHUNK)
            util = dot(feat[mine, :], taste[:, at])
            scaled = util * inv_ref[0:1, at] - alpha2 * inv_ref[1:2, at]
            masked = jnp.where(avail[mine, at] == 1, scaled, NEG)
            ms_ref[mine, at] = masked
            most = jnp.maximum(most, jnp.max(jnp.abs(scaled).reshape(LANES // 8, 8, CHUNK), axis=0))
            wh, wl = halves(jnp.exp(masked))
            wh_ref[mine, at] = wh
            wl_ref[mine, at] = wl
            total = total + dot_nt(near[:, at], jnp.concatenate([wh, wl], axis=0))
        sums[pl.ds(base, WINDOW), mine] = total[:, :LANES] + total[:, LANES:]
        worst[...] = jnp.maximum(worst[...], most)

    @pl.when(jnp.logical_not(narrow))
    def _():
        @pl.loop(0, blocks)
        def _(b):
            mine = pl.ds(pl.multiple_of(b * LANES, LANES), LANES)
            sums[:, mine] = dot_nt(table[...], wh_ref[mine, :]) + dot_nt(table[...], wl_ref[mine, :])

    whole_cot.wait()

    @pl.when(jnp.max(worst[...]) > SAFE)
    def _():
        lane = iota((1, LANES), 1)

        @pl.loop(0, blocks)
        def _(b):
            mine = pl.ds(pl.multiple_of(b * LANES, LANES), LANES)
            carry = jnp.full((LANES, 1), NEG, F32)
            carry_id = jnp.full((1, 1), -1, jnp.int32)
            peak = jnp.zeros((LANES, subs), F32)
            for t in range(tiles):
                at = pl.ds(t * LANES, LANES)
                ids = ids_ref[:, at]
                run = ms_ref[mine, at]
                shift = 1
                while shift < LANES:
                    same = (pltpu.roll(ids, shift, 1) == ids) & (lane >= shift)
                    run = jnp.where(same, jnp.maximum(run, pltpu.roll(run, shift, 1)), run)
                    shift *= 2
                run = jnp.where(ids == carry_id, jnp.maximum(run, carry), run)
                carry = run[:, LANES - 1 :]
                carry_id = ids[:, LANES - 1 :]
                if t + 1 < tiles:
                    following = ids_ref[:, pl.ds((t + 1) * LANES, LANES)][:, 0:1]
                else:
                    following = jnp.full((1, 1), -1, jnp.int32)
                nxt = jnp.where(lane == LANES - 1, following, pltpu.roll(ids, LANES - 1, 1))
                ends = jnp.where((iota((subs, LANES), 0) == ids) & (ids != nxt), 1.0, 0.0).astype(BF16)
                peak = peak + dot_nt(run.astype(BF16), ends)
            peak = jnp.where(peak < EMPTY, 0.0, peak)
            peaks[:, mine] = jnp.transpose(peak)
            peak_half = peak.astype(BF16)
            total = jnp.zeros((subs, 2 * LANES), F32)
            for t in range(tiles):
                at = pl.ds(t * LANES, LANES)
                wh, wl = halves(jnp.exp(ms_ref[mine, at] - dot(peak_half, table[:, at])))
                wh_ref[mine, at] = wh
                wl_ref[mine, at] = wl
                total = total + dot_nt(table[:, at], jnp.concatenate([wh, wl], axis=0))
            sums[:, mine] = total[:, :LANES] + total[:, LANES:]


def condense(b, sums, peaks, ms_ref, cot_ref, cotm_ref, table, cols, ids_ref, part_ref, left_ref, right_ref, lst_ref, c_ref):
    cats = 16
    subs = sums.shape[0]
    width = ids_ref.shape[1]
    mine = pl.ds(b * LANES, LANES)
    for k in range(width // CHUNK):
        at = pl.ds(k * CHUNK, CHUNK)
        cotm_ref[mine, at] = cot_ref[mine, at] * jnp.where(ms_ref[mine, at] > EMPTY, 1.0, 0.0).astype(BF16)
    total = sums[:, mine]
    raw = jnp.where(total > 0.0, peaks[:, mine] + jnp.log(jnp.where(total > 0.0, total, 1.0)), NEG)
    lam, store, par, irho = cols[0], cols[1], cols[2], cols[3]
    cot_total = dot_nt(table[...], cotm_ref[mine, :])
    full = lse2(raw, store)
    lst_ref[:, mine] = full
    c_ref[:, mine] = cot_total
    row = iota((subs, LANES), 0)
    first, last = ids_ref[:, 0:1], ids_ref[:, width - 1 :]
    is_first, is_last = row == first, row == last
    factor = lam * irho
    ratio_all = full * factor
    ratio = jnp.where((row > first) & (row < last), ratio_all, NEG)
    spread = jnp.full((subs, LANES), NEG, F32)
    tops = []
    for c in range(cats):
        hit = par == c
        top = jnp.max(jnp.where(hit, ratio, NEG), axis=0, keepdims=True)
        tops.append(top)
        spread = jnp.where(hit, top, spread)
    tops = jnp.concatenate(tops, axis=0)
    terms = jnp.where(ratio > EMPTY, jnp.exp(ratio - spread), 0.0)
    children = jnp.where(iota((subs, LANES), 1).astype(F32) == par, 1.0, 0.0)
    children = jnp.transpose(children)[0:cats].astype(BF16)
    found = dot(children, jnp.concatenate(halves(terms) + thirds(cot_total), axis=1))
    amount = found[:, 0:LANES] + found[:, LANES : 2 * LANES]
    cat_cot = found[:, 2 * LANES : 3 * LANES] + found[:, 3 * LANES : 4 * LANES] + found[:, 4 * LANES :]
    logs = jnp.where(amount > 0.0, tops + jnp.log(jnp.where(amount > 0.0, amount, 1.0)), NEG)

    def at_row(mask, values):
        return jnp.sum(jnp.where(mask, values, 0.0), axis=0, keepdims=True)

    first_id = jnp.broadcast_to(first.astype(F32), (1, LANES))
    last_id = jnp.broadcast_to(last.astype(F32), (1, LANES))
    blank = jnp.zeros((5, LANES), F32)
    low = at_row(is_first, raw)
    left_ref[b] = jnp.concatenate([low, at_row(is_first, cot_total), first_id, blank], axis=0)
    right_ref[b] = jnp.concatenate([at_row(is_last, raw), at_row(is_last, cot_total), last_id, blank], axis=0)
    ends = jnp.concatenate(
        [
            low, at_row(is_last, full), at_row(is_first, ratio_all), first_id, last_id,
            at_row(is_last, factor), at_row(is_first, par), at_row(is_last, par),
        ],
        axis=0,
    )
    pairs = ((logs[0:8], logs[8:16]), (cat_cot[0:8], cat_cot[8:16]), (ends, pltpu.roll(ends, 4, 0)))
    for k, pair in enumerate(pairs):
        part_ref[2 * b, 8 * k : 8 * k + 8], part_ref[2 * b + 1, 8 * k : 8 * k + 8] = pack(*pair)


ROWS = 20


def unpack_ends(buf, count):
    left = iota((count, LANES), 1) < LANES // 2
    front, back = [], []
    for k in range(4):
        line = buf[pl.ds(16 + k, count, stride=24), :]
        other = turn(line)
        front.append(jnp.where(left, line, other))
        back.append(jnp.where(left, other, line))
    return front + back


def join(buf, count, inner, single):
    low, high, alone, first_id, last_id, factor, first_cat, last_cat = unpack_ends(buf, count)
    place = iota((count, LANES), 0)
    joined = (last_id == pltpu.roll(first_id, count - 1, 0)) & (place < count - 1)
    taken = (first_id == pltpu.roll(last_id, 1, 0)) & (place > 0)
    first = jnp.where(taken, NEG, alone)
    last = jnp.where(joined, lse2(high, pltpu.roll(low, count - 1, 0)), high) * factor
    if single:
        last = jnp.where(first_id == last_id, NEG, last)
    here = iota((8, LANES), 0) + jnp.where(iota((8, LANES), 1) < LANES // 2, 0, 8)
    here = here.astype(F32)
    parts = [buf[24 * d : 24 * d + 8, :] for d in range(count)]
    for d in range(count):
        if d > 0 or not inner:
            parts.append(jnp.where(first_cat[d : d + 1] == here, first[d : d + 1], NEG))
        if d < count - 1 or not inner:
            parts.append(jnp.where(last_cat[d : d + 1] == here, last[d : d + 1], NEG))
    top = functools.reduce(jnp.maximum, parts)
    logs = top + jnp.log(sum(jnp.exp(part - top) for part in parts))
    return logs, sum(buf[24 * d + 8 : 24 * d + 16, :] for d in range(count))


def swap_kernel(
    ny, nz, nx, sums, peaks, ms_ref, cot_ref, table, cols, rows_ref, rho_ref, ids_ref, inv_ref,
    cv_ref, top_ref, nbl_ref, nbr_ref, left_ref, right_ref, lst_ref, c_ref, cg_ref,
    cotm_ref, part_ref, zbuf, line, ybuf, xsrc, xbuf, values, tops,
    nb_send, nb_recv, z_send, z_recv, y_send, y_recv, x_send, x_recv, g_send, g_recv, t_send, t_recv,
):
    sku = lax.axis_index("sku")
    cat = lax.axis_index("cat")
    y, z = lax.div(sku, nz), lax.rem(sku, nz)
    n = ny * nz
    to_right, to_left = lax.rem(sku + 1, n), lax.rem(sku + n - 1, n)
    next_z = [lax.rem(z + k, nz) for k in range(1, nz)]
    along_z = [y * nz + other for other in next_z]
    along_y = [lax.rem(y + k, ny) * nz + z for k in range(1, ny)]
    along_x = [lax.rem(cat + k, nx) for k in range(1, nx)]

    barrier = pltpu.get_barrier_semaphore()
    for other in along_z + along_y + [to_right, to_left]:
        pl.semaphore_signal(barrier, inc=1, device_id={"sku": other}, device_id_type=MESH)
    for other in along_x:
        pl.semaphore_signal(barrier, inc=1, device_id={"cat": other}, device_id_type=MESH)
    for b in range(left_ref.shape[0]):
        condense(
            b, sums, peaks, ms_ref, cot_ref, cotm_ref, table, cols, ids_ref, part_ref, left_ref, right_ref, lst_ref,
            c_ref,
        )
    pl.semaphore_wait(barrier, nz + ny + nx - 1)

    def send(src, dst, send_sem, recv_sem, device):
        copy = pltpu.make_async_remote_copy(
            src_ref=src, dst_ref=dst, send_sem=send_sem, recv_sem=recv_sem, device_id=device, device_id_type=MESH
        )
        copy.start()
        return copy

    used = pl.ds(0, ROWS)

    def slot(k, size):
        return pl.ds(pl.multiple_of(k * 24, 8), size)

    by_z = [
        send(part_ref.at[next_z[k], used], zbuf.at[slot(z, ROWS)], z_send.at[k], z_recv.at[k], {"sku": other})
        for k, other in enumerate(along_z)
    ]
    near = [
        send(right_ref, nbl_ref, nb_send.at[0], nb_recv.at[0], {"sku": to_right}),
        send(left_ref, nbr_ref, nb_send.at[1], nb_recv.at[1], {"sku": to_left}),
    ]
    zbuf[slot(z, 24), :] = part_ref[z]
    ah, al = halves(rows_ref[0:1, :])
    pick = iota((16, ah.shape[1]), 0)
    weights = jnp.where(pick == 0, ah.astype(F32), jnp.where(pick == 1, al.astype(F32), 0.0)).astype(BF16)
    for k in range(cg_ref.shape[1] // CHUNK):
        at = pl.ds(k * CHUNK, CHUNK)
        cg_ref[:, at] = jnp.sum(dot(weights, cotm_ref[:, at]), axis=0, keepdims=True) * inv_ref[0:1, at]
    for copy in by_z:
        copy.wait_recv()

    line[0:8, :], line[8:16, :] = join(zbuf, nz, True, True)
    begin, end = zbuf[16:24, :], zbuf[24 * nz - 8 : 24 * nz, :]
    row, left = iota((8, LANES), 0), iota((8, LANES), 1) < LANES // 2
    from_begin = (row == 2) | (left & ((row == 0) | (row == 3)))
    one = end[3:4] == turn(end)[0:1]
    end = jnp.where(left & (row == 1) & one, NEG, end)
    line[16:24, :] = jnp.where(from_begin, begin, end)

    by_y = [
        send(line.at[used], ybuf.at[slot(y, ROWS)], y_send.at[k], y_recv.at[k], {"sku": other})
        for k, other in enumerate(along_y)
    ]
    ybuf[slot(y, 24), :] = line[...]
    for copy in by_y:
        copy.wait_recv()
    logs, cot = join(ybuf, ny, False, False)
    value = rho_ref[0:8, :] * logs
    values[0:8, :] = value
    values[8:16, :] = cot
    top = jnp.max(value, axis=0, keepdims=True)
    top = jnp.maximum(top, turn(top))
    total = jnp.sum(jnp.exp(value - top), axis=0, keepdims=True)
    cot = jnp.sum(cot, axis=0, keepdims=True)
    xsrc[0:1, :] = top + jnp.log(total + turn(total))
    xsrc[1:2, :] = cot + turn(cot)
    xsrc[2:8, :] = jnp.zeros((6, LANES), F32)

    by_x = [send(xsrc, xbuf.at[k], x_send.at[k], x_recv.at[k], {"cat": other}) for k, other in enumerate(along_x)]
    gather = [
        send(values, cv_ref.at[z], g_send.at[k], g_recv.at[k], {"sku": other}) for k, other in enumerate(along_z)
    ]
    cv_ref[z] = values[...]
    for copy in by_x:
        copy.wait_recv()
    groups = [xsrc[0:1, :]] + [xbuf[k, 0:1, :] for k in range(nx - 1)]
    top = functools.reduce(jnp.maximum, groups + [jnp.zeros((1, LANES), F32)])
    tops[0:1, :] = top + jnp.log(jnp.exp(-top) + sum(jnp.exp(group - top) for group in groups))
    tops[1:2, :] = xsrc[1:2, :] + sum(xbuf[k, 1:2, :] for k in range(nx - 1))
    tops[2:8, :] = jnp.zeros((6, LANES), F32)
    last = [send(tops, top_ref.at[z], t_send.at[k], t_recv.at[k], {"sku": other}) for k, other in enumerate(along_z)]
    top_ref[z] = tops[...]
    for copy in near + gather + last:
        copy.wait_recv()
    for copy in by_z + near + by_y + by_x + gather + last:
        copy.wait_send()


def slope_kernel(
    wh_ref, wl_ref, lst_ref, r_ref, c_ref, cv_ref, top_ref, nbl_ref, nbr_ref, left_ref, right_ref, cg_ref, ids_ref,
    rows_ref, cols, rho_ref, grad_ref, path_ref, hs, paths,
):
    subs = lst_ref.shape[0]
    blocks = nbl_ref.shape[0]
    width = ids_ref.shape[1]
    cats = 16
    base, narrow = reach(ids_ref[...])
    paths[...] = jnp.zeros_like(paths)

    def fill(base, count):
        stretch = pl.ds(base, count)
        lam, par, irho, ilam = cols[0, stretch, :], cols[2, stretch, :], cols[3, stretch, :], cols[4, stretch, :]
        spot = iota((count, LANES), 1)
        parents = jnp.where(((spot % cats).astype(F32) == par) & (spot < 3 * cats), 1.0, 0.0).astype(BF16)
        parents = parents[:, : 3 * cats]
        row = (iota((count, LANES), 0) + base).astype(F32)
        for b in range(blocks):
            at = pl.ds(b * LANES, LANES)
            from_left, from_right = nbl_ref[b], nbr_ref[b]
            first_id, last_id = left_ref[b, 2:3, :], right_ref[b, 2:3, :]
            values, cots = [
                jnp.concatenate(
                    pack(cv_ref[2 * b, 8 * k : 8 * k + 8, :], cv_ref[2 * b + 1, 8 * k : 8 * k + 8, :]), axis=0
                )
                for k in range(2)
            ]
            top = jnp.where(iota((8, LANES), 1) < LANES // 2, top_ref[2 * b], top_ref[2 * b + 1])
            inclusive = top[0:1]
            slopes = (1.0 - 1.0 / rho_ref[8:24, :]) * cots - top[1:2] * jnp.exp(values - inclusive)
            left_hit = (row == first_id) & (from_left[2:3] == first_id)
            right_hit = (row == last_id) & (from_right[2:3] == last_id)
            extra = jnp.where(left_hit, from_left[0:1], jnp.where(right_hit, from_right[0:1], NEG))
            level = lse2(lst_ref[stretch, at], extra)
            other_cot = jnp.where(left_hit, from_left[1:2], jnp.where(right_hit, from_right[1:2], 0.0))
            sub_cot = c_ref[stretch, at] + other_cot
            cat_value = dot(parents, jnp.concatenate(thirds(values), axis=0))
            d_cat = dot(parents, jnp.concatenate(thirds(slopes), axis=0))
            log_sub = (lam * level - cat_value) * irho
            paths[stretch, at] = rows_ref[1:2, at] - level + log_sub + (cat_value - inclusive)
            d_sub = (irho - ilam) * sub_cot + jnp.exp(log_sub) * d_cat
            slope = rows_ref[0:1, at] * jnp.exp(r_ref[stretch, at] - level) * d_sub
            hs[0:count, at], hs[count : 2 * count, at] = halves(slope)
        for k in range(width // CHUNK):
            at = pl.ds(k * CHUNK, CHUNK)
            both = dot(hs[0 : 2 * count, :], wh_ref[:, at])
            found = both[0:count] + both[count:] + dot(hs[0:count, :], wl_ref[:, at])
            hit = iota((count, CHUNK), 0) + base == ids_ref[:, at]
            grad_ref[:, at] = -(jnp.sum(jnp.where(hit, found, 0.0), axis=0, keepdims=True) + cg_ref[:, at])

    @pl.when(narrow)
    def _():
        fill(base, WINDOW)

    @pl.when(jnp.logical_not(narrow))
    def _():
        fill(0, subs)

    for b in range(blocks):
        at = pl.ds(b * LANES, LANES)
        path_ref[at, 0:subs], path_ref[at, subs:] = halves(jnp.transpose(paths[:, at]))


ROW_BLOCK = 128


def demand_kernel(ms_ref, path_ref, table, out_hbm, value_ref, sem):
    markets, width = ms_ref.shape

    def flush(b):
        rows = pl.ds(b * ROW_BLOCK, ROW_BLOCK)
        return pltpu.make_async_copy(value_ref.at[rows], out_hbm.at[rows, 0, :], sem.at[b])

    for b in range(markets // ROW_BLOCK):
        rows = pl.ds(b * ROW_BLOCK, ROW_BLOCK)
        for k in range(width // CHUNK):
            at = pl.ds(k * CHUNK, CHUNK)
            masked = ms_ref[rows, at]
            hits = table[:, at]
            path = dot(path_ref[rows, :], jnp.concatenate([hits, hits], axis=0))
            value_ref[rows, at] = jnp.where(masked > EMPTY, masked + path, 0.0)
        flush(b).start()
    for b in range(markets // ROW_BLOCK):
        flush(b).wait()


def whole():
    return pl.BlockSpec(memory_space=pltpu.VMEM)


def shards(
    n_sku, n_cat, features, taste, price, alpha, market_size, store_brand, sub_scale, cat_scale, availability,
    sku_subcat, subcat_cat, cotangent,
):
    markets, depth = features.shape
    width = price.shape[1]
    subs, cats = sub_scale.shape[1], cat_scale.shape[1]
    blocks = markets // LANES
    operands = (
        features,
        taste.reshape(depth, width),
        price,
        alpha.reshape(1, markets),
        market_size.reshape(1, markets),
        sub_scale,
        store_brand,
        cat_scale,
        subcat_cat,
        availability,
        sku_subcat,
        cotangent.reshape(markets, width),
    )
    operands = [pltpu.with_memory_space_constraint(x, pltpu.HBM) for x in operands]
    sds = jax.ShapeDtypeStruct
    vmem, dma = pltpu.VMEM, pltpu.SemaphoreType.DMA
    ms, wh, wl, cot, sums, peaks, table, cols, rows, rho_rows, ids, inv = pl.pallas_call(
        local_kernel,
        in_specs=[pl.BlockSpec(memory_space=pl.ANY)] * 12,
        out_specs=[whole()] * 12,
        out_shape=[
            sds((markets, width), F32),
            sds((markets, width), BF16),
            sds((markets, width), BF16),
            sds((markets, width), BF16),
            sds((subs, markets), F32),
            sds((subs, markets), F32),
            sds((subs, width), BF16),
            sds((5, subs, LANES), F32),
            sds((8, markets), F32),
            sds((24, LANES), F32),
            sds((1, width), jnp.int32),
            sds((8, width), F32),
        ],
        scratch_shapes=[
            vmem((markets, depth), BF16),
            vmem((depth, width), BF16),
            vmem((1, width), F32),
            vmem((1, subs), F32),
            vmem((1, subs), F32),
            vmem((1, cats), F32),
            vmem((1, subs), jnp.int32),
            vmem((markets, width), jnp.int32),
            vmem((1, markets), F32),
            vmem((8, CHUNK), F32),
            vmem((WINDOW, width), BF16),
            dma((8,)),
            dma((2,)),
            dma((blocks,)),
            dma,
        ],
        compiler_params=pltpu.CompilerParams(vmem_limit_bytes=32 * 1024 * 1024),
        name="local_nests",
    )(*operands)

    nz = 2 * blocks
    ny = n_sku // nz
    cv, top, nbl, nbr, left, right, lst, c, cg = pl.pallas_call(
        functools.partial(swap_kernel, ny, nz, n_cat),
        in_specs=[whole()] * 10,
        out_specs=[whole()] * 9,
        out_shape=[sds((nz, 16, LANES), F32), sds((nz, 8, LANES), F32)]
        + [sds((blocks, 8, LANES), F32)] * 4
        + [sds((subs, markets), F32)] * 2
        + [sds((1, width), F32)],
        scratch_shapes=[
            vmem((markets, width), BF16),
            vmem((nz, 24, LANES), F32),
            vmem((nz * 24, LANES), F32),
            vmem((24, LANES), F32),
            vmem((ny * 24, LANES), F32),
            vmem((8, LANES), F32),
            vmem((n_cat - 1, 8, LANES), F32),
            vmem((16, LANES), F32),
            vmem((8, LANES), F32),
        ]
        + [dma((count,)) for count in (2, nz - 1, ny - 1, n_cat - 1, nz - 1, nz - 1) for _ in range(2)],
        compiler_params=pltpu.CompilerParams(
            collective_id=0, has_side_effects=True, vmem_limit_bytes=16 * 1024 * 1024
        ),
        name="swap_nests",
    )(sums, peaks, ms, cot, table, cols, rows, rho_rows, ids, inv)

    grad, path = pl.pallas_call(
        slope_kernel,
        in_specs=[whole()] * 16,
        out_specs=[whole()] * 2,
        out_shape=[sds((1, width), F32), sds((markets, 2 * subs), BF16)],
        scratch_shapes=[vmem((2 * subs, markets), BF16), vmem((subs, markets), F32)],
        compiler_params=pltpu.CompilerParams(vmem_limit_bytes=16 * 1024 * 1024),
        name="price_slope",
    )(wh, wl, lst, peaks, c, cv, top, nbl, nbr, left, right, cg, ids, rows, cols, rho_rows)
    other = lax.ppermute(grad, "mkt", [(0, 1), (1, 0)])

    demand = pl.pallas_call(
        demand_kernel,
        in_specs=[whole()] * 3,
        out_specs=pl.BlockSpec(memory_space=pl.ANY),
        out_shape=sds((markets, 1, width), F32),
        scratch_shapes=[vmem((markets, width), F32), dma((markets // ROW_BLOCK,))],
        compiler_params=pltpu.CompilerParams(vmem_limit_bytes=16 * 1024 * 1024),
        cost_estimate=pl.CostEstimate(
            flops=2 * markets * width * 2 * subs, bytes_accessed=8 * markets * width, transcendentals=0
        ),
        name="log_demand",
    )(ms, path, table)
    return demand, grad + other


def solution(mesh):
    return jax.shard_map(
        functools.partial(shards, mesh.shape["sku"], mesh.shape["cat"]),
        mesh=mesh,
        in_specs=(
            P("mkt", None),
            P(None, "cat", "sku"),
            P("cat", "sku"),
            P("mkt"),
            P("mkt"),
            P("cat", None),
            P("cat", None),
            P("cat", None),
            P("mkt", "cat", "sku"),
            P("cat", "sku"),
            P("cat", None),
            P("mkt", "cat", "sku"),
        ),
        out_specs=(P("mkt", "cat", "sku"), P("cat", "sku")),
        check_vma=False,
    )
```
